32 devices in a mesh: dp: 16 (over z, y, x), tensor: 2 (over core).
Axes of the slice: x: 2, y: 2, z: 4, core: 2. Of those that a mesh axis runs over, the one named last changes fastest.
Arguments:
- content_input: bfloat16 [16384, 768], P('dp'), may hold values from -6 to 6
- query_input: bfloat16 [16384, 768], P('dp'), may hold values from -6 to 6
- segment_ids: int32 [32, 512], P('dp'), may hold values from 0 to 15, never falling along the last dimension, each value on 1 to 256 neighbouring positions
- orders: int32 [32, 512], P('dp'), may hold values from 0 to 511, each once within a row
- predicted: int32 [32, 512], P('dp'), may hold values 0 or 1
- query_weight: bfloat16 [768, 768], P(None, 'tensor'), may hold values from -0.21875 to 0.21875
- query_bias: float32 [768], P('tensor'), may hold values from -3 to 3
- key_weight: bfloat16 [768, 768], P(None, 'tensor'), may hold values from -0.21875 to 0.21875
- value_weight: bfloat16 [768, 768], P(None, 'tensor'), may hold values from -0.21875 to 0.21875
- value_bias: float32 [768], P('tensor'), may hold values from -3 to 3
- out_weight: bfloat16 [768, 768], P('tensor'), may hold values from -0.875 to 0.875
- out_bias: float32 [768], replicated, may hold values from -3 to 3
- first_gain: float32 [768], replicated, may hold values from 0.25 to 1.75
- first_shift: float32 [768], replicated, may hold values from -2 to 2
- up_weight: bfloat16 [768, 3072], P(None, 'tensor'), may hold values from -0.21875 to 0.21875
- up_bias: float32 [3072], P('tensor'), may hold values from -3 to 3
- down_weight: bfloat16 [3072, 768], P('tensor'), may hold values from -0.109375 to 0.109375
- down_bias: float32 [768], replicated, may hold values from -3 to 3
- second_gain: float32 [768], replicated, may hold values from 0.25 to 1.75
- second_shift: float32 [768], replicated, may hold values from -2 to 2
- bias_table: float32 [32, 12], P(None, 'tensor'), may hold values from -4 to 4
- content_upstream: bfloat16 [16384, 768], P(('dp', 'tensor')), may hold values from -6 to 6
- query_upstream: bfloat16 [16384, 768], P(('dp', 'tensor')), may hold values from -6 to 6
Outputs:
- content_out: bfloat16 [16384, 768], P(('dp', 'tensor'))
- query_out: bfloat16 [16384, 768], P(('dp', 'tensor'))
- grad_content: float32 [16384, 768], P(('dp', 'tensor'))
- grad_query: float32 [16384, 768], P(('dp', 'tensor'))
- grad_query_weight: float32 [768, 768], P('dp', 'tensor')
- grad_key_weight: float32 [768, 768], P('dp', 'tensor')
- grad_value_weight: float32 [768, 768], P('dp', 'tensor')
- grad_out_weight: float32 [768, 768], P('tensor', 'dp')
- grad_up_weight: float32 [768, 3072], P('dp', 'tensor')
- grad_down_weight: float32 [3072, 768], P('tensor', 'dp')
- grad_query_bias: float32 [768], replicated
- grad_value_bias: float32 [768], replicated
- grad_out_bias: float32 [768], replicated
- grad_first_gain: float32 [768], replicated
- grad_first_shift: float32 [768], replicated
- grad_up_bias: float32 [3072], replicated
- grad_down_bias: float32 [768], replicated
- grad_second_gain: float32 [768], replicated
- grad_second_shift: float32 [768], replicated
- grad_bias_table: float32 [32, 12], replicated
The draws below stay inside these ranges and needn't reach their ends.
Inputs may be any that keep to these rules, and one draw needn't show every extreme that they name: `segment_ids`: along each row the segment numbers never fall; a segment covers 1 to 256 positions. `orders`: each row holds every number once.
All inputs are finite; a program needn't handle non-finite values. No bound on the sum of `predicted` on one device may be relied on, other than what follows from the above.
Results may differ from the reference program's by a relative error of at most 0.015.
Values may be sent and summed in bfloat16 or wider, within the bound.
No kernel may reach another device: no remote copies, remote signals or barrier semaphores. Data moves between devices by JAX's collectives and lax.ppermute only.
A program may use at most 192 MiB of HBM per device.

```python
import math
import jax
import jax.numpy as jnp
import numpy as np
from jax import lax

D = 768
HEADS = 12
FF = 3072
BUCKETS = 32
ROW_LEN = 512
ROWS = 32
TOKENS = 16384


def set_ends(values, own_key, least, high):
    shape = values.shape
    index_at = [jax.random.randint(jax.random.fold_in(own_key, axis), (), 0, shape[axis]) for axis in range(len(shape))]
    values = values.at[tuple(index_at)].set(least)
    longest = shape.index(max(shape))
    index_at[longest] = (index_at[longest] + 1) % shape[longest]
    return values.at[tuple(index_at)].set(high)


def steps_of(stream_key, extent, split, smallest, high):
    level = 1.0
    for position, blocks in split:
        draws = jax.random.uniform(jax.random.fold_in(jax.random.fold_in(stream_key, 6), position), (blocks,), jnp.float32, smallest / len(split), high / len(split))
        level = level * jnp.repeat(jnp.exp(draws), extent[position] // blocks).reshape((-1,) + (1,) * (len(extent) - 1 - position))
    return level


def split_up(amount, total, reach, lean):
    portions = [(1 << 20) // math.isqrt(grade ** lean) + 1 for grade in range(2, amount + 1)]
    surplus, holding = total - reach - (amount - 1), [1] * (amount - 1)
    while surplus > 0:
        candidates = [i for i in range(amount - 1) if holding[i] < reach]
        pool, left = sum([portions[i] for i in candidates]), surplus
        for i in candidates:
            addition = min(reach - holding[i], max(1, left * portions[i] // pool), surplus)
            holding[i] = holding[i] + addition
            surplus = surplus - addition
    return np.array([reach] + holding)


def uneven_parts(key, amount, total, bound, slope):
    if amount == 2:
        one = jax.random.randint(key, (), max(1, total - bound), min(bound, total - 1) + 1)
        return jnp.stack([one, total - one])
    sizes = jnp.asarray(split_up(amount, total, bound, slope), jnp.int32)
    pairs = (amount - 1) // 2
    donor, taker = sizes[1:1 + 2 * pairs:2], sizes[2:2 + 2 * pairs:2]
    margin = jnp.minimum(donor - 1, bound - taker)
    moved = jax.random.randint(jax.random.fold_in(key, 1), (pairs,), 0, 1 << 20) % (margin + 1)
    sizes = sizes.at[1:1 + 2 * pairs:2].set(donor - moved).at[2:2 + 2 * pairs:2].set(taker + moved)
    return sizes[jax.random.permutation(jax.random.fold_in(key, 2), amount)]


def scatter_about(stream_key, extent, scale, reach, split=(), kind=jnp.bfloat16):
    array = scale * jax.random.normal(stream_key, extent, jnp.float32)
    if split:
        array = array * steps_of(stream_key, extent, split, -0.22, 0.18)
    return jnp.clip(array, -reach, reach).astype(kind)


def setup_inputs(seed: int = 0) -> dict:
    seeds = jax.random.split(jax.random.key(seed), 24)
    return {
        "content_input": scatter_about(seeds[0], (TOKENS, D), 1.0, 6.0, ((0, 16),)),
        "query_input": scatter_about(seeds[1], (TOKENS, D), 1.0, 6.0, ((0, 16),)),
        "segment_ids": jax.vmap(lambda own: jnp.searchsorted(jnp.cumsum(uneven_parts(own, max(4, ROW_LEN // 32), ROW_LEN, ROW_LEN // 2, 2)), jnp.arange(ROW_LEN), side="right"))(jax.random.split(seeds[2], ROWS)).reshape((ROWS, ROW_LEN)).astype(jnp.int32),
        "orders": jax.vmap(lambda own: jax.random.permutation(own, ROW_LEN))(jax.random.split(seeds[3], ROWS)).reshape((ROWS, ROW_LEN)).astype(jnp.int32),
        "predicted": set_ends((jax.random.randint(seeds[4], (ROWS, ROW_LEN), 0, 20) < 3).astype(jnp.int32), jax.random.fold_in(seeds[4], 1), 0, 1),
        "query_weight": scatter_about(seeds[5], (D, D), D ** -0.5, 0.21875, ((1, 2),)),
        "query_bias": scatter_about(seeds[6], (D,), 0.5, 3.0, ((0, 2),), jnp.float32),
        "key_weight": scatter_about(seeds[7], (D, D), D ** -0.5, 0.21875, ((1, 2),)),
        "value_weight": scatter_about(seeds[8], (D, D), D ** -0.5, 0.21875, ((1, 2),)),
        "value_bias": scatter_about(seeds[9], (D,), 0.5, 3.0, ((0, 2),), jnp.float32),
        "out_weight": scatter_about(seeds[10], (D, D), (D // 16) ** -0.5, 0.875, ((0, 2),)),
        "out_bias": scatter_about(seeds[11], (D,), 0.5, 3.0, (), jnp.float32),
        "first_gain": jnp.clip(1.0 + 0.15 * jax.random.normal(seeds[12], (D,), jnp.float32), 0.25, 1.75),
        "first_shift": scatter_about(seeds[13], (D,), 0.3, 2.0, (), jnp.float32),
        "up_weight": scatter_about(seeds[14], (D, FF), D ** -0.5, 0.21875, ((1, 2),)),
        "up_bias": scatter_about(seeds[15], (FF,), 0.5, 3.0, ((0, 2),), jnp.float32),
        "down_weight": scatter_about(seeds[16], (FF, D), FF ** -0.5, 0.109375, ((0, 2),)),
        "down_bias": scatter_about(seeds[17], (D,), 0.5, 3.0, (), jnp.float32),
        "second_gain": jnp.clip(1.0 + 0.15 * jax.random.normal(seeds[18], (D,), jnp.float32), 0.25, 1.75),
        "second_shift": scatter_about(seeds[19], (D,), 0.3, 2.0, (), jnp.float32),
        "bias_table": scatter_about(seeds[20], (BUCKETS, HEADS), 1.0, 4.0, ((1, 2),), jnp.float32),
        "content_upstream": scatter_about(seeds[21], (TOKENS, D), 1.0, 6.0, ((0, 32),)),
        "query_upstream": scatter_about(seeds[22], (TOKENS, D), 1.0, 6.0, ((0, 32),)),
    }


@jax.custom_vjp
def low(v):
    return lax.optimization_barrier(v.astype(jnp.bfloat16)).astype(jnp.float32)

@jax.custom_vjp
def low_back(v):
    return v

def low_keep(v):
    return (low(v), None)

def low_pass(kept, grad):
    return (grad,)

def back_keep(v):
    return (v, None)

def back_low(kept, grad):
    return (low(grad),)
low.defvjp(low_keep, low_pass)
low_back.defvjp(back_keep, back_low)
norm_eps = 1e-05
big_negative = -1e+30

def bucket_grid(length):
    offsets = np.arange(length)
    distance = np.abs(offsets[:, None] - offsets[None, :])
    limits = 8.0 * 2.0 ** (np.arange(1, 8) / 2.0)
    counted = (distance[:, :, None] >= limits[None, None, :]).sum(axis=2)
    bucket = np.where(distance < 8, distance, 8 + counted)
    bucket = np.minimum(bucket, 15) + 16 * (offsets[None, :] > offsets[:, None])
    return bucket.astype(np.int32)

def dense_dot(left_side, right_side):
    return jnp.dot(left_side, right_side, precision=lax.Precision.HIGHEST)

def layer_norm(values, gain_vec, shift_vec):
    centre = lax.optimization_barrier(jnp.mean(values, axis=-1, keepdims=True))
    centred = values - centre
    variance = lax.optimization_barrier(jnp.mean(centred * centred, axis=-1, keepdims=True))
    return centred * lax.rsqrt(variance + norm_eps) * gain_vec + shift_vec

def row_masks(segment, ordering, flagged):
    same_doc = segment[:, None] == segment[None, :]
    unmasked = (flagged == 0)[None, :]
    earlier = ordering[None, :] < ordering[:, None]
    itself = ordering[None, :] == ordering[:, None]
    starts = jnp.concatenate([jnp.ones((1,), dtype=bool), segment[1:] != segment[:-1]])
    content_mask = same_doc & (unmasked | earlier | itself)
    query_mask = same_doc & (unmasked | earlier | starts[None, :])
    return jnp.stack([content_mask, query_mask])

def attention(queries, keys_low, values_low, pos_bias, segment_ids, orders, predicted):
    row_count = segment_ids.shape[0]
    row_len = segment_ids.shape[1]
    group_size = 4
    groups = row_count // group_size
    head_count = pos_bias.shape[0]
    full_width = queries.shape[-1]
    head_size = full_width // head_count
    score_scale = head_size ** (-0.5)
    group_query = queries.reshape(2, groups, group_size, row_len, head_count, head_size).transpose(1, 0, 2, 3, 4, 5)
    group_key = keys_low.reshape(groups, group_size, row_len, head_count, head_size)
    group_value = values_low.reshape(groups, group_size, row_len, head_count, head_size)
    group_segment = segment_ids.reshape(groups, group_size, row_len)
    group_order = orders.reshape(groups, group_size, row_len)
    group_flag = predicted.reshape(groups, group_size, row_len)

    def group_step(bias_carry, inputs):
        one_query, one_key, one_value, one_segment, one_order, one_flag = inputs
        visible = jax.vmap(row_masks)(one_segment, one_order, one_flag)
        raw_scores = jnp.einsum('sgqhd,gkhd->gshqk', one_query, one_key, precision=lax.Precision.HIGHEST) * score_scale + bias_carry[None, None]
        scores = jnp.where(visible[:, :, None], low_back(raw_scores), big_negative)
        row_top = lax.optimization_barrier(jnp.max(scores, axis=-1, keepdims=True))
        shifted = jnp.exp(scores - row_top)
        weights = low(shifted / lax.optimization_barrier(jnp.sum(shifted, axis=-1, keepdims=True)))
        mixed_out = jnp.einsum('gshqk,gkhd->sgqhd', weights, one_value, precision=lax.Precision.HIGHEST)
        return (bias_carry, mixed_out)
    unused_end, mixed_all = lax.scan(jax.checkpoint(group_step), pos_bias, (group_query, group_key, group_value, group_segment, group_order, group_flag))
    return mixed_all.transpose(1, 0, 2, 3, 4, 5).reshape(2, row_count * row_len, full_width)

def forward(params, segment_ids, orders, predicted):
    content, query_stream, query_weight, query_bias, key_weight, value_weight, value_bias, out_weight, out_bias, first_gain, first_shift, up_weight, up_bias, down_weight, down_bias, second_gain, second_shift, bias_table = params
    streams = jnp.stack([content, query_stream])
    queries = low_back(low(dense_dot(streams, query_weight) + query_bias))
    keys_low = low_back(low(dense_dot(content, key_weight)))
    values_low = low_back(low(dense_dot(content, value_weight) + value_bias))
    bucket_ids = jnp.asarray(bucket_grid(segment_ids.shape[1]))
    pos_bias = jnp.transpose(bias_table[bucket_ids], (2, 0, 1))
    mixed = attention(queries, keys_low, values_low, pos_bias, segment_ids, orders, predicted)
    mixed = low_back(low(mixed))
    attn_sum = low_back(dense_dot(mixed, out_weight))
    first_out = layer_norm(streams + attn_sum + out_bias, first_gain, first_shift)
    up_pre = low_back(dense_dot(low(first_out), up_weight) + up_bias)
    hidden = low(jax.nn.gelu(up_pre, approximate=False))
    down_sum = low_back(dense_dot(hidden, down_weight))
    return layer_norm(first_out + down_sum + down_bias, second_gain, second_shift)

def reference(content_input, query_input, segment_ids, orders, predicted, query_weight, query_bias, key_weight, value_weight, value_bias, out_weight, out_bias, first_gain, first_shift, up_weight, up_bias, down_weight, down_bias, second_gain, second_shift, bias_table, content_upstream, query_upstream):
    floats = tuple((argument.astype(jnp.float32) for argument in (content_input, query_input, query_weight, query_bias, key_weight, value_weight, value_bias, out_weight, out_bias, first_gain, first_shift, up_weight, up_bias, down_weight, down_bias, second_gain, second_shift, bias_table)))

    def forward_fixed(*params):
        return forward(params, segment_ids, orders, predicted)
    primal, pullback = jax.vjp(forward_fixed, *floats)
    upstream = jnp.stack([content_upstream, query_upstream]).astype(jnp.float32)
    gradients = pullback(upstream)
    return (primal[0].astype(jnp.bfloat16), primal[1].astype(jnp.bfloat16), gradients[0], gradients[1], gradients[2], gradients[4], gradients[5], gradients[7], gradients[11], gradients[13], gradients[3], gradients[6], gradients[8], gradients[9], gradients[10], gradients[12], gradients[14], gradients[15], gradients[16], gradients[17])
```

```python
import functools

import jax
import jax.numpy as jnp
import numpy as np
from jax import lax
from jax.experimental import pallas as pl
from jax.experimental.pallas import tpu as pltpu
from jax.sharding import PartitionSpec as P

norm_eps = 1e-05
big_negative = -1e30
root_half = 0.7071067811865476
root_two_pi_inv = 0.3989422804014327

tile = 128
reach = 2
span = (2 * reach + 1) * tile
wide = span + tile
NT = (((1,), (1,)), ((), ()))
NN = (((1,), (0,)), ((), ()))


def dot_f32(left, right, dims=NN):
    return lax.dot_general(left, right, dims, preferred_element_type=jnp.float32)


def bucket_of(offset):
    distance = np.abs(offset)
    limits = 8.0 * 2.0 ** (np.arange(1, 8) / 2.0)
    counted = (distance[..., None] >= limits).sum(axis=-1)
    bucket = np.where(distance < 8, distance, 8 + counted)
    return (np.minimum(bucket, 15) + 16 * (offset < 0)).astype(np.int32)


def band_one_hot(buckets):
    place = np.arange(wide)
    offset = np.where(place < span, place, place - wide) - reach * tile
    return (bucket_of(offset)[:, None] == np.arange(buckets)[None, :]).astype(np.float32)


def key_tiles(b, tiles):
    return list(range(max(0, b - reach), min(tiles - 1, b + reach) + 1))


def attend_kernel(info_ref, t_ref, q_ref, k_ref, v_ref, o_ref, e_ref, linv_ref, mask_ref):
    row_len = k_ref.shape[0]
    tiles = row_len // tile

    @pl.when(pl.program_id(0) == 0)
    def _():
        seg = info_ref[0:1, :]
        order = info_ref[1:2, :]
        flag = info_ref[2:3, :]
        at = lax.broadcasted_iota(jnp.int32, (1, row_len), 1)
        first = (seg != pltpu.roll(seg, 1, 1)) | (at == 0)
        key_content = jnp.where(flag == 0.0, -1.0, order)
        key_query = jnp.where(first, -1.0, key_content)

        def as_column(row):
            return jnp.transpose(jnp.broadcast_to(row, (tile, row_len)))

        seg_col, content_col, query_col = as_column(seg), as_column(key_content), as_column(key_query)
        for b in range(tiles):
            here = slice(b * tile, (b + 1) * tile)
            same = seg_col == seg[:, here]
            mask_ref[b, :, :tile] = jnp.where(same & (content_col <= order[:, here]), 0.0, big_negative)
            mask_ref[b, :, tile:] = jnp.where(same & (query_col < order[:, here]), 0.0, big_negative)

    lane = lax.broadcasted_iota(jnp.int32, (1, tile), 1)
    v_t = jnp.transpose(v_ref[...].astype(jnp.float32)).astype(jnp.bfloat16)
    keys = k_ref[...].astype(jnp.float32) * 0.125
    half = tile // 2
    parts = [[None, None] for _ in range(tiles)]
    for h in range(2):
        in_head = (lane >= h * half) & (lane < (h + 1) * half)
        k_head = jnp.where(in_head, keys, 0.0).astype(jnp.bfloat16)
        band = pltpu.roll(jnp.broadcast_to(t_ref[h], (tile, wide)), 0, 1, stride=1, stride_axis=0)
        for b in range(tiles):
            near = key_tiles(b, tiles)
            q_tile = jnp.concatenate(
                [q_ref[b * tile : (b + 1) * tile, :], q_ref[row_len + b * tile : row_len + (b + 1) * tile, :]], axis=0
            )
            scores = []
            top = None
            for kb in near:
                d = b - kb + reach
                bias = band[:, d * tile : (d + 1) * tile]
                s = dot_f32(k_head[kb * tile : (kb + 1) * tile, :], q_tile, NT)
                s = s + jnp.concatenate([bias, bias], axis=1) + mask_ref[b, kb * tile : (kb + 1) * tile, :]
                scores.append(s)
                one_top = jnp.max(s, axis=0, keepdims=True)
                top = one_top if top is None else jnp.maximum(top, one_top)
            total = None
            weights = []
            for kb, s in zip(near, scores):
                e = jnp.exp(s - top)
                one_total = jnp.sum(e, axis=0, keepdims=True)
                total = one_total if total is None else total + one_total
                e = e.astype(jnp.bfloat16)
                e_ref[0, h, b, kb * tile : (kb + 1) * tile, :] = e
                weights.append(e)
            inverse = 1.0 / total
            linv_ref[0, h * tiles + b : h * tiles + b + 1, :] = inverse
            mixed = dot_f32(
                v_t[h * half : (h + 1) * half, near[0] * tile : (near[-1] + 1) * tile],
                jnp.concatenate(weights, axis=0),
            )
            parts[b][h] = mixed * inverse
    for b in range(tiles):
        both = jnp.transpose(jnp.concatenate(parts[b], axis=0)).astype(jnp.bfloat16)
        o_ref[b * tile : (b + 1) * tile, :] = both[:tile]
        o_ref[row_len + b * tile : row_len + (b + 1) * tile, :] = both[tile:]


def attend(info, band_rows, q, k, v):
    tokens, width = q.shape
    row_len = k.shape[0]
    pairs = width // tile
    tiles = row_len // tile
    pair_block = lambda rows: pl.BlockSpec((rows, tile), lambda p: (0, p))
    return pl.pallas_call(
        attend_kernel,
        grid=(pairs,),
        in_specs=[
            pl.BlockSpec(info.shape, lambda p: (0, 0)),
            pl.BlockSpec((2, 1, wide), lambda p: (p, 0, 0)),
            pair_block(tokens),
            pair_block(row_len),
            pair_block(row_len),
        ],
        out_specs=[
            pair_block(tokens),
            pl.BlockSpec((1, 2, tiles, row_len, 2 * tile), lambda p: (p, 0, 0, 0, 0)),
            pl.BlockSpec((1, 2 * tiles, 2 * tile), lambda p: (p, 0, 0)),
        ],
        out_shape=[
            jax.ShapeDtypeStruct((tokens, width), jnp.bfloat16),
            jax.ShapeDtypeStruct((pairs, 2, tiles, row_len, 2 * tile), jnp.bfloat16),
            jax.ShapeDtypeStruct((pairs, 2 * tiles, 2 * tile), jnp.float32),
        ],
        scratch_shapes=[pltpu.VMEM((tiles, row_len, 2 * tile), jnp.float32)],
        compiler_params=pltpu.CompilerParams(vmem_limit_bytes=40 * 1024 * 1024),
        cost_estimate=pl.CostEstimate(
            flops=pairs * 2 * 2 * 2 * 2 * row_len * row_len * 128,
            bytes_accessed=pairs * 2 * tiles * row_len * 2 * tile * 2,
            transcendentals=pairs * 4 * row_len * row_len,
        ),
        name="attend",
    )(info, band_rows, q, k, v)


def attend_back_kernel(q_ref, k_ref, v_ref, do_ref, o_ref, e_ref, linv_ref, dq_ref, dk_ref, dv_ref, band_ref, dk_acc, dv_acc, g_acc):
    row_len = k_ref.shape[0]
    tiles = row_len // tile
    half = tile // 2
    lane = lax.broadcasted_iota(jnp.int32, (1, tile), 1)
    k_t = jnp.transpose(k_ref[...].astype(jnp.float32)).astype(jnp.bfloat16)
    dk_acc[...] = jnp.zeros_like(dk_acc)
    dv_acc[...] = jnp.zeros_like(dv_acc)
    g_acc[...] = jnp.zeros_like(g_acc)
    for b in range(tiles):
        near = key_tiles(b, tiles)
        keys = slice(near[0] * tile, (near[-1] + 1) * tile)
        here = slice(b * tile, (b + 1) * tile)
        there = slice(row_len + b * tile, row_len + (b + 1) * tile)
        q_tile = jnp.concatenate([q_ref[here, :], q_ref[there, :]], axis=0)
        do_t = jnp.transpose(jnp.concatenate([do_ref[here, :], do_ref[there, :]], axis=0).astype(jnp.float32))
        o_t = jnp.transpose(jnp.concatenate([o_ref[here, :], o_ref[there, :]], axis=0).astype(jnp.float32))
        prod = do_t * o_t
        e_heads, ds_heads, do_heads, q_heads, dq_heads = [], [], [], [], []
        for h in range(2):
            mine = slice(h * half, (h + 1) * half)
            inverse = linv_ref[0, h * tiles + b : h * tiles + b + 1, :]
            delta = jnp.sum(prod[mine], axis=0, keepdims=True) * inverse
            scaled = do_t[mine] * inverse
            blank = jnp.zeros_like(scaled)
            do_head = jnp.concatenate([scaled, blank] if h == 0 else [blank, scaled], axis=0).astype(jnp.bfloat16)
            e_all, ds_all = [], []
            for kb in near:
                d = b - kb + reach
                rows = slice(kb * tile, (kb + 1) * tile)
                e = e_ref[0, h, b, rows, :]
                dp = dot_f32(v_ref[rows, :], do_head)
                ds = e.astype(jnp.float32) * (dp - delta)
                g_acc[h, :, d * tile : (d + 1) * tile] += ds[:, :tile] + ds[:, tile:]
                e_all.append(e)
                ds_all.append(ds.astype(jnp.bfloat16))
            ds_all = jnp.concatenate(ds_all, axis=0)
            e_heads.append(jnp.concatenate(e_all, axis=0))
            ds_heads.append(ds_all)
            do_heads.append(do_head)
            in_head = (lane >= h * half) & (lane < (h + 1) * half)
            q_heads.append(jnp.where(in_head, q_tile.astype(jnp.float32), 0.0).astype(jnp.bfloat16))
            dq_heads.append(dot_f32(k_t[mine, keys], ds_all))
        dv_acc[keys, :] += dot_f32(jnp.concatenate(e_heads, axis=1), jnp.concatenate(do_heads, axis=1), NT)
        dk_acc[keys, :] += dot_f32(jnp.concatenate(ds_heads, axis=1), jnp.concatenate(q_heads, axis=0))
        dq = (jnp.transpose(jnp.concatenate(dq_heads, axis=0)) * 0.125).astype(jnp.bfloat16)
        dq_ref[here, :] = dq[:tile]
        dq_ref[there, :] = dq[tile:]
    dk_ref[...] = (dk_acc[...] * 0.125).astype(jnp.bfloat16)
    dv_ref[...] = dv_acc[...].astype(jnp.bfloat16)
    row = lax.broadcasted_iota(jnp.int32, (8, wide), 0)
    for h in range(2):
        fold = g_acc[h, tile - 8 : tile, :]
        for a in range(tile // 8 - 2, -1, -1):
            fold = g_acc[h, 8 * a : 8 * a + 8, :] + pltpu.roll(fold, wide - 8, 1)
        for bit in (1, 2, 4):
            fold = jnp.where((row & bit) != 0, pltpu.roll(fold, wide - bit, 1), fold)
        band_ref[h] = jnp.sum(fold, axis=0, keepdims=True)


def attend_back(q, k, v, do, o, e, linv):
    tokens, width = q.shape
    row_len = k.shape[0]
    pairs = width // tile
    tiles = row_len // tile
    pair_block = lambda rows: pl.BlockSpec((rows, tile), lambda p: (0, p))
    return pl.pallas_call(
        attend_back_kernel,
        grid=(pairs,),
        in_specs=[
            pair_block(tokens),
            pair_block(row_len),
            pair_block(row_len),
            pair_block(tokens),
            pair_block(tokens),
            pl.BlockSpec((1, 2, tiles, row_len, 2 * tile), lambda p: (p, 0, 0, 0, 0)),
            pl.BlockSpec((1, 2 * tiles, 2 * tile), lambda p: (p, 0, 0)),
        ],
        out_specs=[
            pair_block(tokens),
            pair_block(row_len),
            pair_block(row_len),
            pl.BlockSpec((2, 1, wide), lambda p: (p, 0, 0)),
        ],
        out_shape=[
            jax.ShapeDtypeStruct((tokens, width), jnp.bfloat16),
            jax.ShapeDtypeStruct((row_len, width), jnp.bfloat16),
            jax.ShapeDtypeStruct((row_len, width), jnp.bfloat16),
            jax.ShapeDtypeStruct((2 * pairs, 1, wide), jnp.float32),
        ],
        scratch_shapes=[
            pltpu.VMEM((row_len, tile), jnp.float32),
            pltpu.VMEM((row_len, tile), jnp.float32),
            pltpu.VMEM((2, tile, wide), jnp.float32),
        ],
        compiler_params=pltpu.CompilerParams(vmem_limit_bytes=40 * 1024 * 1024),
        cost_estimate=pl.CostEstimate(
            flops=pairs * 2 * 2 * 4 * 2 * row_len * row_len * 128,
            bytes_accessed=pairs * 2 * tiles * row_len * 2 * tile * 2,
            transcendentals=0,
        ),
        name="attend_back",
    )(q, k, v, do, o, e, linv)


def layer_norm(values, gain_vec, shift_vec):
    centre = jnp.mean(values, axis=-1, keepdims=True)
    centred = values - centre
    variance = jnp.mean(centred * centred, axis=-1, keepdims=True)
    inv_scale = lax.rsqrt(variance + norm_eps)
    normed = centred * inv_scale
    return (normed * gain_vec + shift_vec, normed, inv_scale)


def norm_back(upstream, normed, inv_scale, gain_vec):
    scaled = upstream * gain_vec
    centre = jnp.mean(scaled, axis=-1, keepdims=True)
    along_normed = jnp.mean(scaled * normed, axis=-1, keepdims=True)
    return inv_scale * (scaled - centre - normed * along_normed)


def gelu_parts(pre_act):
    normal_cdf = 0.5 * (1.0 + lax.erf(pre_act * root_half))
    slope = normal_cdf + pre_act * jnp.exp(-0.5 * pre_act * pre_act) * root_two_pi_inv
    return (pre_act * normal_cdf, slope)


def exchange(value, axis_name, bit):
    count = lax.axis_size(axis_name)
    return lax.ppermute(value, axis_name, [(i, i ^ bit) for i in range(count)])


def scatter_sum(own_part, order):
    count = lax.axis_size("dp")
    index = lax.axis_index("dp")
    rows, n = own_part.shape
    block = rows // count
    left = list(range(count.bit_length() - 2, -1, -1))
    value = own_part
    for bit in order:
        at = left.index(bit)
        split = value.reshape(2**at, 2, 2 ** (len(left) - at - 1), block, n)
        mine = (index >> bit) & 1
        sent = lax.dynamic_index_in_dim(split, 1 - mine, 1, keepdims=False).astype(jnp.bfloat16)
        kept = lax.dynamic_index_in_dim(split, mine, 1, keepdims=False)
        value = kept.astype(jnp.float32) + exchange(sent, "dp", 1 << bit).astype(jnp.float32)
        left.remove(bit)
    return value.reshape(block, n)


def sum_all(vector):
    for bit in [1 << b for b in range(lax.axis_size("dp").bit_length() - 1)]:
        vector = vector + exchange(vector, "dp", bit)
    return vector + exchange(vector, "tensor", 1)


def local(
    content_input,
    query_input,
    segment_ids,
    orders,
    predicted,
    query_weight,
    query_bias,
    key_weight,
    value_weight,
    value_bias,
    out_weight,
    out_bias,
    first_gain,
    first_shift,
    up_weight,
    up_bias,
    down_weight,
    down_bias,
    second_gain,
    second_shift,
    bias_table,
    content_upstream,
    query_upstream,
):
    tensor_index = lax.axis_index("tensor")
    row_len = segment_ids.shape[1]
    bits = lax.axis_size("dp").bit_length() - 1
    ways = (
        list(range(bits)),
        [1, 0] + list(range(2, bits)),
        list(range(2, bits)) + [0, 1],
    )

    def cross(value):
        return exchange(value, "tensor", 1)

    def half_of(first, second):
        return jnp.where(tensor_index == 0, first, second)

    query_w = (query_weight, cross(query_weight))
    key_w = (key_weight, cross(key_weight))
    value_w = (value_weight, cross(value_weight))
    query_b = (query_bias, cross(query_bias))
    value_b = (value_bias, cross(value_bias))
    table = jnp.concatenate([bias_table, cross(bias_table)], axis=1)
    out_w = (out_weight, cross(out_weight))
    up_w = (up_weight, cross(up_weight))
    up_b = (up_bias, cross(up_bias))
    down_w = (down_weight, cross(down_weight))

    def own_rows(value):
        return lax.dynamic_slice_in_dim(value, tensor_index * row_len, row_len, 0)

    content = own_rows(content_input)
    streams = jnp.concatenate([content, own_rows(query_input)], axis=0)
    one_row = lambda value: lax.dynamic_index_in_dim(value, tensor_index, 0, keepdims=False)
    info = jnp.stack([one_row(segment_ids), one_row(orders), one_row(predicted)]).astype(jnp.float32)
    info = jnp.concatenate([info, jnp.zeros((5, row_len), jnp.float32)], axis=0)

    heads = bias_table.shape[1]
    one_hot = jnp.asarray(band_one_hot(bias_table.shape[0]))
    band_rows = jnp.einsum("mb,bh->hm", one_hot, table, precision=lax.Precision.HIGHEST)[:, None, :]

    saved = []
    for s in range(2):
        q = (dot_f32(streams, query_w[s]) + query_b[s]).astype(jnp.bfloat16)
        k = dot_f32(content, key_w[s]).astype(jnp.bfloat16)
        v = (dot_f32(content, value_w[s]) + value_b[s]).astype(jnp.bfloat16)
        o, e, linv = attend(info, band_rows[s * heads : (s + 1) * heads], q, k, v)
        saved.append((q, k, v, o, e, linv))
    mixed = [saved[0][3], saved[1][3]]
    attn = dot_f32(mixed[0], out_w[0]) + dot_f32(mixed[1], out_w[1])
    first, first_normed, first_inv = layer_norm(
        streams.astype(jnp.float32) + attn + out_bias, first_gain, first_shift
    )
    first_low = first.astype(jnp.bfloat16)
    hidden, slope = [], []
    for s in range(2):
        act, grad = gelu_parts(dot_f32(first_low, up_w[s]) + up_b[s])
        hidden.append(act.astype(jnp.bfloat16))
        slope.append(grad.astype(jnp.bfloat16))
    down = dot_f32(hidden[0], down_w[0]) + dot_f32(hidden[1], down_w[1])
    final, second_normed, second_inv = layer_norm(first + down + down_bias, second_gain, second_shift)
    final_low = final.astype(jnp.bfloat16)

    upstream = jnp.concatenate([content_upstream, query_upstream], axis=0).astype(jnp.float32)
    second_grad = norm_back(upstream, second_normed, second_inv, second_gain)
    gain_two_grad = jnp.sum(upstream * second_normed, axis=0)
    shift_two_grad = jnp.sum(upstream, axis=0)
    down_bias_grad = jnp.sum(second_grad, axis=0)
    down_low = second_grad.astype(jnp.bfloat16)

    TN = (((0,), (0,)), ((), ()))

    def pair_sum(make, order):
        far = cross(make(1).astype(jnp.bfloat16))
        return scatter_sum(make(0) + far.astype(jnp.float32), order)

    down_weight_grad = pair_sum(lambda s: dot_f32(down_low, hidden[s], TN), ways[0])
    up_low = [(dot_f32(down_low, down_w[s], NT) * slope[s].astype(jnp.float32)).astype(jnp.bfloat16) for s in range(2)]
    up_weight_grad = pair_sum(lambda s: dot_f32(first_low, up_low[s], TN), ways[1])
    up_bias_grad = [jnp.sum(up_low[s].astype(jnp.float32), axis=0) for s in range(2)]
    first_back = second_grad + dot_f32(up_low[0], up_w[0], NT) + dot_f32(up_low[1], up_w[1], NT)
    residual = norm_back(first_back, first_normed, first_inv, first_gain)
    gain_one_grad = jnp.sum(first_back * first_normed, axis=0)
    shift_one_grad = jnp.sum(first_back, axis=0)
    out_bias_grad = jnp.sum(residual, axis=0)
    attn_low = residual.astype(jnp.bfloat16)
    out_weight_grad = pair_sum(lambda s: dot_f32(attn_low, mixed[s], TN), ways[2])

    grads = [None, None]
    for s in (1, 0):
        q, k, v, o, e, linv = saved[s]
        mixed_grad = dot_f32(attn_low, out_w[s], NT).astype(jnp.bfloat16)
        grads[s] = attend_back(q, k, v, mixed_grad, o, e, linv)
    query_weight_grad = pair_sum(lambda s: dot_f32(streams, grads[s][0], TN), ways[0])
    key_weight_grad = pair_sum(lambda s: dot_f32(content, grads[s][1], TN), ways[1])
    value_weight_grad = pair_sum(lambda s: dot_f32(content, grads[s][2], TN), ways[2])
    query_bias_grad = [jnp.sum(grads[s][0].astype(jnp.float32), axis=0) for s in range(2)]
    value_bias_grad = [jnp.sum(grads[s][2].astype(jnp.float32), axis=0) for s in range(2)]
    band_grads = jnp.concatenate([grads[s][3][:, 0, :] for s in range(2)], axis=0)
    table_grad = jnp.einsum("mb,hm->hb", one_hot, band_grads, precision=lax.Precision.HIGHEST)
    from_query = dot_f32(grads[0][0], query_w[0], NT) + dot_f32(grads[1][0], query_w[1], NT) + residual
    content_grad = from_query[:row_len]
    for s in range(2):
        content_grad = content_grad + dot_f32(grads[s][1], key_w[s], NT) + dot_f32(grads[s][2], value_w[s], NT)
    query_grad = from_query[row_len:]

    def in_order(pair):
        return jnp.concatenate([half_of(pair[0], pair[1]), half_of(pair[1], pair[0])], axis=0)

    pieces = [
        gain_one_grad,
        shift_one_grad,
        out_bias_grad,
        gain_two_grad,
        shift_two_grad,
        down_bias_grad,
        in_order(query_bias_grad),
        in_order(value_bias_grad),
        in_order(up_bias_grad),
        in_order([table_grad[:heads], table_grad[heads:]]).reshape(-1),
    ]
    summed = sum_all(jnp.concatenate(pieces))
    ends = np.cumsum([0] + [piece.shape[0] for piece in pieces])
    out = [summed[ends[i] : ends[i + 1]] for i in range(len(pieces))]
    return (
        final_low[:row_len],
        final_low[row_len:],
        content_grad,
        query_grad,
        query_weight_grad,
        key_weight_grad,
        value_weight_grad,
        out_weight_grad.T,
        up_weight_grad,
        down_weight_grad.T,
        out[6],
        out[7],
        out[2],
        out[0],
        out[1],
        out[8],
        out[5],
        out[3],
        out[4],
        out[9].reshape(2 * heads, -1).T,
    )


def solution(mesh):
    placed = (
        P("dp", None),
        P("dp", None),
        P("dp", None),
        P("dp", None),
        P("dp", None),
        P(None, "tensor"),
        P("tensor"),
        P(None, "tensor"),
        P(None, "tensor"),
        P("tensor"),
        P("tensor", None),
        P(),
        P(),
        P(),
        P(None, "tensor"),
        P("tensor"),
        P("tensor", None),
        P(),
        P(),
        P(),
        P(None, "tensor"),
        P(("dp", "tensor"), None),
        P(("dp", "tensor"), None),
    )
    rows_out = P(("dp", "tensor"), None)
    return jax.shard_map(
        local,
        mesh=mesh,
        in_specs=placed,
        out_specs=(
            rows_out,
            rows_out,
            rows_out,
            rows_out,
            P("dp", "tensor"),
            P("dp", "tensor"),
            P("dp", "tensor"),
            P("tensor", "dp"),
            P("dp", "tensor"),
            P("tensor", "dp"),
        )
        + (P(),) * 10,
        check_vma=False,
    )
```

```python
import jax
import jax.numpy as jnp
import numpy as np
from jax import lax
from jax.experimental import pallas as pl
from jax.experimental.pallas import tpu as pltpu
from jax.sharding import PartitionSpec as P

norm_eps = 1e-05
big_negative = -1e30
root_half = 0.7071067811865476
root_two_pi_inv = 0.3989422804014327
bf16 = jnp.bfloat16
f32 = jnp.float32

tile = 128
reach = 2
span = (2 * reach + 1) * tile
wide = span + tile
chunk = 512
side = 256
block = 64
strip = 32
repeat = 4
TN = (((0,), (0,)), ((), ()))
NT = (((1,), (1,)), ((), ()))
NN = (((1,), (0,)), ((), ()))
vmem_limit = 60 * 1024 * 1024


def dot(left, right, dims=NN):
    return lax.dot_general(left, right, dims, preferred_element_type=f32)


def bucket_of(offset):
    distance = np.abs(offset)
    limits = 8.0 * 2.0 ** (np.arange(1, 8) / 2.0)
    counted = (distance[..., None] >= limits).sum(axis=-1)
    bucket = np.where(distance < 8, distance, 8 + counted)
    return (np.minimum(bucket, 15) + 16 * (offset < 0)).astype(np.int32)


def band_buckets():
    place = np.arange(wide)
    return bucket_of(np.where(place < span, place, place - wide) - reach * tile)


def key_tiles(b, tiles):
    return list(range(max(0, b - reach), min(tiles - 1, b + reach) + 1))


def whole(value):
    return pl.BlockSpec(value.shape, lambda *_: (0,) * len(value.shape))


def params():
    return pltpu.CompilerParams(vmem_limit_bytes=vmem_limit)


def attend_kernel(
    part, content_ref, query_ref, seg_ref, order_ref, flag_ref, bucket_ref, table_ref, wq_ref, wk_ref, wv_ref, bq_ref, bv_ref,
    q_ref, k_ref, v_ref, o_ref, ot_ref, e_ref, linv_ref, *rest,
):
    mask_ref, bias_ref, score_ref = rest[-3:]
    ahead = score_ref.shape[0]
    row_len = k_ref.shape[0]
    tiles = row_len // tile
    p = pl.program_id(0)

    @pl.when(p == 0)
    def _():
        row = pl.ds(part[0], 1)
        seg = seg_ref[row, :].astype(f32)
        order = order_ref[row, :].astype(f32)
        flag = flag_ref[row, :]
        at = lax.broadcasted_iota(jnp.int32, (1, row_len), 1)
        first = (seg != pltpu.roll(seg, 1, 1)) | (at == 0)
        key_content = jnp.where(flag == 0, -1.0, order)
        key_query = jnp.where(first, -1.0, key_content)

        def as_column(row):
            return jnp.transpose(jnp.broadcast_to(row, (tile, row_len)))

        seg_col, content_col, query_col = as_column(seg), as_column(key_content), as_column(key_query)
        for b in range(tiles):
            here = slice(b * tile, (b + 1) * tile)
            same = seg_col == seg[:, here]
            mask_ref[b, :, :tile] = jnp.where(same & (content_col <= order[:, here]), 0.0, big_negative)
            mask_ref[b, :, tile:] = jnp.where(same & (query_col < order[:, here]), 0.0, big_negative)
        for n, one_ref in enumerate((bq_ref, bv_ref)):
            flat = one_ref[...].reshape(1, -1)
            for j in range(flat.shape[1] // tile):
                bias_ref[8 * n + j : 8 * n + j + 1, :] = flat[:, j * tile : (j + 1) * tile]
        if len(rest) == 4:
            for b in range(tiles):
                here = slice(b * tile, (b + 1) * tile)
                there = slice(row_len + b * tile, row_len + (b + 1) * tile)
                rest[0][:, here] = jnp.transpose(content_ref[here, :].astype(f32)).astype(bf16)
                rest[0][:, there] = jnp.transpose(query_ref[here, :].astype(f32)).astype(bf16)

    lane = lax.broadcasted_iota(jnp.int32, (1, tile), 1)
    half = tile // 2
    bq, bv = bias_ref[pl.ds(p, 1), :], bias_ref[pl.ds(p + 8, 1), :]
    q_ref[:row_len, :] = (dot(content_ref[...], wq_ref[...]) + bq).astype(bf16)
    q_ref[row_len:, :] = (dot(query_ref[...], wq_ref[...]) + bq).astype(bf16)
    kv = dot(content_ref[...], jnp.concatenate([wk_ref[...], wv_ref[...]], axis=1))
    k_ref[...] = kv[:, :tile].astype(bf16)
    v_ref[...] = (kv[:, tile:] + bv).astype(bf16)
    v_t = jnp.transpose(v_ref[...].astype(f32)).astype(bf16)
    keys = k_ref[...].astype(f32) * 0.125
    buckets = bucket_ref[...]
    parts = [[None, None] for _ in range(tiles)]
    heads_in, bands = [], []
    for h in range(2):
        in_head = (lane >= h * half) & (lane < (h + 1) * half)
        heads_in.append(jnp.where(in_head, keys, 0.0).astype(bf16))
        band_row = jnp.zeros((1, wide), f32)
        for n in range(table_ref.shape[0]):
            band_row = jnp.where(buckets == n, table_ref[n, 2 * p + h], band_row)
        bands.append(pltpu.roll(jnp.broadcast_to(band_row, (tile, wide)), 0, 1, stride=1, stride_axis=0))
    turns = [(h, b) for b in range(tiles) for h in range(2)]

    def score(turn):
        h, b = turns[turn]
        q_tile = jnp.concatenate(
            [q_ref[b * tile : (b + 1) * tile, :], q_ref[row_len + b * tile : row_len + (b + 1) * tile, :]], axis=0
        )
        top = None
        for kb in key_tiles(b, tiles):
            d = b - kb + reach
            rows = slice(kb * tile, (kb + 1) * tile)
            bias = bands[h][:, d * tile : (d + 1) * tile]
            s = dot(heads_in[h][rows, :], q_tile, NT)
            s = s + jnp.concatenate([bias, bias], axis=1) + mask_ref[b, rows, :]
            score_ref[turn % ahead, rows, :] = s
            one_top = jnp.max(s, axis=0, keepdims=True)
            top = one_top if top is None else jnp.maximum(top, one_top)
        return top

    def weigh(turn, top):
        h, b = turns[turn]
        near = key_tiles(b, tiles)
        total = None
        weights = []
        for kb in near:
            rows = slice(kb * tile, (kb + 1) * tile)
            e = jnp.exp(score_ref[turn % ahead, rows, :] - top)
            one_total = jnp.sum(e, axis=0, keepdims=True)
            total = one_total if total is None else total + one_total
            e = e.astype(bf16)
            e_ref[0, h, b, rows, :] = e
            weights.append(e)
        inverse = 1.0 / total
        linv_ref[0, h * tiles + b : h * tiles + b + 1, :] = inverse
        mixed = dot(
            v_t[h * half : (h + 1) * half, near[0] * tile : (near[-1] + 1) * tile], jnp.concatenate(weights, axis=0)
        )
        parts[b][h] = mixed * inverse

    tops = [score(turn) for turn in range(ahead - 1)]
    for turn in range(len(turns)):
        if turn + ahead - 1 < len(turns):
            tops.append(score(turn + ahead - 1))
        weigh(turn, tops[turn])
    for b in range(tiles):
        both = jnp.concatenate(parts[b], axis=0)
        both_t = jnp.transpose(both).astype(bf16)
        both = both.astype(bf16)
        here = slice(b * tile, (b + 1) * tile)
        there = slice(row_len + b * tile, row_len + (b + 1) * tile)
        o_ref[here, :] = both_t[:tile]
        o_ref[there, :] = both_t[tile:]
        ot_ref[:, here] = both[:, :tile]
        ot_ref[:, there] = both[:, tile:]


def attend(part, content, query, rows, buckets, table, wq, wk, wv, bq, bv, keep_t):
    row_len = rows[0].shape[1]
    tokens = 2 * row_len
    model, width = wq.shape
    pairs = width // tile
    tiles = row_len // tile
    own = lambda value: pl.BlockSpec((row_len, value.shape[1]), lambda p, part: (part[0], 0))
    cols = lambda n: pl.BlockSpec((n, tile), lambda p, part: (0, p))
    out = lambda *shape: jax.ShapeDtypeStruct(shape, bf16)
    out_specs = [
        cols(tokens),
        cols(row_len),
        cols(row_len),
        cols(tokens),
        pl.BlockSpec((tile, tokens), lambda p, part: (p, 0)),
        pl.BlockSpec((1, 2, tiles, row_len, 2 * tile), lambda p, part: (p, 0, 0, 0, 0)),
        pl.BlockSpec((1, 2 * tiles, 2 * tile), lambda p, part: (p, 0, 0)),
    ]
    out_shape = [
        out(tokens, width),
        out(row_len, width),
        out(row_len, width),
        out(tokens, width),
        out(width, tokens),
        out(pairs, 2, tiles, row_len, 2 * tile),
        jax.ShapeDtypeStruct((pairs, 2 * tiles, 2 * tile), f32),
    ]
    if keep_t:
        out_specs.append(pl.BlockSpec((model, tokens), lambda p, part: (0, 0)))
        out_shape.append(out(model, tokens))
    return pl.pallas_call(
        attend_kernel,
        grid_spec=pltpu.PrefetchScalarGridSpec(
            num_scalar_prefetch=1,
            grid=(pairs,),
            in_specs=[own(content), own(query)]
            + [whole(row) for row in rows]
            + [whole(buckets), pl.BlockSpec(memory_space=pltpu.SMEM)]
            + [cols(model)] * 3
            + [whole(bq), whole(bv)],
            out_specs=out_specs,
            scratch_shapes=[pltpu.VMEM((tiles, row_len, 2 * tile), f32), pltpu.VMEM((16, tile), f32), pltpu.VMEM((4, row_len, 2 * tile), f32)],
        ),
        out_shape=out_shape,
        compiler_params=params(),
        cost_estimate=pl.CostEstimate(flops=4_000_000_000, bytes_accessed=12_000_000, transcendentals=3_000_000),
        name="attend",
    )(part, content, query, *rows, buckets, table, wq, wk, wv, bq, bv)


def attend_back_kernel(
    al_ref, wo_ref, ot_ref, q_ref, k_ref, v_ref, e_ref, linv_ref, xt_ref, hot_ref,
    dwq_ref, dwk_ref, dwv_ref, small_ref, dq_ref, dk_ref, dv_ref, dk_acc, dv_acc, g_acc, dp_ref, ds_ref,
):
    ahead = dp_ref.shape[0]
    row_len = k_ref.shape[0]
    tiles = row_len // tile
    half = tile // 2
    p = pl.program_id(0)
    lane = lax.broadcasted_iota(jnp.int32, (1, tile), 1)
    k_t = jnp.transpose(k_ref[...].astype(f32)).astype(bf16)
    do_all = dot(wo_ref[...], al_ref[...], NT).astype(bf16).astype(f32)
    dk_acc[...] = jnp.zeros_like(dk_acc)
    dv_acc[...] = jnp.zeros_like(dv_acc)
    g_acc[...] = jnp.zeros_like(g_acc)
    turns = [(h, b) for b in range(tiles) for h in range(2)]
    deltas, do_heads, q_heads = {}, {}, {}

    def places(b):
        return slice(b * tile, (b + 1) * tile), slice(row_len + b * tile, row_len + (b + 1) * tile)

    def spread(turn):
        h, b = turns[turn]
        here, there = places(b)
        mine = slice(h * half, (h + 1) * half)
        inverse = linv_ref[0, h * tiles + b : h * tiles + b + 1, :]
        do_t = jnp.concatenate([do_all[mine, here], do_all[mine, there]], axis=1)
        o_t = jnp.concatenate([ot_ref[mine, here], ot_ref[mine, there]], axis=1).astype(f32)
        deltas[turn] = jnp.sum(do_t * o_t, axis=0, keepdims=True) * inverse
        scaled = do_t * inverse
        blank = jnp.zeros_like(scaled)
        do_heads[turn] = jnp.concatenate([scaled, blank] if h == 0 else [blank, scaled], axis=0).astype(bf16)
        q_tile = jnp.concatenate([q_ref[here, :], q_ref[there, :]], axis=0)
        in_head = (lane >= h * half) & (lane < (h + 1) * half)
        q_heads[turn] = jnp.where(in_head, q_tile.astype(f32), 0.0).astype(bf16)
        for kb in key_tiles(b, tiles):
            rows = slice(kb * tile, (kb + 1) * tile)
            dp_ref[turn % ahead, rows, :] = dot(v_ref[rows, :], do_heads[turn])

    def combine(turn):
        h, b = turns[turn]
        for kb in key_tiles(b, tiles):
            d = b - kb + reach
            rows = slice(kb * tile, (kb + 1) * tile)
            ds = e_ref[0, h, b, rows, :].astype(f32) * (dp_ref[turn % ahead, rows, :] - deltas[turn])
            g_acc[h, :, d * tile : (d + 1) * tile] += ds[:, :tile] + ds[:, tile:]
            ds_ref[b % 2, h, rows, :] = ds.astype(bf16)

    def gather(b):
        here, there = places(b)
        near = key_tiles(b, tiles)
        keys = slice(near[0] * tile, (near[-1] + 1) * tile)
        two = (2 * b, 2 * b + 1)
        dv_acc[keys, :] += dot(
            jnp.concatenate([e_ref[0, h, b, keys, :] for h in range(2)], axis=1),
            jnp.concatenate([do_heads[turn] for turn in two], axis=1),
            NT,
        )
        dk_acc[keys, :] += dot(
            jnp.concatenate([ds_ref[b % 2, h, keys, :] for h in range(2)], axis=1),
            jnp.concatenate([q_heads[turn] for turn in two], axis=0),
        )
        dq_t = [dot(k_t[h * half : (h + 1) * half, keys], ds_ref[b % 2, h, keys, :]) for h in range(2)]
        dq = (jnp.transpose(jnp.concatenate(dq_t, axis=0)) * 0.125).astype(bf16)
        dq_ref[here, :] = dq[:tile]
        dq_ref[there, :] = dq[tile:]

    for turn in range(ahead - 1):
        spread(turn)
    for turn in range(len(turns)):
        if turn + ahead - 1 < len(turns):
            spread(turn + ahead - 1)
        combine(turn)
        if turn % 2 and turn >= 3:
            gather(turn // 2 - 1)
    gather(tiles - 1)
    dk = (dk_acc[...] * 0.125).astype(bf16)
    dv = dv_acc[...].astype(bf16)
    dq = dq_ref[...]
    dk_ref[...] = dk
    dv_ref[...] = dv
    dwq_ref[...] = dot(xt_ref[...], dq).astype(bf16)
    dkv = dot(xt_ref[:, :row_len], jnp.concatenate([dk, dv], axis=1)).astype(bf16)
    dwk_ref[...] = dkv[:, :tile]
    dwv_ref[...] = dkv[:, tile:]
    row = lax.broadcasted_iota(jnp.int32, (8, wide), 0)
    small_ref[0, 0:1, :] = jnp.sum(dq.astype(f32), axis=0, keepdims=True)
    small_ref[0, 1:2, :] = jnp.sum(dv.astype(f32), axis=0, keepdims=True)
    for h in range(2):
        folds = [g_acc[h, a : a + 8, :] for a in range(0, tile, 8)]
        step = 8
        while len(folds) > 1:
            folds = [folds[a] + pltpu.roll(folds[a + 1], wide - step, 1) for a in range(0, len(folds), 2)]
            step *= 2
        fold = folds[0]
        for bit in (1, 2, 4):
            fold = jnp.where((row & bit) != 0, pltpu.roll(fold, wide - bit, 1), fold)
        by_bucket = lax.dot_general(fold, hot_ref[...], NN, precision=lax.Precision.HIGHEST, preferred_element_type=f32)
        small_ref[0, 2 + h : 3 + h, :] = jnp.sum(by_bucket, axis=0, keepdims=True)


def attend_back(from_pair, pairs, al, wo, ot, q, k, v, e, linv, xt, hot):
    tokens, model = al.shape
    width = pairs * tile
    row_len = k.shape[0]
    tiles = row_len // tile
    cols = lambda n: pl.BlockSpec((n, tile), lambda p: (0, p + from_pair))
    rows = lambda n: pl.BlockSpec((tile, n), lambda p: (p + from_pair, 0))
    cols_out = lambda n: pl.BlockSpec((n, tile), lambda p: (0, p))
    shape = jax.ShapeDtypeStruct
    return pl.pallas_call(
        attend_back_kernel,
        grid=(pairs,),
        in_specs=[
            once(al),
            rows(model),
            rows(tokens),
            cols(tokens),
            cols(row_len),
            cols(row_len),
            pl.BlockSpec((1, 2, tiles, row_len, 2 * tile), lambda p: (p + from_pair, 0, 0, 0, 0)),
            pl.BlockSpec((1, 2 * tiles, 2 * tile), lambda p: (p + from_pair, 0, 0)),
            once(xt),
            once(hot),
        ],
        out_specs=[cols_out(model)] * 3
        + [pl.BlockSpec((1, 8, tile), lambda p: (p, 0, 0)), cols_out(tokens), cols_out(row_len), cols_out(row_len)],
        out_shape=[shape((model, width), bf16)] * 3
        + [shape((pairs, 8, tile), f32), shape((tokens, width), bf16)]
        + [shape((row_len, width), bf16)] * 2,
        scratch_shapes=[
            pltpu.VMEM((row_len, tile), f32),
            pltpu.VMEM((row_len, tile), f32),
            pltpu.VMEM((2, tile, wide), f32),
            pltpu.VMEM((3, row_len, 2 * tile), f32),
            pltpu.VMEM((2, 2, row_len, 2 * tile), bf16),
        ],
        compiler_params=params(),
        cost_estimate=pl.CostEstimate(flops=pairs * 4_000_000_000, bytes_accessed=20_000_000, transcendentals=0),
        name="attend_back",
    )(al, wo, ot, q, k, v, e, linv, xt, hot)


def inputs_back_kernel(residual_ref, *refs):
    content_ref, query_ref = refs[-2:]
    row_len = content_ref.shape[0]
    content = residual_ref[:row_len, :]
    query = residual_ref[row_len:, :]
    for at in range(0, len(refs) - 2, 6):
        dq_ref, dk_ref, dv_ref, wq_ref, wk_ref, wv_ref = refs[at : at + 6]
        wq = wq_ref[...]
        content = content + dot(dq_ref[:row_len, :], wq, NT) + dot(dk_ref[...], wk_ref[...], NT) + dot(dv_ref[...], wv_ref[...], NT)
        query = query + dot(dq_ref[row_len:, :], wq, NT)
    content_ref[...] = content
    query_ref[...] = query


def inputs_back(residual, groups):
    tokens, model = residual.shape
    shape = jax.ShapeDtypeStruct((tokens // 2, model), f32)
    args = [residual]
    specs = [once(residual)]
    for grads, weights, at, width in groups:
        args += list(grads) + list(weights)
        specs += [once(one) for one in grads]
        specs += [pl.BlockSpec((model, width), lambda i, at=at: (0, at), pipeline_mode=pl.Buffered(1)) for _ in weights]
    return pl.pallas_call(
        inputs_back_kernel,
        grid=(1,),
        in_specs=specs,
        out_specs=[once(shape)] * 2,
        out_shape=[shape] * 2,
        compiler_params=params(),
        cost_estimate=pl.CostEstimate(flops=2_500_000_000, bytes_accessed=16_000_000, transcendentals=0),
        name="inputs_back",
    )(*args)


def normed_of(values):
    centre = jnp.mean(values, axis=-1, keepdims=True)
    centred = values - centre
    variance = jnp.mean(centred * centred, axis=-1, keepdims=True)
    inv_scale = lax.rsqrt(variance + norm_eps)
    return centred * inv_scale, inv_scale


def norm_back(upstream, normed, inv_scale, gain_vec):
    scaled = upstream * gain_vec
    centre = jnp.mean(scaled, axis=-1, keepdims=True)
    along_normed = jnp.mean(scaled * normed, axis=-1, keepdims=True)
    return inv_scale * (scaled - centre - normed * along_normed)


def eight(values):
    total = values[0:8]
    for i in range(8, values.shape[0], 8):
        total = total + values[i : i + 8]
    return total


def gelu_parts(u):
    bell = jnp.exp(-0.5 * (u * u))
    t = 1.0 / (1.0 + (0.3275911 * root_half) * jnp.abs(u))
    poly = 0.5307027145
    poly = poly * t - 0.7265760135
    poly = poly * t + 0.7107068705
    poly = poly * t - 0.142248368
    poly = poly * t + 0.127414796
    tail = poly * t * bell
    cdf = jnp.where(u >= 0.0, 1.0 - tail, tail)
    return u * cdf, cdf + (u * root_two_pi_inv) * bell


def feed_kernel(
    part, o0_ref, o1_ref, wo0_ref, wo1_ref, content_ref, query_ref, bo_ref, g1_ref, s1_ref, wu0_ref, wu1_ref, bu0_ref, bu1_ref,
    wd0_ref, wd1_ref, bd_ref, g2_ref, s2_ref, cu_ref, qu_ref,
    normed_out, first_out, second_out, inv_ref, fc_ref, fq_ref, sums_ref, dwd0_ref, dwd1_ref, low0_ref, low1_ref, dbu0_ref, dbu1_ref,
    normed_ref, first_ref, acc_ref, d2_ref, hidden_ref, slope_ref, bu_ref, up_ref, sems,
):
    row_len = content_ref.shape[0]
    bo, g1, s1, bd, g2, s2 = (ref[...].reshape(1, -1) for ref in (bo_ref, g1_ref, s1_ref, bd_ref, g2_ref, s2_ref))
    tokens, model = acc_ref.shape
    steps = pl.num_programs(0)
    i = pl.program_id(0)
    copies = [
        pltpu.make_async_copy(normed_ref, normed_out, sems.at[0]),
        pltpu.make_async_copy(first_ref, first_out, sems.at[1]),
        pltpu.make_async_copy(acc_ref, second_out, sems.at[2]),
    ]

    @pl.when(i == 0)
    def _():
        acc_ref[...] = dot(o0_ref[...], wo0_ref[...]) + dot(o1_ref[...], wo1_ref[...])
        for n, one_ref in enumerate((bu0_ref, bu1_ref)):
            flat = one_ref[...].reshape(1, -1)
            for j in range(flat.shape[1] // chunk):
                at = n * (flat.shape[1] // chunk) + j
                bu_ref[at : at + 1, :] = flat[:, j * chunk : (j + 1) * chunk]
        for s, x_ref in enumerate((content_ref, query_ref)):

            def step(r, _, s=s, x_ref=x_ref):
                from_rows = pl.ds(pl.multiple_of(r * strip, strip), strip)
                rows = pl.ds(pl.multiple_of(s * row_len + r * strip, strip), strip)
                normed, inv = normed_of(x_ref[from_rows, :].astype(f32) + acc_ref[rows, :] + bo)
                first = normed * g1 + s1
                normed_ref[rows, :] = normed
                inv_ref[rows, :] = inv
                first_ref[rows, :] = first.astype(bf16)
                acc_ref[rows, :] = first + bd
                return 0

            lax.fori_loop(0, row_len // strip, step, 0, unroll=repeat)
        copies[1].start()

    def forward(wu_ref, wd_ref):
        bias = bu_ref[pl.ds(i, 1), :]
        splits = [slice(j, j + side) for j in range(0, chunk, side)]
        for j, cols in enumerate(splits):
            up_ref[:, cols] = dot(first_ref[...], wu_ref[:, cols]) + bias[:, cols]
        for cols in splits:
            for r in range(0, tokens, block):
                rows = slice(r, r + block)
                hidden, slope = gelu_parts(up_ref[rows, cols])
                hidden_ref[i, rows, cols] = hidden.astype(bf16)
                slope_ref[i, rows, cols] = slope.astype(bf16)
        acc_ref[...] += dot(hidden_ref[i], wd_ref[...])

    @pl.when(i < steps // 4)
    def _():
        forward(wu0_ref, wd0_ref)

    @pl.when((i >= steps // 4) & (i < steps // 2))
    def _():
        forward(wu1_ref, wd1_ref)

    @pl.when(i == steps // 2 - 1)
    def _():
        sums = (jnp.zeros((8, model), f32),) * 3
        for s, (c_ref, out_ref) in enumerate(((cu_ref, fc_ref), (qu_ref, fq_ref))):

            def step(r, sums, s=s, c_ref=c_ref, out_ref=out_ref):
                from_rows = pl.ds(pl.multiple_of(r * strip, strip), strip)
                rows = pl.ds(pl.multiple_of(s * row_len + r * strip, strip), strip)
                normed, inv = normed_of(acc_ref[rows, :])
                out_ref[from_rows, :] = (normed * g2 + s2).astype(bf16)
                c = c_ref[from_rows, :].astype(f32)
                second = norm_back(c, normed, inv, g2)
                acc_ref[rows, :] = second
                d2_ref[rows, :] = second.astype(bf16)
                return (sums[0] + eight(c * normed), sums[1] + eight(c), sums[2] + eight(second))

            sums = lax.fori_loop(0, row_len // strip, step, sums, unroll=repeat)
        for n in range(3):
            sums_ref[n : n + 1, :] = jnp.sum(sums[n], axis=0, keepdims=True)
        copies[2].start()

    def backward(wd_ref, dwd_ref, low_ref, dbu_ref):
        at = i - steps // 2
        up_ref[...] = dot(d2_ref[...], wd_ref[...], NT)
        dwd_ref[...] = dot(d2_ref[...], hidden_ref[at], TN).astype(bf16)
        total = jnp.zeros((8, chunk), f32)
        for r in range(0, tokens, block):
            rows = slice(r, r + block)
            grad = (up_ref[rows, :] * slope_ref[at, rows, :].astype(f32)).astype(bf16)
            low_ref[rows, :] = grad
            total = total + eight(grad.astype(f32))
        dbu_ref[...] = jnp.sum(total, axis=0, keepdims=True)

    @pl.when((i >= steps // 2) & (i < steps * 3 // 4))
    def _():
        backward(wd0_ref, dwd0_ref, low0_ref, dbu0_ref)

    @pl.when(i >= steps * 3 // 4)
    def _():
        backward(wd1_ref, dwd1_ref, low1_ref, dbu1_ref)

    @pl.when(i == 1)
    def _():
        copies[0].start()

    @pl.when(i == steps - 1)
    def _():
        for copy in copies:
            copy.wait()


def once(value):
    return pl.BlockSpec(value.shape, lambda *_: (0,) * len(value.shape), pipeline_mode=pl.Buffered(1))


def feed(part, o, wo, content, query, bo, g1, s1, wu, bu, wd, bd, g2, s2, cu, qu):
    tokens = o[0].shape[0]
    row_len = cu.shape[0]
    model, width = wu[0].shape
    c = width // chunk
    own = pl.BlockSpec((row_len, model), lambda i, part: (part[0], 0), pipeline_mode=pl.Buffered(1))
    up0 = lambda i: jnp.minimum(i, c - 1)
    up1 = lambda i: jnp.clip(i - c, 0, c - 1)
    down0 = lambda i: jnp.where(i < 2 * c, jnp.minimum(i, c - 1), jnp.minimum(i - 2 * c, c - 1))
    down1 = lambda i: jnp.where(i < 3 * c, jnp.clip(i - c, 0, c - 1), i - 3 * c)
    back0 = lambda i: jnp.clip(i - 2 * c, 0, c - 1)
    back1 = lambda i: jnp.clip(i - 3 * c, 0, c - 1)
    cols = lambda n, at: pl.BlockSpec((n, chunk), lambda i, part: (0, at(i)))
    rows = lambda at: pl.BlockSpec((chunk, model), lambda i, part: (at(i), 0))
    anywhere = pl.BlockSpec(memory_space=pl.ANY)
    shape = jax.ShapeDtypeStruct
    out_shape = [
        shape((tokens, model), f32),
        shape((tokens, model), bf16),
        shape((tokens, model), f32),
        shape((tokens, 1), f32),
        shape((row_len, model), bf16),
        shape((row_len, model), bf16),
        shape((8, model), f32),
    ]
    out_shape += [shape((model, width), bf16)] * 2 + [shape((tokens, width), bf16)] * 2 + [shape((1, width), f32)] * 2
    out_specs = [anywhere] * 3 + [once(one) for one in out_shape[3:7]]
    for n in (model, tokens, 1):
        out_specs += [cols(n, back0), cols(n, back1)]
    return pl.pallas_call(
        feed_kernel,
        grid_spec=pltpu.PrefetchScalarGridSpec(
            num_scalar_prefetch=1,
            grid=(4 * c,),
            in_specs=[once(o[0]), once(o[1]), once(wo[0]), once(wo[1]), own, own, once(bo), once(g1), once(s1)]
            + [cols(model, up0), cols(model, up1), once(bu[0]), once(bu[1]), rows(down0), rows(down1)]
            + [once(bd), once(g2), once(s2), once(cu), once(qu)],
            out_specs=out_specs,
            scratch_shapes=[
                pltpu.VMEM((tokens, model), f32),
                pltpu.VMEM((tokens, model), bf16),
                pltpu.VMEM((tokens, model), f32),
                pltpu.VMEM((tokens, model), bf16),
                pltpu.VMEM((2 * c, tokens, chunk), bf16),
                pltpu.VMEM((2 * c, tokens, chunk), bf16),
                pltpu.VMEM((8, chunk), f32),
                pltpu.VMEM((tokens, chunk), f32),
                pltpu.SemaphoreType.DMA((3,)),
            ],
        ),
        out_shape=out_shape,
        compiler_params=params(),
        cost_estimate=pl.CostEstimate(flops=21_000_000_000, bytes_accessed=40_000_000, transcendentals=6_000_000),
        name="feed",
    )(part, o[0], o[1], wo[0], wo[1], content, query, bo, g1, s1, wu[0], wu[1], bu[0], bu[1], wd[0], wd[1], bd, g2, s2, cu, qu)


def up_back_kernel(
    first_ref, low0_ref, low1_ref, wu0_ref, wu1_ref, g1_ref, inv_ref, normed_in, second_in, o0_in, o1_in,
    dwu0_ref, dwu1_ref, residual_ref, al_ref, sums_ref, dwo0_ref, dwo1_ref,
    acc_ref, normed_ref, second_ref, o0_ref, o1_ref, sems,
):
    tokens, model = acc_ref.shape
    i = pl.program_id(0)
    steps = pl.num_programs(0)
    pairs = ((normed_in, normed_ref), (second_in, second_ref), (o0_in, o0_ref), (o1_in, o1_ref))
    copies = [pltpu.make_async_copy(here, there, sems.at[n]) for n, (here, there) in enumerate(pairs)]

    @pl.when(i == 0)
    def _():
        for copy in copies:
            copy.start()
        acc_ref[...] = jnp.zeros_like(acc_ref)

    def units(low_ref, wu_ref, dwu_ref):
        dwu_ref[...] = dot(first_ref[...], low_ref[...], TN).astype(bf16)
        acc_ref[...] += dot(low_ref[...], wu_ref[...], NT)

    @pl.when(i < steps // 2)
    def _():
        units(low0_ref, wu0_ref, dwu0_ref)

    @pl.when(i >= steps // 2)
    def _():
        units(low1_ref, wu1_ref, dwu1_ref)

    @pl.when(i == steps - 1)
    def _():
        for copy in copies:
            copy.wait()
        g1 = g1_ref[...].reshape(1, -1)

        def step(r, sums):
            rows = pl.ds(pl.multiple_of(r * strip, strip), strip)
            back, normed = acc_ref[rows, :] + second_ref[rows, :], normed_ref[rows, :]
            residual = norm_back(back, normed, inv_ref[rows, :], g1)
            residual_ref[rows, :] = residual
            al_ref[rows, :] = residual.astype(bf16)
            return (sums[0] + eight(back * normed), sums[1] + eight(back), sums[2] + eight(residual))

        sums = lax.fori_loop(0, tokens // strip, step, (jnp.zeros((8, model), f32),) * 3, unroll=repeat)
        for n in range(3):
            sums_ref[n : n + 1, :] = jnp.sum(sums[n], axis=0, keepdims=True)
        dwo0_ref[...] = dot(al_ref[...], o0_ref[...], TN).astype(bf16)
        dwo1_ref[...] = dot(al_ref[...], o1_ref[...], TN).astype(bf16)


def up_back(first, low, wu, g1, inv, normed, second, o):
    tokens, width = low[0].shape
    model = first.shape[1]
    c = width // chunk
    at0 = lambda i: jnp.minimum(i, c - 1)
    at1 = lambda i: jnp.maximum(i - c, 0)
    cols = lambda n, at: pl.BlockSpec((n, chunk), lambda i: (0, at(i)))
    anywhere = pl.BlockSpec(memory_space=pl.ANY)
    shape = jax.ShapeDtypeStruct
    out_shape = [
        shape((model, width), bf16),
        shape((model, width), bf16),
        shape((tokens, model), f32),
        shape((tokens, model), bf16),
        shape((8, model), f32),
        shape((model, o[0].shape[1]), bf16),
        shape((model, o[1].shape[1]), bf16),
    ]
    return pl.pallas_call(
        up_back_kernel,
        grid=(2 * c,),
        in_specs=[once(first), cols(tokens, at0), cols(tokens, at1), cols(model, at0), cols(model, at1), once(g1), once(inv)]
        + [anywhere] * 4,
        out_specs=[cols(model, at0), cols(model, at1)] + [once(one) for one in out_shape[2:]],
        out_shape=out_shape,
        scratch_shapes=[
            pltpu.VMEM((tokens, model), f32),
            pltpu.VMEM((tokens, model), f32),
            pltpu.VMEM((tokens, model), f32),
            pltpu.VMEM(o[0].shape, bf16),
            pltpu.VMEM(o[1].shape, bf16),
            pltpu.SemaphoreType.DMA((4,)),
        ],
        compiler_params=params(),
        cost_estimate=pl.CostEstimate(flops=11_000_000_000, bytes_accessed=30_000_000, transcendentals=0),
        name="up_back",
    )(first, low[0], low[1], wu[0], wu[1], g1, inv, normed, second, o[0], o[1])


def pack_kernel(part, one_ref, two_ref, dbu0_ref, dbu1_ref, *rest):
    smalls, out_ref = rest[:-1], rest[-1]
    first = part[0] == 0
    model = one_ref.shape[1]
    out_ref[...] = jnp.zeros_like(out_ref)
    out_ref[0:3, :] = one_ref[0:3, :]
    out_ref[3:6, :] = two_ref[0:3, :]
    pairs = model // tile // 2
    own = jnp.concatenate([ref[...] for ref in smalls[:-1]], axis=0)
    other = smalls[-1][...]
    for row in range(2):
        halves = [jnp.concatenate([half[n, row : row + 1, :] for n in range(pairs)], axis=1) for half in (own, other)]
        out_ref[6 + row : 7 + row, : model // 2] = jnp.where(first, halves[0], halves[1])
        out_ref[6 + row : 7 + row, model // 2 :] = jnp.where(first, halves[1], halves[0])
    tables = [
        jnp.concatenate([half[n, 2 + h : 3 + h, :] for n in range(pairs) for h in range(2)], axis=1) for half in (own, other)
    ]
    ups = [dbu0_ref[...], dbu1_ref[...]]
    for row, (a, b) in enumerate(((0, 1), (1, 0))):
        out_ref[8 + row : 9 + row, :] = jnp.where(first, tables[a], tables[b])
        up = jnp.where(first, ups[a], ups[b])
        rows = up.shape[1] // model
        for n in range(rows):
            at = 10 + row * rows + n
            out_ref[at : at + 1, :] = up[:, n * model : (n + 1) * model]


def pack(part, one, two, dbu0, dbu1, smalls):
    args = (one, two, dbu0, dbu1) + tuple(smalls)
    model = one.shape[1]
    return pl.pallas_call(
        pack_kernel,
        grid_spec=pltpu.PrefetchScalarGridSpec(
            num_scalar_prefetch=1, grid=(1,), in_specs=[whole(arg) for arg in args], out_specs=pl.BlockSpec((16, model), lambda *_: (0, 0))
        ),
        out_shape=jax.ShapeDtypeStruct((16, model), f32),
        compiler_params=params(),
        name="pack",
    )(part, *args)


def unpack_kernel(mine_ref, far_ref, *outs):
    rows = mine_ref[...] + far_ref[...]
    model = rows.shape[1]
    for n in range(8):
        outs[n][...] = rows[n : n + 1, :].reshape(model)
    up = jnp.concatenate([rows[n : n + 1, :] for n in range(10, 10 + outs[8].shape[0] // model)], axis=1)
    outs[8][...] = up.reshape(outs[8].shape[0])
    heads = [rows[8 + half : 9 + half, n * tile : (n + 1) * tile] for half in range(2) for n in range(model // tile)]
    table = jnp.concatenate(heads + [jnp.zeros((16 - len(heads), tile), f32)], axis=0)
    outs[9][...] = jnp.transpose(table)[: outs[9].shape[0], : len(heads)]


def unpack(mine, far, units, buckets, heads):
    model = mine.shape[1]
    shapes = [(model,)] * 8 + [(units,), (buckets, heads)]
    out_shape = [jax.ShapeDtypeStruct(shape, f32) for shape in shapes]
    return pl.pallas_call(unpack_kernel, out_shape=out_shape, compiler_params=params(), name="unpack")(mine, far)


def exchange(value, axis_name, bit):
    count = lax.axis_size(axis_name)
    return lax.ppermute(value, axis_name, [(i, i ^ bit) for i in range(count)])


class Chain:
    def __init__(self, parts, order):
        self.count = lax.axis_size("dp")
        rows, n = parts[0][0].shape[0], sum(part[0].shape[1] for part in parts)
        self.block, self.n = rows // self.count, n
        self.left = list(range(self.count.bit_length() - 2, -1, -1))
        self.order = list(order)
        sums = [own.astype(f32) + far.astype(f32) for own, far in parts]
        self.value = sums[0] if len(sums) == 1 else jnp.concatenate(sums, axis=1)

    def send(self):
        bit = self.order.pop(0)
        at = self.left.index(bit)
        split = self.value.reshape(2**at, 2, 2 ** (len(self.left) - at - 1), self.block, self.n)
        mine = (lax.axis_index("dp") >> bit) & 1
        sent = lax.dynamic_index_in_dim(split, 1 - mine, 1, keepdims=False).astype(bf16)
        self.kept = lax.dynamic_index_in_dim(split, mine, 1, keepdims=False)
        self.left.remove(bit)
        return exchange(sent, "dp", 1 << bit)

    def take(self, received):
        self.value = self.kept + received.astype(f32)

    def finish(self):
        while self.order:
            self.take(self.send())
        return self.value.reshape(self.block, self.n)


def gate(value, *arrived):
    out = lax.optimization_barrier((value,) + arrived)
    return out if arrived else out[0]


def local(
    content_input,
    query_input,
    segment_ids,
    orders,
    predicted,
    query_weight,
    query_bias,
    key_weight,
    value_weight,
    value_bias,
    out_weight,
    out_bias,
    first_gain,
    first_shift,
    up_weight,
    up_bias,
    down_weight,
    down_bias,
    second_gain,
    second_shift,
    bias_table,
    content_upstream,
    query_upstream,
):
    tensor_index = lax.axis_index("tensor")
    bits = lax.axis_size("dp").bit_length() - 1
    part = tensor_index.astype(jnp.int32).reshape(1)
    far_of = lambda value: exchange(value, "tensor", 1)

    def order(*first):
        first = [bit for bit in first if bit < bits]
        return first + [bit for bit in range(bits) if bit not in first]

    own_attention = (query_weight, key_weight, value_weight, query_bias, value_bias, bias_table)
    far_attention = tuple(far_of(value) for value in own_attention)
    rows = (segment_ids, orders, predicted)
    heads = bias_table.shape[1]
    buckets = band_buckets()
    hot = jnp.asarray((buckets[:, None] == np.arange(tile)[None, :]).astype(np.float32))
    buckets = jnp.asarray(buckets[None, :])

    def attention(values, keep_t):
        wq, wk, wv, bq, bv, table = values
        return attend(part, content_input, query_input, rows, buckets, table, wq, wk, wv, bq, bv, keep_t)

    own = attention(own_attention, True)
    streams_t = own[7]
    sent = gate(own[6], out_weight, up_weight, down_weight, up_bias)[1:]
    out_far, up_far, down_far, up_bias_far = (far_of(value) for value in sent)
    saved = [own[:7], attention(far_attention, False)]
    out_w, up_w, down_w = (out_weight, out_far), (up_weight, up_far), (down_weight, down_far)
    attention_w = [own_attention[:3], far_attention[:3]]
    o = (saved[0][3], saved[1][3])
    normed, first, second, inv, final_c, final_q, sums_two, dwd0, dwd1, low0, low1, dbu0, dbu1 = feed(
        part, o, out_w, content_input, query_input, out_bias, first_gain, first_shift, up_w, (up_bias, up_bias_far), down_w,
        down_bias, second_gain, second_shift, content_upstream, query_upstream,
    )
    far_d = far_of(dwd1)
    dwu0, dwu1, residual, al, sums_one, dwo0, dwo1 = up_back(first, (low0, low1), up_w, first_gain, inv, normed, second, o)
    al, far_d = gate(al, far_d)
    chain_d = Chain([(dwd0, far_d)], order(0, 1))
    coming_d = chain_d.send()
    chain_u = Chain([(dwu0, far_of(dwu1)), (dwo0, far_of(dwo1))], order(2, 0, 1))
    coming_u = chain_u.send()

    def attention_back(s, from_pair, pairs, al):
        q, k, v, _, ot, e, linv = saved[s]
        return attend_back(from_pair, pairs, al, out_w[s], ot, q, k, v, e, linv, streams_t, hot)

    pairs = query_weight.shape[1] // tile
    late = 1
    early = pairs - late
    split, side_width = early * tile, late * tile
    other = attention_back(1, 0, pairs, al)
    far = [far_of(other[i]) for i in range(3)]
    al, coming_d, *held = gate(al, coming_d, *other)
    chain_d.take(coming_d)
    coming_d = chain_d.send()
    own_early = attention_back(0, 0, early, al)
    al, coming_d, coming_u, *far = gate(al, coming_d, coming_u, *far, own_early[0])[:6]
    chain_d.take(coming_d)
    coming_d = chain_d.send()
    chain_u.take(coming_u)
    coming_u = chain_u.send()
    chain_a = Chain([(own_early[i], far[i][:, :split]) for i in range(3)], order(1, 0))
    coming_a = chain_a.send()
    own_late = attention_back(0, early, late, al)
    content_grad, query_grad = inputs_back(
        residual,
        [
            (own_early[4:7], attention_w[0], 0, split),
            (own_late[4:7], attention_w[0], early // late, side_width),
            (other[4:7], attention_w[1], 0, split + side_width),
        ],
    )
    packed = pack(part, sums_one, sums_two, dbu0, dbu1, [own_early[3], own_late[3], other[3]])
    chain_b = Chain([(own_late[i], far[i][:, split:]) for i in range(3)], order(2, 1, 0))
    coming_b = chain_b.send()
    chains = [[chain_d, coming_d], [chain_a, coming_a], [chain_b, coming_b], [chain_u, coming_u]]
    bit = 0
    while any(chain.order for chain, _ in chains) or bit < bits:
        if bit < bits:
            coming = exchange(packed, "dp", 1 << bit)
            bit += 1
        for entry in chains:
            if entry[0].order:
                entry[0].take(entry[1])
                entry[1] = entry[0].send()
        packed = packed + coming
        live = [entry for entry in chains if entry[0].order]
        out = gate(packed, *[entry[1] for entry in live]) if live else [packed]
        packed = out[0]
        for entry, value in zip(live, out[1:]):
            entry[1] = value
    for chain, value in chains:
        chain.take(value)
    down_weight_grad, grads_a, grads_b, up_out = (chain.value.reshape(chain.block, chain.n) for chain, _ in chains)
    small = unpack(packed, far_of(packed), 2 * up_bias.shape[0], bias_table.shape[0], 2 * heads)
    units = up_weight.shape[1]
    query_weight_grad, key_weight_grad, value_weight_grad = (
        jnp.concatenate([grads_a[:, i * split : (i + 1) * split], grads_b[:, i * side_width : (i + 1) * side_width]], axis=1) for i in range(3)
    )
    return (
        final_c,
        final_q,
        content_grad,
        query_grad,
        query_weight_grad,
        key_weight_grad,
        value_weight_grad,
        up_out[:, units:].T,
        up_out[:, :units],
        down_weight_grad.T,
        small[6],
        small[7],
        small[2],
        small[0],
        small[1],
        small[8],
        small[5],
        small[3],
        small[4],
        small[9],
    )


def solution(mesh):
    placed = (
        P("dp", None),
        P("dp", None),
        P("dp", None),
        P("dp", None),
        P("dp", None),
        P(None, "tensor"),
        P("tensor"),
        P(None, "tensor"),
        P(None, "tensor"),
        P("tensor"),
        P("tensor", None),
        P(),
        P(),
        P(),
        P(None, "tensor"),
        P("tensor"),
        P("tensor", None),
        P(),
        P(),
        P(),
        P(None, "tensor"),
        P(("dp", "tensor"), None),
        P(("dp", "tensor"), None),
    )
    rows_out = P(("dp", "tensor"), None)
    return jax.shard_map(
        local,
        mesh=mesh,
        in_specs=placed,
        out_specs=(
            rows_out,
            rows_out,
            rows_out,
            rows_out,
            P("dp", "tensor"),
            P("dp", "tensor"),
            P("dp", "tensor"),
            P("tensor", "dp"),
            P("dp", "tensor"),
            P("tensor", "dp"),
        )
        + (P(),) * 10,
        check_vma=False,
    )
```

```python
import jax
import jax.numpy as jnp
import numpy as np
from jax import lax
from jax.experimental import pallas as pl
from jax.experimental.pallas import tpu as pltpu
from jax.sharding import PartitionSpec as P

norm_eps = 1e-05
big_negative = -1e30
root_half = 0.7071067811865476
root_two_pi_inv = 0.3989422804014327
bf16 = jnp.bfloat16
f32 = jnp.float32

tile = 128
reach = 2
span = (2 * reach + 1) * tile
wide = span + tile
chunk = 512
side = 256
block = 64
strip = 128
repeat = 4
TN = (((0,), (0,)), ((), ()))
NT = (((1,), (1,)), ((), ()))
NN = (((1,), (0,)), ((), ()))
vmem_limit = 60 * 1024 * 1024
light = pl.CostEstimate(flops=1_000_000, bytes_accessed=1_000_000, transcendentals=0)


def dot(left, right, dims=NN):
    return lax.dot_general(left, right, dims, preferred_element_type=f32)


def bucket_of(offset):
    distance = np.abs(offset)
    limits = 8.0 * 2.0 ** (np.arange(1, 8) / 2.0)
    counted = (distance[..., None] >= limits).sum(axis=-1)
    bucket = np.where(distance < 8, distance, 8 + counted)
    return (np.minimum(bucket, 15) + 16 * (offset < 0)).astype(np.int32)


def band_buckets():
    place = np.arange(wide)
    return bucket_of(np.where(place < span, place, place - wide) - reach * tile)


def key_tiles(b, tiles):
    return list(range(max(0, b - reach), min(tiles - 1, b + reach) + 1))


def whole(value):
    return pl.BlockSpec(value.shape, lambda *_: (0,) * len(value.shape))


def once(value):
    return pl.BlockSpec(value.shape, lambda *_: (0,) * len(value.shape), pipeline_mode=pl.Buffered(1))


def params():
    return pltpu.CompilerParams(vmem_limit_bytes=vmem_limit)


table_at = 8


def bundle_kernel(bq_ref, bv_ref, bu_ref, table_ref, out_ref):
    model = out_ref.shape[1]
    out_ref[...] = jnp.zeros_like(out_ref)
    out_ref[0:1, :] = jnp.concatenate([bq_ref[...].reshape(1, -1), bv_ref[...].reshape(1, -1)], axis=1)
    up = bu_ref[...].reshape(1, -1)
    for n in range(up.shape[1] // model):
        out_ref[1 + n : 2 + n, :] = up[:, n * model : (n + 1) * model]
    out_ref[table_at : table_at + table_ref.shape[0], : table_ref.shape[1]] = table_ref[...]


def bundle(bq, bv, bu, table):
    out_shape = jax.ShapeDtypeStruct((2 * table_at, 2 * bq.shape[0]), f32)
    return pl.pallas_call(bundle_kernel, out_shape=out_shape, compiler_params=params(), name="bundle")(bq, bv, bu, table)


def attend_kernel(
    part, content_ref, query_ref, seg_ref, order_ref, flag_ref, hot_ref, bundle_ref, wq_ref, wk_ref, wv_ref,
    q_ref, k_ref, v_ref, o_ref, ot_ref, e_ref, linv_ref, *rest,
):
    mask_ref, bias_ref, band_ref, score_ref = rest[-4:]
    ahead = score_ref.shape[0]
    row_len = k_ref.shape[0]
    tiles = row_len // tile
    p = pl.program_id(0)

    @pl.when(p == 0)
    def _():
        row = pl.ds(part[0], 1)
        seg = seg_ref[row, :].astype(f32)
        order = order_ref[row, :].astype(f32)
        flag = flag_ref[row, :]
        at = lax.broadcasted_iota(jnp.int32, (1, row_len), 1)
        first = (seg != pltpu.roll(seg, 1, 1)) | (at == 0)
        key_content = jnp.where(flag == 0, -1.0, order)
        key_query = jnp.where(first, -1.0, key_content)

        def as_column(row):
            return jnp.transpose(jnp.broadcast_to(row, (tile, row_len)))

        seg_col, content_col, query_col = as_column(seg), as_column(key_content), as_column(key_query)
        for b in range(tiles):
            here = slice(b * tile, (b + 1) * tile)
            same = seg_col == seg[:, here]
            mask_ref[b, :, :tile] = jnp.where(same & (content_col <= order[:, here]), 0.0, big_negative)
            mask_ref[b, :, tile:] = jnp.where(same & (query_col < order[:, here]), 0.0, big_negative)
        width = bundle_ref.shape[1] // 2
        for n in range(2):
            for j in range(width // tile):
                at = n * width + j * tile
                bias_ref[8 * n + j : 8 * n + j + 1, :] = bundle_ref[0:1, at : at + tile]
        band_ref[...] = lax.dot_general(
            bundle_ref[table_at:, :tile], hot_ref[...], NT, precision=lax.Precision.HIGHEST, preferred_element_type=f32
        )
        if len(rest) == 5:
            for b in range(tiles):
                here = slice(b * tile, (b + 1) * tile)
                there = slice(row_len + b * tile, row_len + (b + 1) * tile)
                rest[0][:, here] = jnp.transpose(content_ref[here, :].astype(f32)).astype(bf16)
                rest[0][:, there] = jnp.transpose(query_ref[here, :].astype(f32)).astype(bf16)

    lane = lax.broadcasted_iota(jnp.int32, (1, tile), 1)
    half = tile // 2
    bq, bv = bias_ref[pl.ds(p, 1), :], bias_ref[pl.ds(p + 8, 1), :]
    q_ref[:row_len, :] = (dot(content_ref[...], wq_ref[...]) + bq).astype(bf16)
    q_ref[row_len:, :] = (dot(query_ref[...], wq_ref[...]) + bq).astype(bf16)
    kv = dot(content_ref[...], jnp.concatenate([wk_ref[...], wv_ref[...]], axis=1))
    k_ref[...] = kv[:, :tile].astype(bf16)
    v_ref[...] = (kv[:, tile:] + bv).astype(bf16)
    v_t = jnp.transpose(v_ref[...].astype(f32)).astype(bf16)
    keys = k_ref[...].astype(f32) * 0.125
    parts = [[None, None] for _ in range(tiles)]
    heads_in, bands = [], []
    for h in range(2):
        in_head = (lane >= h * half) & (lane < (h + 1) * half)
        heads_in.append(jnp.where(in_head, keys, 0.0).astype(bf16))
        band_row = band_ref[pl.ds(2 * p + h, 1), :]
        bands.append(pltpu.roll(jnp.broadcast_to(band_row, (tile, wide)), 0, 1, stride=1, stride_axis=0))
    turns = [(h, b) for b in range(tiles) for h in range(2)]

    def score(turn):
        h, b = turns[turn]
        q_tile = jnp.concatenate(
            [q_ref[b * tile : (b + 1) * tile, :], q_ref[row_len + b * tile : row_len + (b + 1) * tile, :]], axis=0
        )
        top = None
        for kb in key_tiles(b, tiles):
            d = b - kb + reach
            rows = slice(kb * tile, (kb + 1) * tile)
            bias = bands[h][:, d * tile : (d + 1) * tile]
            s = dot(heads_in[h][rows, :], q_tile, NT)
            s = s + jnp.concatenate([bias, bias], axis=1) + mask_ref[b, rows, :]
            score_ref[turn % ahead, rows, :] = s
            one_top = jnp.max(s, axis=0, keepdims=True)
            top = one_top if top is None else jnp.maximum(top, one_top)
        return top

    def weigh(turn, top):
        h, b = turns[turn]
        near = key_tiles(b, tiles)
        total = None
        weights = []
        for kb in near:
            rows = slice(kb * tile, (kb + 1) * tile)
            e = jnp.exp(score_ref[turn % ahead, rows, :] - top)
            one_total = jnp.sum(e, axis=0, keepdims=True)
            total = one_total if total is None else total + one_total
            e = e.astype(bf16)
            e_ref[0, h, b, rows, :] = e
            weights.append(e)
        inverse = 1.0 / total
        linv_ref[0, h * tiles + b : h * tiles + b + 1, :] = inverse
        mixed = dot(
            v_t[h * half : (h + 1) * half, near[0] * tile : (near[-1] + 1) * tile], jnp.concatenate(weights, axis=0)
        )
        parts[b][h] = mixed * inverse

    tops = [score(turn) for turn in range(ahead - 1)]
    for turn in range(len(turns)):
        if turn + ahead - 1 < len(turns):
            tops.append(score(turn + ahead - 1))
        weigh(turn, tops[turn])
    for b in range(tiles):
        both = jnp.concatenate(parts[b], axis=0)
        both_t = jnp.transpose(both).astype(bf16)
        both = both.astype(bf16)
        here = slice(b * tile, (b + 1) * tile)
        there = slice(row_len + b * tile, row_len + (b + 1) * tile)
        o_ref[here, :] = both_t[:tile]
        o_ref[there, :] = both_t[tile:]
        ot_ref[:, here] = both[:, :tile]
        ot_ref[:, there] = both[:, tile:]


def attend(part, content, query, rows, hot, bundled, wq, wk, wv, keep_t):
    row_len = rows[0].shape[1]
    tokens = 2 * row_len
    model, width = wq.shape
    pairs = width // tile
    tiles = row_len // tile
    own = lambda value: pl.BlockSpec((row_len, value.shape[1]), lambda p, part: (part[0], 0))
    cols = lambda n: pl.BlockSpec((n, tile), lambda p, part: (0, p))
    out = lambda *shape: jax.ShapeDtypeStruct(shape, bf16)
    out_specs = [
        cols(tokens),
        cols(row_len),
        cols(row_len),
        cols(tokens),
        pl.BlockSpec((tile, tokens), lambda p, part: (p, 0)),
        pl.BlockSpec((1, 2, tiles, row_len, 2 * tile), lambda p, part: (p, 0, 0, 0, 0)),
        pl.BlockSpec((1, 2 * tiles, 2 * tile), lambda p, part: (p, 0, 0)),
    ]
    out_shape = [
        out(tokens, width),
        out(row_len, width),
        out(row_len, width),
        out(tokens, width),
        out(width, tokens),
        out(pairs, 2, tiles, row_len, 2 * tile),
        jax.ShapeDtypeStruct((pairs, 2 * tiles, 2 * tile), f32),
    ]
    if keep_t:
        out_specs.append(pl.BlockSpec((model, tokens), lambda p, part: (0, 0)))
        out_shape.append(out(model, tokens))
    return pl.pallas_call(
        attend_kernel,
        grid_spec=pltpu.PrefetchScalarGridSpec(
            num_scalar_prefetch=1,
            grid=(pairs,),
            in_specs=[own(content), own(query)]
            + [whole(row) for row in rows]
            + [once(hot), once(bundled)]
            + [cols(model)] * 3,
            out_specs=out_specs,
            scratch_shapes=[pltpu.VMEM((tiles, row_len, 2 * tile), f32), pltpu.VMEM((16, tile), f32), pltpu.VMEM((8, wide), f32), pltpu.VMEM((4, row_len, 2 * tile), f32)],
        ),
        out_shape=out_shape,
        compiler_params=params(),
        cost_estimate=light,
        name="attend",
    )(part, content, query, *rows, hot, bundled, wq, wk, wv)


def attend_back_kernel(
    al_ref, wo_ref, ot_ref, q_ref, k_ref, v_ref, e_ref, linv_ref, xt_ref, hot_ref,
    dw_ref, small_ref, dq_ref, dk_ref, dv_ref, dk_acc, dv_acc, g_acc, dp_ref, ds_ref,
):
    ahead = dp_ref.shape[0]
    row_len = k_ref.shape[0]
    tiles = row_len // tile
    half = tile // 2
    p = pl.program_id(0)
    lane = lax.broadcasted_iota(jnp.int32, (1, tile), 1)
    k_t = jnp.transpose(k_ref[...].astype(f32)).astype(bf16)
    do_all = dot(wo_ref[...], al_ref[...], NT).astype(bf16).astype(f32)
    dk_acc[...] = jnp.zeros_like(dk_acc)
    dv_acc[...] = jnp.zeros_like(dv_acc)
    g_acc[...] = jnp.zeros_like(g_acc)
    turns = [(h, b) for b in range(tiles) for h in range(2)]
    deltas, do_heads, q_heads = {}, {}, {}

    def places(b):
        return slice(b * tile, (b + 1) * tile), slice(row_len + b * tile, row_len + (b + 1) * tile)

    def spread(turn):
        h, b = turns[turn]
        here, there = places(b)
        mine = slice(h * half, (h + 1) * half)
        inverse = linv_ref[0, h * tiles + b : h * tiles + b + 1, :]
        do_t = jnp.concatenate([do_all[mine, here], do_all[mine, there]], axis=1)
        o_t = jnp.concatenate([ot_ref[mine, here], ot_ref[mine, there]], axis=1).astype(f32)
        deltas[turn] = jnp.sum(do_t * o_t, axis=0, keepdims=True) * inverse
        scaled = do_t * inverse
        blank = jnp.zeros_like(scaled)
        do_heads[turn] = jnp.concatenate([scaled, blank] if h == 0 else [blank, scaled], axis=0).astype(bf16)
        q_tile = jnp.concatenate([q_ref[here, :], q_ref[there, :]], axis=0)
        in_head = (lane >= h * half) & (lane < (h + 1) * half)
        q_heads[turn] = jnp.where(in_head, q_tile.astype(f32), 0.0).astype(bf16)
        for kb in key_tiles(b, tiles):
            rows = slice(kb * tile, (kb + 1) * tile)
            dp_ref[turn % ahead, rows, :] = dot(v_ref[rows, :], do_heads[turn])

    def combine(turn):
        h, b = turns[turn]
        for kb in key_tiles(b, tiles):
            d = b - kb + reach
            rows = slice(kb * tile, (kb + 1) * tile)
            ds = e_ref[0, h, b, rows, :].astype(f32) * (dp_ref[turn % ahead, rows, :] - deltas[turn])
            g_acc[h, :, d * tile : (d + 1) * tile] += ds[:, :tile] + ds[:, tile:]
            ds_ref[b % 2, h, rows, :] = ds.astype(bf16)

    def gather(b):
        here, there = places(b)
        near = key_tiles(b, tiles)
        keys = slice(near[0] * tile, (near[-1] + 1) * tile)
        two = (2 * b, 2 * b + 1)
        dv_acc[keys, :] += dot(
            jnp.concatenate([e_ref[0, h, b, keys, :] for h in range(2)], axis=1),
            jnp.concatenate([do_heads[turn] for turn in two], axis=1),
            NT,
        )
        dk_acc[keys, :] += dot(
            jnp.concatenate([ds_ref[b % 2, h, keys, :] for h in range(2)], axis=1),
            jnp.concatenate([q_heads[turn] for turn in two], axis=0),
        )
        dq_t = [dot(k_t[h * half : (h + 1) * half, keys], ds_ref[b % 2, h, keys, :]) for h in range(2)]
        dq = (jnp.transpose(jnp.concatenate(dq_t, axis=0)) * 0.125).astype(bf16)
        dq_ref[here, :] = dq[:tile]
        dq_ref[there, :] = dq[tile:]

    for turn in range(ahead - 1):
        spread(turn)
    for turn in range(len(turns)):
        if turn + ahead - 1 < len(turns):
            spread(turn + ahead - 1)
        combine(turn)
        if turn % 2 and turn >= 3:
            gather(turn // 2 - 1)
    gather(tiles - 1)
    dk = (dk_acc[...] * 0.125).astype(bf16)
    dv = dv_acc[...].astype(bf16)
    dq = dq_ref[...]
    dk_ref[...] = dk
    dv_ref[...] = dv
    dw_ref[:, :tile] = dot(xt_ref[...], dq).astype(bf16)
    dw_ref[:, tile:] = dot(xt_ref[:, :row_len], jnp.concatenate([dk, dv], axis=1)).astype(bf16)
    row = lax.broadcasted_iota(jnp.int32, (8, wide), 0)
    small_ref[0, 0:1, :] = jnp.sum(dq.astype(f32), axis=0, keepdims=True)
    small_ref[0, 1:2, :] = jnp.sum(dv.astype(f32), axis=0, keepdims=True)
    for h in range(2):
        folds = [g_acc[h, a : a + 8, :] for a in range(0, tile, 8)]
        step = 8
        while len(folds) > 1:
            folds = [folds[a] + pltpu.roll(folds[a + 1], wide - step, 1) for a in range(0, len(folds), 2)]
            step *= 2
        fold = folds[0]
        for bit in (1, 2, 4):
            fold = jnp.where((row & bit) != 0, pltpu.roll(fold, wide - bit, 1), fold)
        by_bucket = lax.dot_general(fold, hot_ref[...], NN, precision=lax.Precision.HIGHEST, preferred_element_type=f32)
        small_ref[0, 2 + h : 3 + h, :] = jnp.sum(by_bucket, axis=0, keepdims=True)


def attend_back(from_pair, pairs, al, wo, ot, q, k, v, e, linv, xt, hot):
    tokens, model = al.shape
    width = pairs * tile
    row_len = k.shape[0]
    tiles = row_len // tile
    cols = lambda n: pl.BlockSpec((n, tile), lambda p: (0, p + from_pair))
    rows = lambda n: pl.BlockSpec((tile, n), lambda p: (p + from_pair, 0))
    cols_out = lambda n: pl.BlockSpec((n, tile), lambda p: (0, p))
    shape = jax.ShapeDtypeStruct
    return pl.pallas_call(
        attend_back_kernel,
        grid=(pairs,),
        in_specs=[
            once(al),
            rows(model),
            rows(tokens),
            cols(tokens),
            cols(row_len),
            cols(row_len),
            pl.BlockSpec((1, 2, tiles, row_len, 2 * tile), lambda p: (p + from_pair, 0, 0, 0, 0)),
            pl.BlockSpec((1, 2 * tiles, 2 * tile), lambda p: (p + from_pair, 0, 0)),
            once(xt),
            once(hot),
        ],
        out_specs=[pl.BlockSpec((model, 3 * tile), lambda p: (0, p))]
        + [pl.BlockSpec((1, 8, tile), lambda p: (p, 0, 0)), cols_out(tokens), cols_out(row_len), cols_out(row_len)],
        out_shape=[shape((model, 3 * width), bf16)]
        + [shape((pairs, 8, tile), f32), shape((tokens, width), bf16)]
        + [shape((row_len, width), bf16)] * 2,
        scratch_shapes=[
            pltpu.VMEM((row_len, tile), f32),
            pltpu.VMEM((row_len, tile), f32),
            pltpu.VMEM((2, tile, wide), f32),
            pltpu.VMEM((3, row_len, 2 * tile), f32),
            pltpu.VMEM((2, 2, row_len, 2 * tile), bf16),
        ],
        compiler_params=params(),
        cost_estimate=light,
        name="attend_back",
    )(al, wo, ot, q, k, v, e, linv, xt, hot)


def inputs_back_kernel(residual_ref, *refs):
    content_ref, query_ref = refs[-2:]
    row_len = content_ref.shape[0]
    content = residual_ref[:row_len, :]
    query = residual_ref[row_len:, :]
    for at in range(0, len(refs) - 2, 6):
        dq_ref, dk_ref, dv_ref, wq_ref, wk_ref, wv_ref = refs[at : at + 6]
        wq = wq_ref[...]
        content = content + dot(dq_ref[:row_len, :], wq, NT) + dot(dk_ref[...], wk_ref[...], NT) + dot(dv_ref[...], wv_ref[...], NT)
        query = query + dot(dq_ref[row_len:, :], wq, NT)
    content_ref[...] = content
    query_ref[...] = query


def inputs_back(residual, groups):
    tokens, model = residual.shape
    shape = jax.ShapeDtypeStruct((tokens // 2, model), f32)
    args = [residual]
    specs = [once(residual)]
    for grads, weights, at, width in groups:
        args += list(grads) + list(weights)
        specs += [once(one) for one in grads]
        specs += [pl.BlockSpec((model, width), lambda i, at=at: (0, at), pipeline_mode=pl.Buffered(1)) for _ in weights]
    return pl.pallas_call(
        inputs_back_kernel,
        grid=(1,),
        in_specs=specs,
        out_specs=[once(shape)] * 2,
        out_shape=[shape] * 2,
        compiler_params=params(),
        cost_estimate=light,
        name="inputs_back",
    )(*args)


def normed_of(values):
    centre = jnp.mean(values, axis=-1, keepdims=True)
    centred = values - centre
    variance = jnp.mean(centred * centred, axis=-1, keepdims=True)
    inv_scale = lax.rsqrt(variance + norm_eps)
    return centred * inv_scale, inv_scale


def norm_back(upstream, normed, inv_scale, gain_vec):
    scaled = upstream * gain_vec
    centre = jnp.mean(scaled, axis=-1, keepdims=True)
    along_normed = jnp.mean(scaled * normed, axis=-1, keepdims=True)
    return inv_scale * (scaled - centre - normed * along_normed)


def eight(values):
    total = values[0:8]
    for i in range(8, values.shape[0], 8):
        total = total + values[i : i + 8]
    return total


def gelu_parts(u):
    bell = jnp.exp(-0.5 * (u * u))
    t = 1.0 / (1.0 + (0.3275911 * root_half) * jnp.abs(u))
    poly = 0.5307027145
    poly = poly * t - 0.7265760135
    poly = poly * t + 0.7107068705
    poly = poly * t - 0.142248368
    poly = poly * t + 0.127414796
    tail = poly * t * bell
    cdf = jnp.where(u >= 0.0, 1.0 - tail, tail)
    return u * cdf, cdf + (u * root_two_pi_inv) * bell


def feed_kernel(
    part, o0_ref, o1_ref, wo0_ref, wo1_ref, content_ref, query_ref, bo_ref, g1_ref, s1_ref, wu0_ref, wu1_ref, bu0_ref, bu1_ref,
    wd0_ref, wd1_ref, bd_ref, g2_ref, s2_ref, cu_ref, qu_ref,
    normed_out, first_out, second_out, inv_ref, fc_ref, fq_ref, sums_ref, dwd0_ref, dwd1_ref, low0_ref, low1_ref, dbu0_ref, dbu1_ref,
    normed_ref, first_ref, acc_ref, d2_ref, hidden_ref, slope_ref, bu_ref, up_ref, sems,
):
    row_len = content_ref.shape[0]
    bo, g1, s1, bd, g2, s2 = (ref[...].reshape(1, -1) for ref in (bo_ref, g1_ref, s1_ref, bd_ref, g2_ref, s2_ref))
    tokens, model = acc_ref.shape
    steps = pl.num_programs(0)
    i = pl.program_id(0)
    steps_of_half = hidden_ref.shape[0] // 2
    copies = [
        pltpu.make_async_copy(normed_ref, normed_out, sems.at[0]),
        pltpu.make_async_copy(first_ref, first_out, sems.at[1]),
        pltpu.make_async_copy(acc_ref, second_out, sems.at[2]),
    ]

    @pl.when(i == 0)
    def _():
        acc_ref[...] = dot(o0_ref[...], wo0_ref[...]) + dot(o1_ref[...], wo1_ref[...])
        for n, one_ref in enumerate((bu0_ref, bu1_ref)):
            flat = jnp.concatenate([one_ref[1 + j : 2 + j, :] for j in range(steps_of_half * chunk // model)], axis=1)
            for j in range(flat.shape[1] // chunk):
                at = n * (flat.shape[1] // chunk) + j
                bu_ref[at : at + 1, :] = flat[:, j * chunk : (j + 1) * chunk]
        for s, x_ref in enumerate((content_ref, query_ref)):

            def step(r, _, s=s, x_ref=x_ref):
                from_rows = pl.ds(pl.multiple_of(r * strip, strip), strip)
                rows = pl.ds(pl.multiple_of(s * row_len + r * strip, strip), strip)
                normed, inv = normed_of(x_ref[from_rows, :].astype(f32) + acc_ref[rows, :] + bo)
                first = normed * g1 + s1
                normed_ref[rows, :] = normed
                inv_ref[rows, :] = inv
                first_ref[rows, :] = first.astype(bf16)
                acc_ref[rows, :] = first + bd
                return 0

            lax.fori_loop(0, row_len // strip, step, 0, unroll=repeat)
        copies[1].start()

    def forward(wu_ref, wd_ref):
        bias = bu_ref[pl.ds(i, 1), :]
        splits = [slice(j, j + side) for j in range(0, chunk, side)]
        for j, cols in enumerate(splits):
            up_ref[:, cols] = dot(first_ref[...], wu_ref[:, cols]) + bias[:, cols]
        for cols in splits:
            for r in range(0, tokens, block):
                rows = slice(r, r + block)
                hidden, slope = gelu_parts(up_ref[rows, cols])
                hidden_ref[i, rows, cols] = hidden.astype(bf16)
                slope_ref[i, rows, cols] = slope.astype(bf16)
        acc_ref[...] += dot(hidden_ref[i], wd_ref[...])

    @pl.when(i < steps // 4)
    def _():
        forward(wu0_ref, wd0_ref)

    @pl.when((i >= steps // 4) & (i < steps // 2))
    def _():
        forward(wu1_ref, wd1_ref)

    @pl.when(i == steps // 2 - 1)
    def _():
        sums = (jnp.zeros((8, model), f32),) * 3
        for s, (c_ref, out_ref) in enumerate(((cu_ref, fc_ref), (qu_ref, fq_ref))):

            def step(r, sums, s=s, c_ref=c_ref, out_ref=out_ref):
                from_rows = pl.ds(pl.multiple_of(r * strip, strip), strip)
                rows = pl.ds(pl.multiple_of(s * row_len + r * strip, strip), strip)
                normed, inv = normed_of(acc_ref[rows, :])
                out_ref[from_rows, :] = (normed * g2 + s2).astype(bf16)
                c = c_ref[from_rows, :].astype(f32)
                second = norm_back(c, normed, inv, g2)
                acc_ref[rows, :] = second
                d2_ref[rows, :] = second.astype(bf16)
                return (sums[0] + eight(c * normed), sums[1] + eight(c), sums[2] + eight(second))

            sums = lax.fori_loop(0, row_len // strip, step, sums, unroll=repeat)
        for n in range(3):
            sums_ref[n : n + 1, :] = jnp.sum(sums[n], axis=0, keepdims=True)
        copies[2].start()

    def backward(wd_ref, dwd_ref, low_ref, dbu_ref):
        at = i - steps // 2
        up_ref[...] = dot(d2_ref[...], wd_ref[...], NT)
        dwd_ref[...] = dot(d2_ref[...], hidden_ref[at], TN).astype(bf16)
        total = jnp.zeros((8, chunk), f32)
        for r in range(0, tokens, block):
            rows = slice(r, r + block)
            grad = (up_ref[rows, :] * slope_ref[at, rows, :].astype(f32)).astype(bf16)
            low_ref[rows, :] = grad
            total = total + eight(grad.astype(f32))
        dbu_ref[...] = jnp.sum(total, axis=0, keepdims=True)

    @pl.when((i >= steps // 2) & (i < steps * 3 // 4))
    def _():
        backward(wd0_ref, dwd0_ref, low0_ref, dbu0_ref)

    @pl.when(i >= steps * 3 // 4)
    def _():
        backward(wd1_ref, dwd1_ref, low1_ref, dbu1_ref)

    @pl.when(i == 1)
    def _():
        copies[0].start()

    @pl.when(i == steps - 1)
    def _():
        for copy in copies:
            copy.wait()


def feed(part, o, wo, content, query, bo, g1, s1, wu, bu, wd, bd, g2, s2, cu, qu):
    tokens = o[0].shape[0]
    row_len = cu.shape[0]
    model, width = wu[0].shape
    c = width // chunk
    own = pl.BlockSpec((row_len, model), lambda i, part: (part[0], 0), pipeline_mode=pl.Buffered(1))
    up0 = lambda i: jnp.minimum(i, c - 1)
    up1 = lambda i: jnp.clip(i - c, 0, c - 1)
    down0 = lambda i: jnp.where(i < 2 * c, jnp.minimum(i, c - 1), jnp.minimum(i - 2 * c, c - 1))
    down1 = lambda i: jnp.where(i < 3 * c, jnp.clip(i - c, 0, c - 1), i - 3 * c)
    back0 = lambda i: jnp.clip(i - 2 * c, 0, c - 1)
    back1 = lambda i: jnp.clip(i - 3 * c, 0, c - 1)
    cols = lambda n, at: pl.BlockSpec((n, chunk), lambda i, part: (0, at(i)))
    rows = lambda at: pl.BlockSpec((chunk, model), lambda i, part: (at(i), 0))
    anywhere = pl.BlockSpec(memory_space=pl.ANY)
    shape = jax.ShapeDtypeStruct
    out_shape = [
        shape((tokens, model), f32),
        shape((tokens, model), bf16),
        shape((tokens, model), f32),
        shape((tokens, 1), f32),
        shape((row_len, model), bf16),
        shape((row_len, model), bf16),
        shape((8, model), f32),
    ]
    out_shape += [shape((model, width), bf16)] * 2 + [shape((tokens, width), bf16)] * 2 + [shape((1, width), f32)] * 2
    out_specs = [anywhere] * 3 + [once(one) for one in out_shape[3:7]]
    for n in (model, tokens, 1):
        out_specs += [cols(n, back0), cols(n, back1)]
    return pl.pallas_call(
        feed_kernel,
        grid_spec=pltpu.PrefetchScalarGridSpec(
            num_scalar_prefetch=1,
            grid=(4 * c,),
            in_specs=[once(o[0]), once(o[1]), once(wo[0]), once(wo[1]), own, own, once(bo), once(g1), once(s1)]
            + [cols(model, up0), cols(model, up1), once(bu[0]), once(bu[1]), rows(down0), rows(down1)]
            + [once(bd), once(g2), once(s2), once(cu), once(qu)],
            out_specs=out_specs,
            scratch_shapes=[
                pltpu.VMEM((tokens, model), f32),
                pltpu.VMEM((tokens, model), bf16),
                pltpu.VMEM((tokens, model), f32),
                pltpu.VMEM((tokens, model), bf16),
                pltpu.VMEM((2 * c, tokens, chunk), bf16),
                pltpu.VMEM((2 * c, tokens, chunk), bf16),
                pltpu.VMEM((8, chunk), f32),
                pltpu.VMEM((tokens, chunk), f32),
                pltpu.SemaphoreType.DMA((3,)),
            ],
        ),
        out_shape=out_shape,
        compiler_params=params(),
        cost_estimate=light,
        name="feed",
    )(part, o[0], o[1], wo[0], wo[1], content, query, bo, g1, s1, wu[0], wu[1], bu[0], bu[1], wd[0], wd[1], bd, g2, s2, cu, qu)


def up_back_kernel(
    first_ref, low0_ref, low1_ref, wu0_ref, wu1_ref, g1_ref, inv_ref, normed_in, second_in, o0_in, o1_in,
    dwu0_ref, dwu1_ref, residual_ref, al_ref, sums_ref, dwo0_ref, dwo1_ref,
    acc_ref, normed_ref, second_ref, o0_ref, o1_ref, sems,
):
    tokens, model = acc_ref.shape
    i = pl.program_id(0)
    steps = pl.num_programs(0)
    pairs = ((normed_in, normed_ref), (second_in, second_ref), (o0_in, o0_ref), (o1_in, o1_ref))
    copies = [pltpu.make_async_copy(here, there, sems.at[n]) for n, (here, there) in enumerate(pairs)]

    @pl.when(i == 0)
    def _():
        for copy in copies:
            copy.start()
        acc_ref[...] = jnp.zeros_like(acc_ref)

    def units(low_ref, wu_ref, dwu_ref):
        dwu_ref[...] = dot(first_ref[...], low_ref[...], TN).astype(bf16)
        acc_ref[...] += dot(low_ref[...], wu_ref[...], NT)

    @pl.when(i < steps // 2)
    def _():
        units(low0_ref, wu0_ref, dwu0_ref)

    @pl.when(i >= steps // 2)
    def _():
        units(low1_ref, wu1_ref, dwu1_ref)

    @pl.when(i == steps - 1)
    def _():
        for copy in copies:
            copy.wait()
        g1 = g1_ref[...].reshape(1, -1)

        def step(r, sums):
            rows = pl.ds(pl.multiple_of(r * strip, strip), strip)
            back, normed = acc_ref[rows, :] + second_ref[rows, :], normed_ref[rows, :]
            residual = norm_back(back, normed, inv_ref[rows, :], g1)
            residual_ref[rows, :] = residual
            al_ref[rows, :] = residual.astype(bf16)
            return (sums[0] + eight(back * normed), sums[1] + eight(back), sums[2] + eight(residual))

        sums = lax.fori_loop(0, tokens // strip, step, (jnp.zeros((8, model), f32),) * 3, unroll=repeat)
        for n in range(3):
            sums_ref[n : n + 1, :] = jnp.sum(sums[n], axis=0, keepdims=True)
        dwo0_ref[...] = dot(al_ref[...], o0_ref[...], TN).astype(bf16)
        dwo1_ref[...] = dot(al_ref[...], o1_ref[...], TN).astype(bf16)


def up_back(first, low, wu, g1, inv, normed, second, o):
    tokens, width = low[0].shape
    model = first.shape[1]
    c = width // chunk
    at0 = lambda i: jnp.minimum(i, c - 1)
    at1 = lambda i: jnp.maximum(i - c, 0)
    cols = lambda n, at: pl.BlockSpec((n, chunk), lambda i: (0, at(i)))
    anywhere = pl.BlockSpec(memory_space=pl.ANY)
    shape = jax.ShapeDtypeStruct
    out_shape = [
        shape((model, width), bf16),
        shape((model, width), bf16),
        shape((tokens, model), f32),
        shape((tokens, model), bf16),
        shape((8, model), f32),
        shape((model, o[0].shape[1]), bf16),
        shape((model, o[1].shape[1]), bf16),
    ]
    return pl.pallas_call(
        up_back_kernel,
        grid=(2 * c,),
        in_specs=[once(first), cols(tokens, at0), cols(tokens, at1), cols(model, at0), cols(model, at1), once(g1), once(inv)]
        + [anywhere] * 4,
        out_specs=[cols(model, at0), cols(model, at1)] + [once(one) for one in out_shape[2:]],
        out_shape=out_shape,
        scratch_shapes=[
            pltpu.VMEM((tokens, model), f32),
            pltpu.VMEM((tokens, model), f32),
            pltpu.VMEM((tokens, model), f32),
            pltpu.VMEM(o[0].shape, bf16),
            pltpu.VMEM(o[1].shape, bf16),
            pltpu.SemaphoreType.DMA((4,)),
        ],
        compiler_params=params(),
        cost_estimate=light,
        name="up_back",
    )(first, low[0], low[1], wu[0], wu[1], g1, inv, normed, second, o[0], o[1])


def pack_kernel(part, one_ref, two_ref, dbu0_ref, dbu1_ref, *rest):
    smalls, out_ref = rest[:-1], rest[-1]
    first = part[0] == 0
    model = one_ref.shape[1]
    out_ref[...] = jnp.zeros_like(out_ref)
    out_ref[0:3, :] = one_ref[0:3, :]
    out_ref[3:6, :] = two_ref[0:3, :]
    pairs = model // tile // 2
    own = jnp.concatenate([ref[...] for ref in smalls[:-1]], axis=0)
    other = smalls[-1][...]
    for row in range(2):
        halves = [jnp.concatenate([half[n, row : row + 1, :] for n in range(pairs)], axis=1) for half in (own, other)]
        out_ref[6 + row : 7 + row, : model // 2] = jnp.where(first, halves[0], halves[1])
        out_ref[6 + row : 7 + row, model // 2 :] = jnp.where(first, halves[1], halves[0])
    tables = [
        jnp.concatenate([half[n, 2 + h : 3 + h, :] for n in range(pairs) for h in range(2)], axis=1) for half in (own, other)
    ]
    ups = [dbu0_ref[...], dbu1_ref[...]]
    for row, (a, b) in enumerate(((0, 1), (1, 0))):
        out_ref[8 + row : 9 + row, :] = jnp.where(first, tables[a], tables[b])
        up = jnp.where(first, ups[a], ups[b])
        rows = up.shape[1] // model
        for n in range(rows):
            at = 10 + row * rows + n
            out_ref[at : at + 1, :] = up[:, n * model : (n + 1) * model]


def pack(part, one, two, dbu0, dbu1, smalls):
    args = (one, two, dbu0, dbu1) + tuple(smalls)
    model = one.shape[1]
    return pl.pallas_call(
        pack_kernel,
        grid_spec=pltpu.PrefetchScalarGridSpec(
            num_scalar_prefetch=1, grid=(1,), in_specs=[whole(arg) for arg in args], out_specs=pl.BlockSpec((16, model), lambda *_: (0, 0))
        ),
        out_shape=jax.ShapeDtypeStruct((16, model), f32),
        compiler_params=params(),
        name="pack",
    )(part, *args)


def exchange(value, axis_name, bit):
    count = lax.axis_size(axis_name)
    return lax.ppermute(value, axis_name, [(i, i ^ bit) for i in range(count)])


class Term:
    def __init__(self, pieces, left):
        self.pieces, self.left = pieces, left

    def places(self, flips, free):
        weight = {one: 1 << (len(self.left) - 1 - n) for n, one in enumerate(self.left)}
        own = {one: -w if one in flips else w for one, w in weight.items() if one not in free}
        start = sum(weight[one] for one in flips)
        for n in range(1 << len(free)):
            yield start + sum(weight[one] for m, one in enumerate(free) if n >> (len(free) - 1 - m) & 1), own


class Chain:
    def __init__(self, parts, order):
        bits = sum(len(step) for step in order)
        self.block = parts[0][0][0].shape[0] >> bits
        self.left = tuple(range(bits - 1, -1, -1))
        self.order = list(order)
        self.parts = [[Term([(array, 0, low, high - low)], self.left) for array, low, high in terms] for terms in parts]

    def step(self):
        bits = self.order.pop(0)
        self.left = tuple(one for one in self.left if one not in bits)
        return bits


def departures(chains, small=False):
    (bits,) = {chain.step() for chain in chains}
    before = [list(terms) for chain in chains for terms in chain.parts]
    masks = range(1, 1 << len(bits))
    return [Parcel(chains, before, [one for n, one in enumerate(bits) if mask >> n & 1], small) for mask in masks]


class Parcel:
    def __init__(self, chains, before, flips, small):
        self.chains, self.flips, self.small = chains, flips, small
        self.block = chains[0].block
        self.parts = list(zip(before, [chain.left for chain in chains for _ in chain.parts]))
        widths = [sum(piece[3] for piece in terms[0].pieces) for terms, _ in self.parts]
        self.width = min(widths)
        self.spots, self.rows = [], 0
        for (_, left), n in zip(self.parts, widths):
            spots = []
            for at in range(0, n, self.width):
                spots.append((self.rows, at))
                self.rows += self.block << len(left)
            self.spots.append(spots)

    def go(self, sent):
        self.coming = exchange(sent, "dp", sum(1 << one for one in self.flips))

    def land(self, coming):
        spots = iter(self.spots)
        for chain in self.chains:
            for terms in chain.parts:
                terms.append(Term([(coming, row, 0, self.width) for row, _ in next(spots)], chain.left))
        return (coming, self.rows) if self.small else None


def read_plain(terms, flips, free, block):
    index = lax.axis_index("dp")
    total = 0.0
    for term in terms:
        rows = block << len(term.left)
        value = jnp.concatenate([array[row : row + rows, col : col + n] for array, row, col, n in term.pieces], axis=1)
        value = value.reshape((2,) * len(term.left) + (block, value.shape[1]))
        for axis, one in reversed(list(enumerate(term.left))):
            if one not in free:
                mine = (index >> one) & 1
                value = lax.dynamic_index_in_dim(value, 1 - mine if one in flips else mine, axis, keepdims=False)
        total = total + value.reshape(block << len(free), value.shape[-1]).astype(f32)
    return total


class Reader:
    def __init__(self, block):
        self.block, self.arrays, self.copies, self.counts = block, [], [], {}

    def read(self, terms, flips, free):
        blocks = [[] for _ in range(1 << len(free))]
        for term in terms:
            for n, (at, own) in enumerate(term.places(flips, free)):
                slots = []
                for array, row, col, width in term.pieces:
                    known = [m for m, one in enumerate(self.arrays) if one is array]
                    if not known:
                        known = [len(self.arrays)]
                        self.arrays.append(array)
                    slot = self.counts.get((width, array.dtype), 0)
                    self.counts[(width, array.dtype)] = slot + 1
                    self.copies.append((known[0], row + at * self.block, own, col, width, array.dtype, slot))
                    slots.append((width, array.dtype, slot))
                blocks[n].append(slots)
        return blocks

    def scratch(self):
        kinds = list(self.counts)
        return [pltpu.VMEM((self.counts[kind], self.block, kind[0]), kind[1]) for kind in kinds] + [
            pltpu.SemaphoreType.DMA((len(self.copies),))
        ]

    def start(self, index, array_refs, scratch):
        buffers = dict(zip(self.counts, scratch))
        made = []
        for n, (array, row, own, col, width, dtype, slot) in enumerate(self.copies):
            at = row + self.block * sum(((index >> one) & 1) * w for one, w in own.items())
            rows = pl.ds(pl.multiple_of(at, 16), self.block)
            copy = pltpu.make_async_copy(array_refs[array].at[rows, col : col + width], buffers[(width, dtype)].at[slot], scratch[-1].at[n])
            copy.start()
            made.append(copy)
        return buffers, made

    @staticmethod
    def add(buffers, terms):
        total = None
        for slots in terms:
            value = [buffers[(width, dtype)][slot].astype(f32) for width, dtype, slot in slots]
            value = value[0] if len(value) == 1 else jnp.concatenate(value, axis=1)
            total = value if total is None else total + value
        return total


def halves_of(got, rows):
    return [(coming[at : at + rows], coming[at + rows : at + 2 * rows]) for coming, at in got]


def join_small(packed, got):
    wide = [jnp.concatenate(one, axis=1).astype(f32) for one in got]
    if len(wide) == 3:
        return (packed + wide[0]) + (wide[1] + wide[2])
    return packed + wide[0] if wide else packed


def post(index, parcels, packed=None, got=()):
    block = parcels[0].block
    smalls = [parcel for parcel in parcels if parcel.small]
    if block % 16:
        sents = []
        if smalls:
            packed = lax.reduce_precision(join_small(packed, halves_of(got, packed.shape[0])), 8, 7)
        for parcel in parcels:
            values = []
            for (terms, left), spots in zip(parcel.parts, parcel.spots):
                value = read_plain(terms, parcel.flips, left, block).astype(bf16)
                values += [value[:, at : at + parcel.width] for _, at in spots]
            if parcel.small:
                half = packed.shape[1] // 2
                values += [packed[:, :half].astype(bf16), packed[:, half:].astype(bf16)]
            sents.append(jnp.concatenate(values, axis=0))
        return sents + ([packed] if smalls else [])
    reader = Reader(block)
    plans = [[reader.read(terms, parcel.flips, left) for terms, left in parcel.parts] for parcel in parcels]
    shapes = [jax.ShapeDtypeStruct((parcel.rows + (2 * packed.shape[0] if parcel.small else 0), parcel.width), bf16) for parcel in parcels]
    extra, extra_specs = [], []
    if smalls:
        extra = [packed] + [coming for coming, _ in got for _ in range(2)]
        shapes.append(jax.ShapeDtypeStruct(packed.shape, f32))
        extra_specs = [once(packed)] + [
            pl.BlockSpec((packed.shape[0], coming.shape[1]), lambda *_, n=at // packed.shape[0] + half: (n, 0))
            for coming, at in got
            for half in range(2)
        ]

    def kernel(index_ref, *refs):
        array_refs = refs[: len(reader.arrays)]
        extra_refs = refs[len(reader.arrays) : len(reader.arrays) + len(extra)]
        outs = refs[len(reader.arrays) + len(extra) :][: len(shapes)]
        buffers, made = reader.start(index_ref[0], array_refs, refs[len(reader.arrays) + len(extra) + len(shapes) :])
        if smalls:
            value = join_small(
                extra_refs[0][...], [(extra_refs[n][...], extra_refs[n + 1][...]) for n in range(1, len(extra), 2)]
            ).astype(bf16)
            outs[-1][...] = value.astype(f32)
            for parcel, out in zip(parcels, outs):
                if parcel.small:
                    half, rows = value.shape[1] // 2, value.shape[0]
                    at = parcel.rows
                    out[at : at + rows, :] = value[:, :half]
                    out[at + rows : at + 2 * rows, :] = value[:, half:]
        for copy in made:
            copy.wait()
        for parcel, plan, out in zip(parcels, plans, outs):
            for spots, blocks in zip(parcel.spots, plan):
                for n, terms in enumerate(blocks):
                    value = reader.add(buffers, terms).astype(bf16)
                    for row, at in spots:
                        out[row + n * block : row + (n + 1) * block, :] = value[:, at : at + parcel.width]

    return pl.pallas_call(
        kernel,
        grid_spec=pltpu.PrefetchScalarGridSpec(
            num_scalar_prefetch=1,
            grid=(1,),
            in_specs=[pl.BlockSpec(memory_space=pltpu.HBM)] * len(reader.arrays) + extra_specs,
            out_specs=[once(one) for one in shapes],
            scratch_shapes=reader.scratch(),
        ),
        out_shape=shapes,
        compiler_params=params(),
        cost_estimate=light,
        name="post",
    )(index, *reader.arrays, *extra)


def total_of(index, name, parts, block, extra, shapes, write):
    plain = block % 16
    reader = Reader(block)
    plans = [] if plain else [reader.read(terms, (), ())[0] for terms in parts]
    arrays = [read_plain(terms, (), (), block) for terms in parts] if plain else reader.arrays

    def kernel(index_ref, *refs):
        array_refs, extra_refs = refs[: len(arrays)], refs[len(arrays) :][: len(extra)]
        outs, scratch = refs[len(arrays) + len(extra) :][: len(shapes)], refs[len(arrays) + len(extra) + len(shapes) :]
        if plain:
            sums = [ref[...] for ref in array_refs]
        else:
            buffers, made = reader.start(index_ref[0], array_refs, scratch)
            for copy in made:
                copy.wait()
            sums = [reader.add(buffers, plan) for plan in plans]
        write(sums, extra_refs, outs)

    return pl.pallas_call(
        kernel,
        grid_spec=pltpu.PrefetchScalarGridSpec(
            num_scalar_prefetch=1,
            grid=(1,),
            in_specs=[once(one) if plain else pl.BlockSpec(memory_space=pltpu.HBM) for one in arrays] + [once(one) for one in extra],
            out_specs=[once(one) for one in shapes],
            scratch_shapes=[] if plain else reader.scratch(),
        ),
        out_shape=shapes,
        compiler_params=params(),
        cost_estimate=light,
        name=name,
    )(index, *arrays, *extra)


def finish_wide(index, groups, block):
    shapes = [jax.ShapeDtypeStruct((block, sum(sum(piece[3] for piece in terms[0].pieces) for terms in group)), f32) for group in groups]

    def write(sums, _, outs):
        for group, out in zip(groups, outs):
            out[...] = jnp.concatenate(sums[: len(group)], axis=1)
            sums = sums[len(group) :]

    return total_of(index, "finish_wide", [terms for group in groups for terms in group], block, [], shapes, write)


def finish(index, packed, far, parts, block, units, buckets, heads):
    model = packed.shape[1]
    f32_of = lambda *shape: jax.ShapeDtypeStruct(shape, f32)
    shapes = [f32_of(model)] * 8 + [f32_of(units), f32_of(heads, buckets)] + [f32_of(block, len(parts) * tile)] * 3

    def write(sums, extra_refs, outs):
        rows = extra_refs[0][...] + extra_refs[1][...]
        for n in range(8):
            outs[n][...] = rows[n : n + 1, :].reshape(model)
        up = jnp.concatenate([rows[n : n + 1, :] for n in range(10, 10 + units // model)], axis=1)
        outs[8][...] = up.reshape(units)
        heads_of = [rows[8 + half : 9 + half, n * tile : (n + 1) * tile] for half in range(2) for n in range(model // tile)]
        outs[9][...] = jnp.concatenate(heads_of, axis=0)[:heads, :buckets]
        for n in range(3):
            for pair, value in enumerate(sums):
                outs[10 + n][:, pair * tile : (pair + 1) * tile] = value[:, n * tile : (n + 1) * tile]

    return total_of(index, "finish", parts, block, [packed, far], shapes, write)


def wide_groups(x, y, z):
    return [[z.parts[2]], [y.parts[0], z.parts[1]], [x.parts[0], z.parts[0]]]


def gate(*values):
    return lax.optimization_barrier(values)


def local(
    content_input,
    query_input,
    segment_ids,
    orders,
    predicted,
    query_weight,
    query_bias,
    key_weight,
    value_weight,
    value_bias,
    out_weight,
    out_bias,
    first_gain,
    first_shift,
    up_weight,
    up_bias,
    down_weight,
    down_bias,
    second_gain,
    second_shift,
    bias_table,
    content_upstream,
    query_upstream,
):
    tensor_index = lax.axis_index("tensor")
    bits = lax.axis_size("dp").bit_length() - 1
    part = tensor_index.astype(jnp.int32).reshape(1)
    far_of = lambda value: exchange(value, "tensor", 1)

    def order(*first):
        named = [bit for step in first for bit in step]
        return list(first) + [(bit,) for bit in range(bits) if bit not in named]

    own_bundle = bundle(query_bias, value_bias, up_bias, bias_table.T)
    own_attention = (own_bundle, query_weight, key_weight, value_weight)
    far_attention = tuple(far_of(value) for value in own_attention)
    rows = (segment_ids, orders, predicted)
    heads = bias_table.shape[1]
    buckets = band_buckets()
    hot = jnp.asarray((buckets[:, None] == np.arange(tile)[None, :]).astype(np.float32))

    def attention(values, keep_t):
        return attend(part, content_input, query_input, rows, hot, *values, keep_t)

    own = attention(own_attention, True)
    streams_t = own[7]
    sent = gate(*far_attention, out_weight, up_weight, down_weight)
    far_attention = sent[:4]
    out_far, up_far, down_far = (far_of(value) for value in sent[4:])
    saved = [own[:7], attention(far_attention, False)]
    out_w, up_w, down_w = (out_weight, out_far), (up_weight, up_far), (down_weight, down_far)
    bundles = (own_bundle, far_attention[0])
    attention_w = [own_attention[1:], far_attention[1:]]
    o = (saved[0][3], saved[1][3])
    normed, first, second, inv, final_c, final_q, sums_two, dwd0, dwd1, low0, low1, dbu0, dbu1 = feed(
        part, o, out_w, content_input, query_input, out_bias, first_gain, first_shift, up_w, bundles, down_w,
        down_bias, second_gain, second_shift, content_upstream, query_upstream,
    )
    far_d = far_of(dwd1)
    dwu0, dwu1, residual, al, sums_one, dwo0, dwo1 = up_back(first, (low0, low1), up_w, first_gain, inv, normed, second, o)
    far_u, far_o = far_of(dwu1), far_of(dwo1)
    index = lax.axis_index("dp").astype(jnp.int32).reshape(1)
    units = dwd0.shape[1]
    cut = units * 3 // 4
    width = query_weight.shape[1]
    both = lambda own, far, low, high: [(own, low, high), (far, low, high)]

    def leave(parcels, after, packed=None, got=()):
        sents = post(index, parcels, packed, got)
        after, *sents = gate(after, *sents)
        for parcel, sent in zip(parcels, sents):
            parcel.go(sent)
        return (after, sents[-1]) if packed is not None else after

    def arrive(parcels, after):
        after, *came = gate(after, *[parcel.coming for parcel in parcels])
        return after, [parcel.land(one) for parcel, one in zip(parcels, came)]

    chain_x = Chain([both(dwd0, far_d, 0, cut)], order((0,), (1,), (2,)))
    first_x = departures([chain_x])
    far_u, far_o = leave(first_x, (far_u, far_o))
    chain_y = Chain([both(dwu0, far_u, 0, cut)], order((1,), (0,), (2,)))
    chain_z = Chain(
        [both(dwd0, far_d, cut, units), both(dwu0, far_u, cut, units), both(dwo0, far_o, 0, width)],
        order((2,), (3,), (0, 1)),
    )
    first_yz = departures([chain_y]) + departures([chain_z])
    al = leave(first_yz, al)

    def attention_back(s, from_pair, pairs, al):
        q, k, v, _, ot, e, linv = saved[s]
        return attend_back(from_pair, pairs, al, out_w[s], ot, q, k, v, e, linv, streams_t, hot)

    pairs = width // tile
    late = 1
    early = pairs - late
    split, side_width = early * tile, late * tile
    other = attention_back(1, 0, pairs, al)
    al, _ = arrive(first_x + first_yz, gate(al, other[0])[0])
    seconds = departures([chain_x]) + departures([chain_y]) + departures([chain_z])
    al = leave(seconds, al)
    dw_other, al = gate(other[0], al)
    far = far_of(dw_other)
    own_early = attention_back(0, 0, early, al)
    al, far, dw_early = gate(al, far, own_early[0])
    al, _ = arrive(seconds[:2], al)
    triple = 3 * tile
    of_pair = lambda n: (n * triple, (n + 1) * triple)
    chain_a = Chain([[(dw_early, *of_pair(n)), (far, *of_pair(n))] for n in range(early)], order((0, 1), (2, 3)))
    third_a, third_xy = departures([chain_a]), departures([chain_x, chain_y])
    al = leave(third_a + third_xy, al)
    own_late = attention_back(0, early, late, al)
    packed = pack(part, sums_one, sums_two, dbu0, dbu1, [own_early[1], own_late[1], other[1]])
    dw_late = own_late[0]
    chain_b = Chain([[(dw_late, *of_pair(n)), (far, *of_pair(early + n))] for n in range(late)], order((0, 1), (2, 3)))
    residual, _ = arrive(seconds[2:] + third_xy, residual)
    fourth = departures([chain_x, chain_y])
    parcels = departures([chain_b, chain_z], True)
    residual, packed = leave(parcels + fourth, residual, packed)
    content_grad, query_grad = inputs_back(
        residual,
        [
            (own_early[2:5], attention_w[0], 0, split),
            (own_late[2:5], attention_w[0], early // late, side_width),
            (other[2:5], attention_w[1], 0, split + side_width),
        ],
    )
    content_grad, _ = arrive(third_a, content_grad)
    content_grad, got = arrive(parcels, content_grad)
    chains = [chain_a, chain_b]
    wide_out = None
    while chain_a.order:
        parcels = departures(chains, True)
        content_grad, packed = leave(parcels, content_grad, packed, got)
        if wide_out is None:
            content_grad, _ = arrive(fourth, content_grad)
        if not chain_x.order and wide_out is None:
            wide_out = finish_wide(index, wide_groups(chain_x, chain_y, chain_z), chain_a.block)
            content_grad, *wide_out = gate(content_grad, *wide_out)
        content_grad, got = arrive(parcels, content_grad)
        chains = [chain_a, chain_b, chain_x, chain_y, chain_z]
    if wide_out is None:
        wide_out = finish_wide(index, wide_groups(chain_x, chain_y, chain_z), chain_a.block)
    packed = join_small(packed, halves_of(got, packed.shape[0]))
    parts = chain_a.parts + chain_b.parts
    out = finish(index, packed, far_of(packed), parts, chain_a.block, 2 * units, bias_table.shape[0], 2 * heads)
    return (
        final_c,
        final_q,
        content_grad,
        query_grad,
        *out[10:13],
        wide_out[0].T,
        wide_out[1],
        wide_out[2].T,
        out[6],
        out[7],
        out[2],
        out[0],
        out[1],
        out[8],
        out[5],
        out[3],
        out[4],
        out[9].T,
    )


def solution(mesh):
    placed = (
        P("dp", None),
        P("dp", None),
        P("dp", None),
        P("dp", None),
        P("dp", None),
        P(None, "tensor"),
        P("tensor"),
        P(None, "tensor"),
        P(None, "tensor"),
        P("tensor"),
        P("tensor", None),
        P(),
        P(),
        P(),
        P(None, "tensor"),
        P("tensor"),
        P("tensor", None),
        P(),
        P(),
        P(),
        P(None, "tensor"),
        P(("dp", "tensor"), None),
        P(("dp", "tensor"), None),
    )
    rows_out = P(("dp", "tensor"), None)
    return jax.shard_map(
        local,
        mesh=mesh,
        in_specs=placed,
        out_specs=(
            rows_out,
            rows_out,
            rows_out,
            rows_out,
            P("dp", "tensor"),
            P("dp", "tensor"),
            P("dp", "tensor"),
            P("tensor", "dp"),
            P("dp", "tensor"),
            P("tensor", "dp"),
        )
        + (P(),) * 10,
        check_vma=False,
    )
```

```python
import math

import jax
import jax.numpy as jnp
import numpy as np
from jax import lax
from jax.experimental import pallas as pl
from jax.experimental.pallas import tpu as pltpu
from jax.sharding import PartitionSpec as P

norm_eps = 1e-05
big_negative = -1e30
root_half = 0.7071067811865476
root_two_pi_inv = 0.3989422804014327
bf16 = jnp.bfloat16
f32 = jnp.float32

tile = 128
reach = 2
span = (2 * reach + 1) * tile
wide = span + tile
chunk = 512
side = 256
block = 64
strip = 128
repeat = 4
TN = (((0,), (0,)), ((), ()))
NT = (((1,), (1,)), ((), ()))
NN = (((1,), (0,)), ((), ()))
light = pl.CostEstimate(flops=1_000_000, bytes_accessed=1_000_000, transcendentals=0)


def dot(left, right, dims=NN):
    return lax.dot_general(left, right, dims, preferred_element_type=f32)


def bucket_of(offset):
    distance = np.abs(offset)
    limits = 8.0 * 2.0 ** (np.arange(1, 8) / 2.0)
    counted = (distance[..., None] >= limits).sum(axis=-1)
    bucket = np.where(distance < 8, distance, 8 + counted)
    return (np.minimum(bucket, 15) + 16 * (offset < 0)).astype(np.int32)


def band_buckets():
    place = np.arange(wide)
    return bucket_of(np.where(place < span, place, place - wide) - reach * tile)


def key_tiles(b, tiles):
    return list(range(max(0, b - reach), min(tiles - 1, b + reach) + 1))


def whole(value):
    return pl.BlockSpec(value.shape, lambda *_: (0,) * len(value.shape))


def once(value):
    return pl.BlockSpec(value.shape, lambda *_: (0,) * len(value.shape), pipeline_mode=pl.Buffered(1))


def params(mebibytes):
    return pltpu.CompilerParams(vmem_limit_bytes=mebibytes * 1024 * 1024)


table_at = 8


def bundle_kernel(bq_ref, bv_ref, bu_ref, table_ref, out_ref):
    model = out_ref.shape[1]
    out_ref[...] = jnp.zeros_like(out_ref)
    out_ref[0:1, :] = jnp.concatenate([bq_ref[...].reshape(1, -1), bv_ref[...].reshape(1, -1)], axis=1)
    up = bu_ref[...].reshape(1, -1)
    for n in range(up.shape[1] // model):
        out_ref[1 + n : 2 + n, :] = up[:, n * model : (n + 1) * model]
    out_ref[table_at : table_at + table_ref.shape[0], : table_ref.shape[1]] = table_ref[...]


def bundle(bq, bv, bu, table):
    out_shape = jax.ShapeDtypeStruct((2 * table_at, 2 * bq.shape[0]), f32)
    return pl.pallas_call(bundle_kernel, out_shape=out_shape, compiler_params=params(60), name="bundle")(bq, bv, bu, table)


def attend_kernel(
    part, content_ref, query_ref, seg_ref, order_ref, flag_ref, hot_ref, bundle_ref, wq_ref, wk_ref, wv_ref,
    q_ref, k_ref, v_ref, o_ref, ot_ref, e_ref, linv_ref, *rest,
):
    mask_ref, bias_ref, band_ref, score_ref = rest[-4:]
    ahead = score_ref.shape[0]
    row_len = k_ref.shape[0]
    tiles = row_len // tile
    p = pl.program_id(0)

    @pl.when(p == 0)
    def _():
        row = pl.ds(part[0], 1)
        seg = seg_ref[row, :].astype(f32)
        order = order_ref[row, :].astype(f32)
        flag = flag_ref[row, :]
        at = lax.broadcasted_iota(jnp.int32, (1, row_len), 1)
        first = (seg != pltpu.roll(seg, 1, 1)) | (at == 0)
        key_content = jnp.where(flag == 0, -1.0, order)
        key_query = jnp.where(first, -1.0, key_content)

        def as_column(row):
            return jnp.transpose(jnp.broadcast_to(row, (tile, row_len)))

        seg_col, content_col, query_col = as_column(seg), as_column(key_content), as_column(key_query)
        for b in range(tiles):
            here = slice(b * tile, (b + 1) * tile)
            same = seg_col == seg[:, here]
            mask_ref[b, :, :tile] = jnp.where(same & (content_col <= order[:, here]), 0.0, big_negative)
            mask_ref[b, :, tile:] = jnp.where(same & (query_col < order[:, here]), 0.0, big_negative)
        width = bundle_ref.shape[1] // 2
        for n in range(2):
            for j in range(width // tile):
                at = n * width + j * tile
                bias_ref[8 * n + j : 8 * n + j + 1, :] = bundle_ref[0:1, at : at + tile]
        band_ref[...] = lax.dot_general(
            bundle_ref[table_at:, :tile], hot_ref[...], NT, precision=lax.Precision.HIGHEST, preferred_element_type=f32
        )
        if len(rest) == 5:
            for b in range(tiles):
                here = slice(b * tile, (b + 1) * tile)
                there = slice(row_len + b * tile, row_len + (b + 1) * tile)
                rest[0][:, here] = jnp.transpose(content_ref[here, :].astype(f32)).astype(bf16)
                rest[0][:, there] = jnp.transpose(query_ref[here, :].astype(f32)).astype(bf16)

    lane = lax.broadcasted_iota(jnp.int32, (1, tile), 1)
    half = tile // 2
    bq, bv = bias_ref[pl.ds(p, 1), :], bias_ref[pl.ds(p + 8, 1), :]
    q_ref[:row_len, :] = (dot(content_ref[...], wq_ref[...]) + bq).astype(bf16)
    q_ref[row_len:, :] = (dot(query_ref[...], wq_ref[...]) + bq).astype(bf16)
    kv = dot(content_ref[...], jnp.concatenate([wk_ref[...], wv_ref[...]], axis=1))
    k_ref[...] = kv[:, :tile].astype(bf16)
    v_ref[...] = (kv[:, tile:] + bv).astype(bf16)
    v_t = jnp.transpose(v_ref[...].astype(f32)).astype(bf16)
    keys = k_ref[...].astype(f32) * 0.125
    parts = [[None, None] for _ in range(tiles)]
    heads_in, bands = [], []
    for h in range(2):
        in_head = (lane >= h * half) & (lane < (h + 1) * half)
        heads_in.append(jnp.where(in_head, keys, 0.0).astype(bf16))
        band_row = band_ref[pl.ds(2 * p + h, 1), :]
        bands.append(pltpu.roll(jnp.broadcast_to(band_row, (tile, wide)), 0, 1, stride=1, stride_axis=0))
    turns = [(h, b) for b in range(tiles) for h in range(2)]

    def score(turn):
        h, b = turns[turn]
        q_tile = jnp.concatenate(
            [q_ref[b * tile : (b + 1) * tile, :], q_ref[row_len + b * tile : row_len + (b + 1) * tile, :]], axis=0
        )
        top = None
        for kb in key_tiles(b, tiles):
            d = b - kb + reach
            rows = slice(kb * tile, (kb + 1) * tile)
            bias = bands[h][:, d * tile : (d + 1) * tile]
            s = dot(heads_in[h][rows, :], q_tile, NT)
            s = s + jnp.concatenate([bias, bias], axis=1) + mask_ref[b, rows, :]
            score_ref[turn % ahead, rows, :] = s
            one_top = jnp.max(s, axis=0, keepdims=True)
            top = one_top if top is None else jnp.maximum(top, one_top)
        return top

    def weigh(turn, top):
        h, b = turns[turn]
        near = key_tiles(b, tiles)
        total = None
        weights = []
        for kb in near:
            rows = slice(kb * tile, (kb + 1) * tile)
            e = jnp.exp(score_ref[turn % ahead, rows, :] - top)
            one_total = jnp.sum(e, axis=0, keepdims=True)
            total = one_total if total is None else total + one_total
            e = e.astype(bf16)
            e_ref[0, h, b, rows, :] = e
            weights.append(e)
        inverse = 1.0 / total
        linv_ref[0, h * tiles + b : h * tiles + b + 1, :] = inverse
        mixed = dot(
            v_t[h * half : (h + 1) * half, near[0] * tile : (near[-1] + 1) * tile], jnp.concatenate(weights, axis=0)
        )
        parts[b][h] = mixed * inverse

    tops = [score(turn) for turn in range(ahead - 1)]
    for turn in range(len(turns)):
        if turn + ahead - 1 < len(turns):
            tops.append(score(turn + ahead - 1))
        weigh(turn, tops[turn])
    for b in range(tiles):
        both = jnp.concatenate(parts[b], axis=0)
        both_t = jnp.transpose(both).astype(bf16)
        both = both.astype(bf16)
        here = slice(b * tile, (b + 1) * tile)
        there = slice(row_len + b * tile, row_len + (b + 1) * tile)
        o_ref[here, :] = both_t[:tile]
        o_ref[there, :] = both_t[tile:]
        ot_ref[:, here] = both[:, :tile]
        ot_ref[:, there] = both[:, tile:]


def attend(part, content, query, rows, hot, bundled, wq, wk, wv, keep_t):
    row_len = rows[0].shape[1]
    tokens = 2 * row_len
    model, width = wq.shape
    pairs = width // tile
    tiles = row_len // tile
    own = lambda value: pl.BlockSpec((row_len, value.shape[1]), lambda p, part: (part[0], 0))
    cols = lambda n: pl.BlockSpec((n, tile), lambda p, part: (0, p))
    out = lambda *shape: jax.ShapeDtypeStruct(shape, bf16)
    out_specs = [
        cols(tokens),
        cols(row_len),
        cols(row_len),
        cols(tokens),
        pl.BlockSpec((tile, tokens), lambda p, part: (p, 0)),
        pl.BlockSpec((1, 2, tiles, row_len, 2 * tile), lambda p, part: (p, 0, 0, 0, 0)),
        pl.BlockSpec((1, 2 * tiles, 2 * tile), lambda p, part: (p, 0, 0)),
    ]
    out_shape = [
        out(tokens, width),
        out(row_len, width),
        out(row_len, width),
        out(tokens, width),
        out(width, tokens),
        out(pairs, 2, tiles, row_len, 2 * tile),
        jax.ShapeDtypeStruct((pairs, 2 * tiles, 2 * tile), f32),
    ]
    if keep_t:
        out_specs.append(pl.BlockSpec((model, tokens), lambda p, part: (0, 0)))
        out_shape.append(out(model, tokens))
    return pl.pallas_call(
        attend_kernel,
        grid_spec=pltpu.PrefetchScalarGridSpec(
            num_scalar_prefetch=1,
            grid=(pairs,),
            in_specs=[own(content), own(query)]
            + [whole(row) for row in rows]
            + [once(hot), once(bundled)]
            + [cols(model)] * 3,
            out_specs=out_specs,
            scratch_shapes=[pltpu.VMEM((tiles, row_len, 2 * tile), f32), pltpu.VMEM((16, tile), f32), pltpu.VMEM((8, wide), f32), pltpu.VMEM((4, row_len, 2 * tile), f32)],
        ),
        out_shape=out_shape,
        compiler_params=params(60),
        cost_estimate=light,
        name="attend",
    )(part, content, query, *rows, hot, bundled, wq, wk, wv)


def attend_back_kernel(
    al_ref, wo_ref, ot_ref, q_ref, k_ref, v_ref, e_ref, linv_ref, xt_ref, hot_ref,
    dw_ref, small_ref, dq_ref, dk_ref, dv_ref, dk_acc, dv_acc, g_acc, dp_ref, ds_ref,
):
    ahead = dp_ref.shape[0]
    row_len = k_ref.shape[0]
    tiles = row_len // tile
    half = tile // 2
    p = pl.program_id(0)
    lane = lax.broadcasted_iota(jnp.int32, (1, tile), 1)
    k_t = jnp.transpose(k_ref[...].astype(f32)).astype(bf16)
    do_all = dot(wo_ref[...], al_ref[...], NT).astype(bf16).astype(f32)
    dk_acc[...] = jnp.zeros_like(dk_acc)
    dv_acc[...] = jnp.zeros_like(dv_acc)
    g_acc[...] = jnp.zeros_like(g_acc)
    turns = [(h, b) for b in range(tiles) for h in range(2)]
    deltas, do_heads, q_heads = {}, {}, {}

    def places(b):
        return slice(b * tile, (b + 1) * tile), slice(row_len + b * tile, row_len + (b + 1) * tile)

    def spread(turn):
        h, b = turns[turn]
        here, there = places(b)
        mine = slice(h * half, (h + 1) * half)
        inverse = linv_ref[0, h * tiles + b : h * tiles + b + 1, :]
        do_t = jnp.concatenate([do_all[mine, here], do_all[mine, there]], axis=1)
        o_t = jnp.concatenate([ot_ref[mine, here], ot_ref[mine, there]], axis=1).astype(f32)
        deltas[turn] = jnp.sum(do_t * o_t, axis=0, keepdims=True) * inverse
        scaled = do_t * inverse
        blank = jnp.zeros_like(scaled)
        do_heads[turn] = jnp.concatenate([scaled, blank] if h == 0 else [blank, scaled], axis=0).astype(bf16)
        q_tile = jnp.concatenate([q_ref[here, :], q_ref[there, :]], axis=0)
        in_head = (lane >= h * half) & (lane < (h + 1) * half)
        q_heads[turn] = jnp.where(in_head, q_tile.astype(f32), 0.0).astype(bf16)
        for kb in key_tiles(b, tiles):
            rows = slice(kb * tile, (kb + 1) * tile)
            dp_ref[turn % ahead, rows, :] = dot(v_ref[rows, :], do_heads[turn])

    def combine(turn):
        h, b = turns[turn]
        for kb in key_tiles(b, tiles):
            d = b - kb + reach
            rows = slice(kb * tile, (kb + 1) * tile)
            ds = e_ref[0, h, b, rows, :].astype(f32) * (dp_ref[turn % ahead, rows, :] - deltas[turn])
            g_acc[h, :, d * tile : (d + 1) * tile] += ds[:, :tile] + ds[:, tile:]
            ds_ref[b % 2, h, rows, :] = ds.astype(bf16)

    def gather(b):
        here, there = places(b)
        near = key_tiles(b, tiles)
        keys = slice(near[0] * tile, (near[-1] + 1) * tile)
        two = (2 * b, 2 * b + 1)
        dv_acc[keys, :] += dot(
            jnp.concatenate([e_ref[0, h, b, keys, :] for h in range(2)], axis=1),
            jnp.concatenate([do_heads[turn] for turn in two], axis=1),
            NT,
        )
        dk_acc[keys, :] += dot(
            jnp.concatenate([ds_ref[b % 2, h, keys, :] for h in range(2)], axis=1),
            jnp.concatenate([q_heads[turn] for turn in two], axis=0),
        )
        dq_t = [dot(k_t[h * half : (h + 1) * half, keys], ds_ref[b % 2, h, keys, :]) for h in range(2)]
        dq = (jnp.transpose(jnp.concatenate(dq_t, axis=0)) * 0.125).astype(bf16)
        dq_ref[here, :] = dq[:tile]
        dq_ref[there, :] = dq[tile:]

    for turn in range(ahead - 1):
        spread(turn)
    for turn in range(len(turns)):
        if turn + ahead - 1 < len(turns):
            spread(turn + ahead - 1)
        combine(turn)
        if turn % 2 and turn >= 3:
            gather(turn // 2 - 1)
    gather(tiles - 1)
    dk = (dk_acc[...] * 0.125).astype(bf16)
    dv = dv_acc[...].astype(bf16)
    dq = dq_ref[...]
    dk_ref[...] = dk
    dv_ref[...] = dv
    dw_ref[:, :tile] = dot(xt_ref[...], dq).astype(bf16)
    dw_ref[:, tile:] = dot(xt_ref[:, :row_len], jnp.concatenate([dk, dv], axis=1)).astype(bf16)
    row = lax.broadcasted_iota(jnp.int32, (8, wide), 0)
    small_ref[0, 0:1, :] = jnp.sum(dq.astype(f32), axis=0, keepdims=True)
    small_ref[0, 1:2, :] = jnp.sum(dv.astype(f32), axis=0, keepdims=True)
    for h in range(2):
        folds = [g_acc[h, a : a + 8, :] for a in range(0, tile, 8)]
        step = 8
        while len(folds) > 1:
            folds = [folds[a] + pltpu.roll(folds[a + 1], wide - step, 1) for a in range(0, len(folds), 2)]
            step *= 2
        fold = folds[0]
        for bit in (1, 2, 4):
            fold = jnp.where((row & bit) != 0, pltpu.roll(fold, wide - bit, 1), fold)
        by_bucket = lax.dot_general(fold, hot_ref[...], NN, precision=lax.Precision.HIGHEST, preferred_element_type=f32)
        small_ref[0, 2 + h : 3 + h, :] = jnp.sum(by_bucket, axis=0, keepdims=True)


def attend_back(from_pair, pairs, al, wo, ot, q, k, v, e, linv, xt, hot):
    tokens, model = al.shape
    width = pairs * tile
    row_len = k.shape[0]
    tiles = row_len // tile
    cols = lambda n: pl.BlockSpec((n, tile), lambda p: (0, p + from_pair))
    rows = lambda n: pl.BlockSpec((tile, n), lambda p: (p + from_pair, 0))
    cols_out = lambda n: pl.BlockSpec((n, tile), lambda p: (0, p))
    shape = jax.ShapeDtypeStruct
    return pl.pallas_call(
        attend_back_kernel,
        grid=(pairs,),
        in_specs=[
            once(al),
            rows(model),
            rows(tokens),
            cols(tokens),
            cols(row_len),
            cols(row_len),
            pl.BlockSpec((1, 2, tiles, row_len, 2 * tile), lambda p: (p + from_pair, 0, 0, 0, 0)),
            pl.BlockSpec((1, 2 * tiles, 2 * tile), lambda p: (p + from_pair, 0, 0)),
            once(xt),
            once(hot),
        ],
        out_specs=[pl.BlockSpec((model, 3 * tile), lambda p: (0, p))]
        + [pl.BlockSpec((1, 8, tile), lambda p: (p, 0, 0)), cols_out(tokens), cols_out(row_len), cols_out(row_len)],
        out_shape=[shape((model, 3 * width), bf16)]
        + [shape((pairs, 8, tile), f32), shape((tokens, width), bf16)]
        + [shape((row_len, width), bf16)] * 2,
        scratch_shapes=[
            pltpu.VMEM((row_len, tile), f32),
            pltpu.VMEM((row_len, tile), f32),
            pltpu.VMEM((2, tile, wide), f32),
            pltpu.VMEM((3, row_len, 2 * tile), f32),
            pltpu.VMEM((2, 2, row_len, 2 * tile), bf16),
        ],
        compiler_params=params(26),
        cost_estimate=light,
        name="attend_back",
    )(al, wo, ot, q, k, v, e, linv, xt, hot)


def inputs_back_kernel(residual_ref, *refs):
    content_ref, query_ref = refs[-2:]
    row_len = content_ref.shape[0]
    content = residual_ref[:row_len, :]
    query = residual_ref[row_len:, :]
    for at in range(0, len(refs) - 2, 6):
        dq_ref, dk_ref, dv_ref, wq_ref, wk_ref, wv_ref = refs[at : at + 6]
        wq = wq_ref[...]
        content = content + dot(dq_ref[:row_len, :], wq, NT) + dot(dk_ref[...], wk_ref[...], NT) + dot(dv_ref[...], wv_ref[...], NT)
        query = query + dot(dq_ref[row_len:, :], wq, NT)
    content_ref[...] = content
    query_ref[...] = query


def inputs_back(residual, groups):
    tokens, model = residual.shape
    shape = jax.ShapeDtypeStruct((tokens // 2, model), f32)
    args = [residual]
    specs = [once(residual)]
    for grads, weights, at, width in groups:
        args += list(grads) + list(weights)
        specs += [once(one) for one in grads]
        specs += [pl.BlockSpec((model, width), lambda i, at=at: (0, at), pipeline_mode=pl.Buffered(1)) for _ in weights]
    return pl.pallas_call(
        inputs_back_kernel,
        grid=(1,),
        in_specs=specs,
        out_specs=[once(shape)] * 2,
        out_shape=[shape] * 2,
        compiler_params=params(30),
        cost_estimate=light,
        name="inputs_back",
    )(*args)


def normed_of(values):
    centre = jnp.mean(values, axis=-1, keepdims=True)
    centred = values - centre
    variance = jnp.mean(centred * centred, axis=-1, keepdims=True)
    inv_scale = lax.rsqrt(variance + norm_eps)
    return centred * inv_scale, inv_scale


def norm_back(upstream, normed, inv_scale, gain_vec):
    scaled = upstream * gain_vec
    centre = jnp.mean(scaled, axis=-1, keepdims=True)
    along_normed = jnp.mean(scaled * normed, axis=-1, keepdims=True)
    return inv_scale * (scaled - centre - normed * along_normed)


def eight(values):
    total = values[0:8]
    for i in range(8, values.shape[0], 8):
        total = total + values[i : i + 8]
    return total


def gelu_parts(u):
    bell = jnp.exp(-0.5 * (u * u))
    t = 1.0 / (1.0 + (0.3275911 * root_half) * jnp.abs(u))
    poly = 0.5307027145
    poly = poly * t - 0.7265760135
    poly = poly * t + 0.7107068705
    poly = poly * t - 0.142248368
    poly = poly * t + 0.127414796
    tail = poly * t * bell
    cdf = jnp.where(u >= 0.0, 1.0 - tail, tail)
    return u * cdf, cdf + (u * root_two_pi_inv) * bell


def feed_kernel(
    part, o0_ref, o1_ref, wo0_ref, wo1_ref, content_ref, query_ref, bo_ref, g1_ref, s1_ref, wu0_ref, wu1_ref, bu0_ref, bu1_ref,
    wd0_ref, wd1_ref, bd_ref, g2_ref, s2_ref, cu_ref, qu_ref,
    normed_out, first_out, second_out, inv_ref, fc_ref, fq_ref, sums_ref, dwd0_ref, dwd1_ref, low0_ref, low1_ref, dbu0_ref, dbu1_ref,
    normed_ref, first_ref, acc_ref, d2_ref, hidden_ref, slope_ref, bu_ref, up_ref, sems,
):
    row_len = content_ref.shape[0]
    bo, g1, s1, bd, g2, s2 = (ref[...].reshape(1, -1) for ref in (bo_ref, g1_ref, s1_ref, bd_ref, g2_ref, s2_ref))
    tokens, model = acc_ref.shape
    steps = pl.num_programs(0)
    i = pl.program_id(0)
    steps_of_half = hidden_ref.shape[0] // 2
    copies = [
        pltpu.make_async_copy(normed_ref, normed_out, sems.at[0]),
        pltpu.make_async_copy(first_ref, first_out, sems.at[1]),
        pltpu.make_async_copy(acc_ref, second_out, sems.at[2]),
    ]

    @pl.when(i == 0)
    def _():
        acc_ref[...] = dot(o0_ref[...], wo0_ref[...]) + dot(o1_ref[...], wo1_ref[...])
        for n, one_ref in enumerate((bu0_ref, bu1_ref)):
            flat = jnp.concatenate([one_ref[1 + j : 2 + j, :] for j in range(steps_of_half * chunk // model)], axis=1)
            for j in range(flat.shape[1] // chunk):
                at = n * (flat.shape[1] // chunk) + j
                bu_ref[at : at + 1, :] = flat[:, j * chunk : (j + 1) * chunk]
        for s, x_ref in enumerate((content_ref, query_ref)):

            def step(r, _, s=s, x_ref=x_ref):
                from_rows = pl.ds(pl.multiple_of(r * strip, strip), strip)
                rows = pl.ds(pl.multiple_of(s * row_len + r * strip, strip), strip)
                normed, inv = normed_of(x_ref[from_rows, :].astype(f32) + acc_ref[rows, :] + bo)
                first = normed * g1 + s1
                normed_ref[rows, :] = normed
                inv_ref[rows, :] = inv
                first_ref[rows, :] = first.astype(bf16)
                acc_ref[rows, :] = first + bd
                return 0

            lax.fori_loop(0, row_len // strip, step, 0, unroll=repeat)
        copies[1].start()

    def forward(wu_ref, wd_ref):
        bias = bu_ref[pl.ds(i, 1), :]
        splits = [slice(j, j + side) for j in range(0, chunk, side)]
        for j, cols in enumerate(splits):
            up_ref[:, cols] = dot(first_ref[...], wu_ref[:, cols]) + bias[:, cols]
        for cols in splits:
            for r in range(0, tokens, block):
                rows = slice(r, r + block)
                hidden, slope = gelu_parts(up_ref[rows, cols])
                hidden_ref[i, rows, cols] = hidden.astype(bf16)
                slope_ref[i, rows, cols] = slope.astype(bf16)
        acc_ref[...] += dot(hidden_ref[i], wd_ref[...])

    @pl.when(i < steps // 4)
    def _():
        forward(wu0_ref, wd0_ref)

    @pl.when((i >= steps // 4) & (i < steps // 2))
    def _():
        forward(wu1_ref, wd1_ref)

    @pl.when(i == steps // 2 - 1)
    def _():
        sums = (jnp.zeros((8, model), f32),) * 3
        for s, (c_ref, out_ref) in enumerate(((cu_ref, fc_ref), (qu_ref, fq_ref))):

            def step(r, sums, s=s, c_ref=c_ref, out_ref=out_ref):
                from_rows = pl.ds(pl.multiple_of(r * strip, strip), strip)
                rows = pl.ds(pl.multiple_of(s * row_len + r * strip, strip), strip)
                normed, inv = normed_of(acc_ref[rows, :])
                out_ref[from_rows, :] = (normed * g2 + s2).astype(bf16)
                c = c_ref[from_rows, :].astype(f32)
                second = norm_back(c, normed, inv, g2)
                acc_ref[rows, :] = second
                d2_ref[rows, :] = second.astype(bf16)
                return (sums[0] + eight(c * normed), sums[1] + eight(c), sums[2] + eight(second))

            sums = lax.fori_loop(0, row_len // strip, step, sums, unroll=repeat)
        for n in range(3):
            sums_ref[n : n + 1, :] = jnp.sum(sums[n], axis=0, keepdims=True)
        copies[2].start()

    def backward(wd_ref, dwd_ref, low_ref, dbu_ref):
        at = i - steps // 2
        up_ref[...] = dot(d2_ref[...], wd_ref[...], NT)
        dwd_ref[...] = dot(d2_ref[...], hidden_ref[at], TN).astype(bf16)
        total = jnp.zeros((8, chunk), f32)
        for r in range(0, tokens, block):
            rows = slice(r, r + block)
            grad = (up_ref[rows, :] * slope_ref[at, rows, :].astype(f32)).astype(bf16)
            low_ref[rows, :] = grad
            total = total + eight(grad.astype(f32))
        dbu_ref[...] = jnp.sum(total, axis=0, keepdims=True)

    @pl.when((i >= steps // 2) & (i < steps * 3 // 4))
    def _():
        backward(wd0_ref, dwd0_ref, low0_ref, dbu0_ref)

    @pl.when(i >= steps * 3 // 4)
    def _():
        backward(wd1_ref, dwd1_ref, low1_ref, dbu1_ref)

    @pl.when(i == 1)
    def _():
        copies[0].start()

    @pl.when(i == steps - 1)
    def _():
        for copy in copies:
            copy.wait()


def feed(part, o, wo, content, query, bo, g1, s1, wu, bu, wd, bd, g2, s2, cu, qu):
    tokens = o[0].shape[0]
    row_len = cu.shape[0]
    model, width = wu[0].shape
    c = width // chunk
    own = pl.BlockSpec((row_len, model), lambda i, part: (part[0], 0), pipeline_mode=pl.Buffered(1))
    up0 = lambda i: jnp.minimum(i, c - 1)
    up1 = lambda i: jnp.clip(i - c, 0, c - 1)
    down0 = lambda i: jnp.where(i < 2 * c, jnp.minimum(i, c - 1), jnp.minimum(i - 2 * c, c - 1))
    down1 = lambda i: jnp.where(i < 3 * c, jnp.clip(i - c, 0, c - 1), i - 3 * c)
    back0 = lambda i: jnp.clip(i - 2 * c, 0, c - 1)
    back1 = lambda i: jnp.clip(i - 3 * c, 0, c - 1)
    cols = lambda n, at: pl.BlockSpec((n, chunk), lambda i, part: (0, at(i)))
    rows = lambda at: pl.BlockSpec((chunk, model), lambda i, part: (at(i), 0))
    anywhere = pl.BlockSpec(memory_space=pl.ANY)
    shape = jax.ShapeDtypeStruct
    out_shape = [
        shape((tokens, model), f32),
        shape((tokens, model), bf16),
        shape((tokens, model), f32),
        shape((tokens, 1), f32),
        shape((row_len, model), bf16),
        shape((row_len, model), bf16),
        shape((8, model), f32),
    ]
    out_shape += [shape((model, width), bf16)] * 2 + [shape((tokens, width), bf16)] * 2 + [shape((1, width), f32)] * 2
    out_specs = [anywhere] * 3 + [once(one) for one in out_shape[3:7]]
    for n in (model, tokens, 1):
        out_specs += [cols(n, back0), cols(n, back1)]
    return pl.pallas_call(
        feed_kernel,
        grid_spec=pltpu.PrefetchScalarGridSpec(
            num_scalar_prefetch=1,
            grid=(4 * c,),
            in_specs=[once(o[0]), once(o[1]), once(wo[0]), once(wo[1]), own, own, once(bo), once(g1), once(s1)]
            + [cols(model, up0), cols(model, up1), once(bu[0]), once(bu[1]), rows(down0), rows(down1)]
            + [once(bd), once(g2), once(s2), once(cu), once(qu)],
            out_specs=out_specs,
            scratch_shapes=[
                pltpu.VMEM((tokens, model), f32),
                pltpu.VMEM((tokens, model), bf16),
                pltpu.VMEM((tokens, model), f32),
                pltpu.VMEM((tokens, model), bf16),
                pltpu.VMEM((2 * c, tokens, chunk), bf16),
                pltpu.VMEM((2 * c, tokens, chunk), bf16),
                pltpu.VMEM((8, chunk), f32),
                pltpu.VMEM((tokens, chunk), f32),
                pltpu.SemaphoreType.DMA((3,)),
            ],
        ),
        out_shape=out_shape,
        compiler_params=params(60),
        cost_estimate=light,
        name="feed",
    )(part, o[0], o[1], wo[0], wo[1], content, query, bo, g1, s1, wu[0], wu[1], bu[0], bu[1], wd[0], wd[1], bd, g2, s2, cu, qu)


def up_units(first_ref, low_ref, wu_ref, dwu_ref, acc_ref):
    @pl.when(pl.program_id(0) == 0)
    def _():
        acc_ref[...] = jnp.zeros_like(acc_ref)

    dwu_ref[...] = dot(first_ref[...], low_ref[...], TN).astype(bf16)
    acc_ref[...] += dot(low_ref[...], wu_ref[...], NT)


def up_back(first, low, wu):
    tokens, width = low.shape
    model = first.shape[1]
    cols = lambda n: pl.BlockSpec((n, chunk), lambda i: (0, i))
    acc = jax.ShapeDtypeStruct((tokens, model), f32)
    return pl.pallas_call(
        up_units,
        grid=(width // chunk,),
        in_specs=[once(first), cols(tokens), cols(model)],
        out_specs=[cols(model), once(acc)],
        out_shape=[jax.ShapeDtypeStruct((model, width), bf16), acc],
        compiler_params=params(60),
        cost_estimate=light,
        name="up_back",
    )(first, low, wu)


def up_back_last_kernel(
    first_ref, low_ref, wu_ref, g1_ref, inv_ref, normed_in, second_in, part_in, o0_in, o1_in,
    dwu_ref, residual_ref, al_ref, sums_ref, dwo0_ref, dwo1_ref,
    acc_ref, normed_ref, second_ref, part_ref, o0_ref, o1_ref, sems,
):
    tokens, model = acc_ref.shape
    i = pl.program_id(0)
    pairs = ((normed_in, normed_ref), (second_in, second_ref), (part_in, part_ref), (o0_in, o0_ref), (o1_in, o1_ref))
    copies = [pltpu.make_async_copy(here, there, sems.at[n]) for n, (here, there) in enumerate(pairs)]

    @pl.when(i == 0)
    def _():
        for copy in copies:
            copy.start()

    up_units(first_ref, low_ref, wu_ref, dwu_ref, acc_ref)

    @pl.when(i == pl.num_programs(0) - 1)
    def _():
        for copy in copies:
            copy.wait()
        g1 = g1_ref[...].reshape(1, -1)

        def step(r, sums):
            rows = pl.ds(pl.multiple_of(r * strip, strip), strip)
            back, normed = acc_ref[rows, :] + part_ref[rows, :] + second_ref[rows, :], normed_ref[rows, :]
            residual = norm_back(back, normed, inv_ref[rows, :], g1)
            residual_ref[rows, :] = residual
            al_ref[rows, :] = residual.astype(bf16)
            return (sums[0] + eight(back * normed), sums[1] + eight(back), sums[2] + eight(residual))

        sums = lax.fori_loop(0, tokens // strip, step, (jnp.zeros((8, model), f32),) * 3, unroll=repeat)
        for n in range(3):
            sums_ref[n : n + 1, :] = jnp.sum(sums[n], axis=0, keepdims=True)
        dwo0_ref[...] = dot(al_ref[...], o0_ref[...], TN).astype(bf16)
        dwo1_ref[...] = dot(al_ref[...], o1_ref[...], TN).astype(bf16)


def up_back_last(first, low, wu, g1, inv, normed, second, partial, o):
    tokens, width = low.shape
    model = first.shape[1]
    cols = lambda n: pl.BlockSpec((n, chunk), lambda i: (0, i))
    anywhere = pl.BlockSpec(memory_space=pl.ANY)
    shape = jax.ShapeDtypeStruct
    out_shape = [
        shape((model, width), bf16),
        shape((tokens, model), f32),
        shape((tokens, model), bf16),
        shape((8, model), f32),
        shape((model, o[0].shape[1]), bf16),
        shape((model, o[1].shape[1]), bf16),
    ]
    return pl.pallas_call(
        up_back_last_kernel,
        grid=(width // chunk,),
        in_specs=[once(first), cols(tokens), cols(model), once(g1), once(inv)] + [anywhere] * 5,
        out_specs=[cols(model)] + [once(one) for one in out_shape[1:]],
        out_shape=out_shape,
        scratch_shapes=[pltpu.VMEM((tokens, model), f32)] * 4
        + [pltpu.VMEM(o[0].shape, bf16), pltpu.VMEM(o[1].shape, bf16), pltpu.SemaphoreType.DMA((5,))],
        compiler_params=params(40),
        cost_estimate=light,
        name="up_back_last",
    )(first, low, wu, g1, inv, normed, second, partial, o[0], o[1])


def pack_kernel(part, one_ref, two_ref, dbu0_ref, dbu1_ref, *rest):
    smalls, out_ref = rest[:-1], rest[-1]
    first = part[0] == 0
    model = one_ref.shape[1]
    out_ref[...] = jnp.zeros_like(out_ref)
    out_ref[0:3, :] = one_ref[0:3, :]
    out_ref[3:6, :] = two_ref[0:3, :]
    pairs = model // tile // 2
    own = jnp.concatenate([ref[...] for ref in smalls[:-1]], axis=0)
    other = smalls[-1][...]
    for row in range(2):
        halves = [jnp.concatenate([half[n, row : row + 1, :] for n in range(pairs)], axis=1) for half in (own, other)]
        out_ref[6 + row : 7 + row, : model // 2] = jnp.where(first, halves[0], halves[1])
        out_ref[6 + row : 7 + row, model // 2 :] = jnp.where(first, halves[1], halves[0])
    tables = [
        jnp.concatenate([half[n, 2 + h : 3 + h, :] for n in range(pairs) for h in range(2)], axis=1) for half in (own, other)
    ]
    ups = [dbu0_ref[...], dbu1_ref[...]]
    for row, (a, b) in enumerate(((0, 1), (1, 0))):
        out_ref[8 + row : 9 + row, :] = jnp.where(first, tables[a], tables[b])
        up = jnp.where(first, ups[a], ups[b])
        rows = up.shape[1] // model
        for n in range(rows):
            at = 10 + row * rows + n
            out_ref[at : at + 1, :] = up[:, n * model : (n + 1) * model]


def pack(part, one, two, dbu0, dbu1, smalls):
    args = (one, two, dbu0, dbu1) + tuple(smalls)
    model = one.shape[1]
    return pl.pallas_call(
        pack_kernel,
        grid_spec=pltpu.PrefetchScalarGridSpec(
            num_scalar_prefetch=1, grid=(1,), in_specs=[whole(arg) for arg in args], out_specs=pl.BlockSpec((16, model), lambda *_: (0, 0))
        ),
        out_shape=jax.ShapeDtypeStruct((16, model), f32),
        compiler_params=params(4),
        name="pack",
    )(part, *args)


def exchange(value, axis_name, bit):
    count = lax.axis_size(axis_name)
    return lax.ppermute(value, axis_name, [(i, i ^ bit) for i in range(count)])


class Term:
    def __init__(self, pieces, left):
        self.pieces, self.left = pieces, left

    def places(self, flips, free):
        weight = {one: 1 << (len(self.left) - 1 - n) for n, one in enumerate(self.left)}
        own = {one: -w if one in flips else w for one, w in weight.items() if one not in free}
        start = sum(weight[one] for one in flips)
        for n in range(1 << len(free)):
            yield start + sum(weight[one] for m, one in enumerate(free) if n >> (len(free) - 1 - m) & 1), own


class Chain:
    def __init__(self, parts, order):
        bits = sum(len(step) for step in order)
        self.block = parts[0][0][0].shape[0] >> bits
        self.left = tuple(range(bits - 1, -1, -1))
        self.order = list(order)
        self.parts = [[Term([(array, 0, low, high - low)], self.left) for array, low, high in terms] for terms in parts]

    def step(self):
        bits = self.order.pop(0)
        self.left = tuple(one for one in self.left if one not in bits)
        return bits


def departures(chains, small=False):
    (bits,) = {chain.step() for chain in chains}
    before = [list(terms) for chain in chains for terms in chain.parts]
    masks = range(1, 1 << len(bits))
    return [Parcel(chains, before, [one for n, one in enumerate(bits) if mask >> n & 1], small) for mask in masks]


class Parcel:
    def __init__(self, chains, before, flips, small):
        self.chains, self.flips, self.small = chains, flips, small
        self.block = chains[0].block
        self.parts = list(zip(before, [chain.left for chain in chains for _ in chain.parts]))
        widths = [sum(piece[3] for piece in terms[0].pieces) for terms, _ in self.parts]
        self.width = math.gcd(*widths)
        self.spots, self.rows = [], 0
        for (_, left), n in zip(self.parts, widths):
            spots = []
            for at in range(0, n, self.width):
                spots.append((self.rows, at))
                self.rows += self.block << len(left)
            self.spots.append(spots)

    def go(self, sent):
        self.coming = exchange(sent, "dp", sum(1 << one for one in self.flips))

    def land(self, coming):
        spots = iter(self.spots)
        for chain in self.chains:
            for terms in chain.parts:
                terms.append(Term([(coming, row, 0, self.width) for row, _ in next(spots)], chain.left))
        return (coming, self.rows) if self.small else None


def read_plain(terms, flips, free, block):
    index = lax.axis_index("dp")
    total = 0.0
    for term in terms:
        rows = block << len(term.left)
        value = jnp.concatenate([array[row : row + rows, col : col + n] for array, row, col, n in term.pieces], axis=1)
        value = value.reshape((2,) * len(term.left) + (block, value.shape[1]))
        for axis, one in reversed(list(enumerate(term.left))):
            if one not in free:
                mine = (index >> one) & 1
                value = lax.dynamic_index_in_dim(value, 1 - mine if one in flips else mine, axis, keepdims=False)
        total = total + value.reshape(block << len(free), value.shape[-1]).astype(f32)
    return total


class Reader:
    def __init__(self, block):
        self.block, self.arrays, self.copies, self.counts = block, [], [], {}

    def read(self, terms, flips, free):
        blocks = [[] for _ in range(1 << len(free))]
        for term in terms:
            for n, (at, own) in enumerate(term.places(flips, free)):
                slots = []
                for array, row, col, width in term.pieces:
                    known = [m for m, one in enumerate(self.arrays) if one is array]
                    if not known:
                        known = [len(self.arrays)]
                        self.arrays.append(array)
                    slot = self.counts.get((width, array.dtype), 0)
                    self.counts[(width, array.dtype)] = slot + 1
                    self.copies.append((known[0], row + at * self.block, own, col, width, array.dtype, slot))
                    slots.append((width, array.dtype, slot))
                blocks[n].append(slots)
        return blocks

    def scratch(self):
        kinds = list(self.counts)
        return [pltpu.VMEM((self.counts[kind], self.block, kind[0]), kind[1]) for kind in kinds] + [
            pltpu.SemaphoreType.DMA((len(self.copies),))
        ]

    def start(self, index, array_refs, scratch):
        buffers = dict(zip(self.counts, scratch))
        made = []
        for n, (array, row, own, col, width, dtype, slot) in enumerate(self.copies):
            at = row + self.block * sum(((index >> one) & 1) * w for one, w in own.items())
            rows = pl.ds(pl.multiple_of(at, 16), self.block)
            copy = pltpu.make_async_copy(array_refs[array].at[rows, col : col + width], buffers[(width, dtype)].at[slot], scratch[-1].at[n])
            copy.start()
            made.append(copy)
        return buffers, made

    @staticmethod
    def add(buffers, terms):
        total = None
        for slots in terms:
            value = [buffers[(width, dtype)][slot].astype(f32) for width, dtype, slot in slots]
            value = value[0] if len(value) == 1 else jnp.concatenate(value, axis=1)
            total = value if total is None else total + value
        return total


def halves_of(got, rows):
    return [(coming[at : at + rows], coming[at + rows : at + 2 * rows]) for coming, at in got]


def join_small(packed, got):
    wide = [jnp.concatenate(one, axis=1).astype(f32) for one in got]
    if len(wide) == 3:
        return (packed + wide[0]) + (wide[1] + wide[2])
    return packed + wide[0] if wide else packed


def post(index, parcels, packed=None, got=()):
    block = parcels[0].block
    smalls = [parcel for parcel in parcels if parcel.small]
    if block % 16:
        sents = []
        if smalls:
            packed = lax.reduce_precision(join_small(packed, halves_of(got, packed.shape[0])), 8, 7)
        for parcel in parcels:
            values = []
            for (terms, left), spots in zip(parcel.parts, parcel.spots):
                value = read_plain(terms, parcel.flips, left, block).astype(bf16)
                values += [value[:, at : at + parcel.width] for _, at in spots]
            if parcel.small:
                half = packed.shape[1] // 2
                values += [packed[:, :half].astype(bf16), packed[:, half:].astype(bf16)]
            sents.append(jnp.concatenate(values, axis=0))
        return sents + ([packed] if smalls else [])
    reader = Reader(block)
    plans = [[reader.read(terms, parcel.flips, left) for terms, left in parcel.parts] for parcel in parcels]
    shapes = [jax.ShapeDtypeStruct((parcel.rows + (2 * packed.shape[0] if parcel.small else 0), parcel.width), bf16) for parcel in parcels]
    extra, extra_specs = [], []
    if smalls:
        extra = [packed] + [coming for coming, _ in got for _ in range(2)]
        shapes.append(jax.ShapeDtypeStruct(packed.shape, f32))
        extra_specs = [once(packed)] + [
            pl.BlockSpec((packed.shape[0], coming.shape[1]), lambda *_, n=at // packed.shape[0] + half: (n, 0))
            for coming, at in got
            for half in range(2)
        ]

    def kernel(index_ref, *refs):
        array_refs = refs[: len(reader.arrays)]
        extra_refs = refs[len(reader.arrays) : len(reader.arrays) + len(extra)]
        outs = refs[len(reader.arrays) + len(extra) :][: len(shapes)]
        buffers, made = reader.start(index_ref[0], array_refs, refs[len(reader.arrays) + len(extra) + len(shapes) :])
        if smalls:
            value = join_small(
                extra_refs[0][...], [(extra_refs[n][...], extra_refs[n + 1][...]) for n in range(1, len(extra), 2)]
            ).astype(bf16)
            outs[-1][...] = value.astype(f32)
            for parcel, out in zip(parcels, outs):
                if parcel.small:
                    half, rows = value.shape[1] // 2, value.shape[0]
                    at = parcel.rows
                    out[at : at + rows, :] = value[:, :half]
                    out[at + rows : at + 2 * rows, :] = value[:, half:]
        for copy in made:
            copy.wait()
        for parcel, plan, out in zip(parcels, plans, outs):
            for spots, blocks in zip(parcel.spots, plan):
                for n, terms in enumerate(blocks):
                    value = reader.add(buffers, terms).astype(bf16)
                    for row, at in spots:
                        out[row + n * block : row + (n + 1) * block, :] = value[:, at : at + parcel.width]

    return pl.pallas_call(
        kernel,
        grid_spec=pltpu.PrefetchScalarGridSpec(
            num_scalar_prefetch=1,
            grid=(1,),
            in_specs=[pl.BlockSpec(memory_space=pltpu.HBM)] * len(reader.arrays) + extra_specs,
            out_specs=[once(one) for one in shapes],
            scratch_shapes=reader.scratch(),
        ),
        out_shape=shapes,
        compiler_params=params(16),
        cost_estimate=light,
        name="post",
    )(index, *reader.arrays, *extra)


def total_of(index, name, parts, block, extra, shapes, write):
    plain = block % 16
    reader = Reader(block)
    plans = [] if plain else [reader.read(terms, (), ())[0] for terms in parts]
    arrays = [read_plain(terms, (), (), block) for terms in parts] if plain else reader.arrays

    def kernel(index_ref, *refs):
        array_refs, extra_refs = refs[: len(arrays)], refs[len(arrays) :][: len(extra)]
        outs, scratch = refs[len(arrays) + len(extra) :][: len(shapes)], refs[len(arrays) + len(extra) + len(shapes) :]
        if plain:
            sums = [ref[...] for ref in array_refs]
        else:
            buffers, made = reader.start(index_ref[0], array_refs, scratch)
            for copy in made:
                copy.wait()
            sums = [reader.add(buffers, plan) for plan in plans]
        write(sums, extra_refs, outs)

    return pl.pallas_call(
        kernel,
        grid_spec=pltpu.PrefetchScalarGridSpec(
            num_scalar_prefetch=1,
            grid=(1,),
            in_specs=[once(one) if plain else pl.BlockSpec(memory_space=pltpu.HBM) for one in arrays] + [once(one) for one in extra],
            out_specs=[once(one) for one in shapes],
            scratch_shapes=[] if plain else reader.scratch(),
        ),
        out_shape=shapes,
        compiler_params=params(8),
        cost_estimate=light,
        name=name,
    )(index, *arrays, *extra)


def finish_wide(index, groups, block):
    shapes = [jax.ShapeDtypeStruct((block, sum(sum(piece[3] for piece in terms[0].pieces) for terms in group)), f32) for group in groups]

    def write(sums, _, outs):
        for group, out in zip(groups, outs):
            out[...] = jnp.concatenate(sums[: len(group)], axis=1)
            sums = sums[len(group) :]

    return total_of(index, "finish_wide", [terms for group in groups for terms in group], block, [], shapes, write)


def finish(index, packed, far, parts, block, units, buckets, heads):
    model = packed.shape[1]
    f32_of = lambda *shape: jax.ShapeDtypeStruct(shape, f32)
    shapes = [f32_of(model)] * 8 + [f32_of(units), f32_of(heads, buckets)] + [f32_of(block, len(parts) * tile)] * 3

    def write(sums, extra_refs, outs):
        rows = extra_refs[0][...] + extra_refs[1][...]
        for n in range(8):
            outs[n][...] = rows[n : n + 1, :].reshape(model)
        up = jnp.concatenate([rows[n : n + 1, :] for n in range(10, 10 + units // model)], axis=1)
        outs[8][...] = up.reshape(units)
        heads_of = [rows[8 + half : 9 + half, n * tile : (n + 1) * tile] for half in range(2) for n in range(model // tile)]
        outs[9][...] = jnp.concatenate(heads_of, axis=0)[:heads, :buckets]
        for n in range(3):
            for pair, value in enumerate(sums):
                outs[10 + n][:, pair * tile : (pair + 1) * tile] = value[:, n * tile : (n + 1) * tile]

    return total_of(index, "finish", parts, block, [packed, far], shapes, write)


def wide_groups(x, y, z):
    return [[z.parts[1]], [y.parts[0], z.parts[0]], [x.parts[0]]]


def gate(*values):
    return lax.optimization_barrier(values)


def local(
    content_input,
    query_input,
    segment_ids,
    orders,
    predicted,
    query_weight,
    query_bias,
    key_weight,
    value_weight,
    value_bias,
    out_weight,
    out_bias,
    first_gain,
    first_shift,
    up_weight,
    up_bias,
    down_weight,
    down_bias,
    second_gain,
    second_shift,
    bias_table,
    content_upstream,
    query_upstream,
):
    tensor_index = lax.axis_index("tensor")
    bits = lax.axis_size("dp").bit_length() - 1
    part = tensor_index.astype(jnp.int32).reshape(1)
    far_of = lambda value: exchange(value, "tensor", 1)

    def order(*first):
        named = [bit for step in first for bit in step]
        return list(first) + [(bit,) for bit in range(bits) if bit not in named]

    own_bundle = bundle(query_bias, value_bias, up_bias, bias_table.T)
    own_attention = (own_bundle, query_weight, key_weight, value_weight)
    far_attention = tuple(far_of(value) for value in own_attention)
    rows = (segment_ids, orders, predicted)
    heads = bias_table.shape[1]
    buckets = band_buckets()
    hot = jnp.asarray((buckets[:, None] == np.arange(tile)[None, :]).astype(np.float32))

    def attention(values, keep_t):
        return attend(part, content_input, query_input, rows, hot, *values, keep_t)

    own = attention(own_attention, True)
    streams_t = own[7]
    sent = gate(*far_attention, out_weight, up_weight, down_weight)
    far_attention = sent[:4]
    out_far, up_far, down_far = (far_of(value) for value in sent[4:])
    saved = [own[:7], attention(far_attention, False)]
    out_w, up_w, down_w = (out_weight, out_far), (up_weight, up_far), (down_weight, down_far)
    bundles = (own_bundle, far_attention[0])
    attention_w = [own_attention[1:], far_attention[1:]]
    o = (saved[0][3], saved[1][3])
    normed, first, second, inv, final_c, final_q, sums_two, dwd0, dwd1, low0, low1, dbu0, dbu1 = feed(
        part, o, out_w, content_input, query_input, out_bias, first_gain, first_shift, up_w, bundles, down_w,
        down_bias, second_gain, second_shift, content_upstream, query_upstream,
    )
    far_d = far_of(dwd1)
    index = lax.axis_index("dp").astype(jnp.int32).reshape(1)
    units = dwd0.shape[1]
    cut = units * 3 // 4
    width = query_weight.shape[1]
    both = lambda own, far, low, high: [(own, low, high), (far, low, high)]

    def leave(parcels, after, packed=None, got=()):
        sents = post(index, parcels, packed, got)
        after, *sents = gate(after, *sents)
        for parcel, sent in zip(parcels, sents):
            parcel.go(sent)
        return (after, sents[-1]) if packed is not None else after

    def arrive(parcels, after):
        after, *came = gate(after, *[parcel.coming for parcel in parcels])
        return after, [parcel.land(one) for parcel, one in zip(parcels, came)]

    dwu1, partial = up_back(first, low1, up_w[1])
    chain_x = Chain([both(dwd0, far_d, 0, units)], order((0,), (1,), (2,)))
    first_x = departures([chain_x])
    partial, _ = gate(partial, far_d)
    partial, dwu1 = leave(first_x, (partial, dwu1))
    far_u = far_of(dwu1)
    dwu0, residual, al, sums_one, dwo0, dwo1 = up_back_last(first, low0, up_w[0], first_gain, inv, normed, second, partial, o)
    far_o = far_of(dwo1)
    al, far_u, far_o = gate(al, far_u, far_o)
    chain_y = Chain([both(dwu0, far_u, 0, cut)], order((1,), (0,), (2,)))
    chain_z = Chain([both(dwu0, far_u, cut, units), both(dwo0, far_o, 0, width)], order((2,), (3,), (0, 1)))
    first_y, first_z = departures([chain_y]), departures([chain_z])
    al = leave(first_y + first_z, al)

    def attention_back(s, from_pair, pairs, al):
        q, k, v, _, ot, e, linv = saved[s]
        return attend_back(from_pair, pairs, al, out_w[s], ot, q, k, v, e, linv, streams_t, hot)

    pairs = width // tile
    late = 1
    early = pairs - late
    split, side_width = early * tile, late * tile
    other = attention_back(1, 0, pairs, al)
    al, _ = arrive(first_x + first_y + first_z, gate(al, other[0])[0])
    second_x, second_y, second_z = (departures([chain]) for chain in (chain_x, chain_y, chain_z))
    al = leave(second_y + second_x + second_z, al)
    dw_other, al = gate(other[0], al)
    far = far_of(dw_other)
    own_early = attention_back(0, 0, early, al)
    al, far, dw_early = gate(al, far, own_early[0])
    al, _ = arrive(second_x + second_y, al)
    triple = 3 * tile
    of_pair = lambda n: (n * triple, (n + 1) * triple)
    chain_a = Chain([[(dw_early, *of_pair(n)), (far, *of_pair(n))] for n in range(early)], order((0, 1), (2, 3)))
    first_a, third = departures([chain_a]), departures([chain_x, chain_y])
    al = leave(first_a + third, al)
    own_late = attention_back(0, early, late, al)
    packed = pack(part, sums_one, sums_two, dbu0, dbu1, [own_early[1], own_late[1], other[1]])
    dw_late = own_late[0]
    chain_b = Chain([[(dw_late, *of_pair(n)), (far, *of_pair(early + n))] for n in range(late)], order((0, 1), (2, 3)))
    residual, _ = arrive(second_z + third, residual)
    fourth = departures([chain_x, chain_y])
    parcels = departures([chain_b, chain_z], True)
    residual, packed = leave(parcels + fourth, residual, packed)
    content_grad, query_grad = inputs_back(
        residual,
        [
            (own_early[2:5], attention_w[0], 0, split),
            (own_late[2:5], attention_w[0], early // late, side_width),
            (other[2:5], attention_w[1], 0, split + side_width),
        ],
    )
    content_grad, _ = arrive(first_a, content_grad)
    content_grad, got = arrive(parcels, content_grad)
    chains = [chain_a, chain_b]
    wide_out = None
    while chain_a.order:
        parcels = departures(chains, True)
        content_grad, packed = leave(parcels, content_grad, packed, got)
        if wide_out is None:
            content_grad, _ = arrive(fourth, content_grad)
        if not chain_x.order and wide_out is None:
            wide_out = finish_wide(index, wide_groups(chain_x, chain_y, chain_z), chain_a.block)
            content_grad, *wide_out = gate(content_grad, *wide_out)
        content_grad, got = arrive(parcels, content_grad)
        chains = [chain_a, chain_b, chain_x, chain_y, chain_z]
    if wide_out is None:
        wide_out = finish_wide(index, wide_groups(chain_x, chain_y, chain_z), chain_a.block)
    packed = join_small(packed, halves_of(got, packed.shape[0]))
    parts = chain_a.parts + chain_b.parts
    out = finish(index, packed, far_of(packed), parts, chain_a.block, 2 * units, bias_table.shape[0], 2 * heads)
    return (
        final_c,
        final_q,
        content_grad,
        query_grad,
        *out[10:13],
        wide_out[0].T,
        wide_out[1],
        wide_out[2].T,
        out[6],
        out[7],
        out[2],
        out[0],
        out[1],
        out[8],
        out[5],
        out[3],
        out[4],
        out[9].T,
    )


def solution(mesh):
    placed = (
        P("dp", None),
        P("dp", None),
        P("dp", None),
        P("dp", None),
        P("dp", None),
        P(None, "tensor"),
        P("tensor"),
        P(None, "tensor"),
        P(None, "tensor"),
        P("tensor"),
        P("tensor", None),
        P(),
        P(),
        P(),
        P(None, "tensor"),
        P("tensor"),
        P("tensor", None),
        P(),
        P(),
        P(),
        P(None, "tensor"),
        P(("dp", "tensor"), None),
        P(("dp", "tensor"), None),
    )
    rows_out = P(("dp", "tensor"), None)
    return jax.shard_map(
        local,
        mesh=mesh,
        in_specs=placed,
        out_specs=(
            rows_out,
            rows_out,
            rows_out,
            rows_out,
            P("dp", "tensor"),
            P("dp", "tensor"),
            P("dp", "tensor"),
            P("tensor", "dp"),
            P("dp", "tensor"),
            P("tensor", "dp"),
        )
        + (P(),) * 10,
        check_vma=False,
    )
```

```python
import math

import jax
import jax.numpy as jnp
import numpy as np
from jax import lax
from jax.experimental import pallas as pl
from jax.experimental.pallas import tpu as pltpu
from jax.sharding import PartitionSpec as P

norm_eps = 1e-05
big_negative = -1e30
root_half = 0.7071067811865476
root_two_pi_inv = 0.3989422804014327
bf16 = jnp.bfloat16
f32 = jnp.float32

tile = 128
reach = 2
span = (2 * reach + 1) * tile
wide = span + tile
chunk = 512
side = 256
block = 64
strip = 128
repeat = 4
TN = (((0,), (0,)), ((), ()))
NT = (((1,), (1,)), ((), ()))
NN = (((1,), (0,)), ((), ()))
light = pl.CostEstimate(flops=1_000_000, bytes_accessed=1_000_000, transcendentals=0)


def dot(left, right, dims=NN):
    return lax.dot_general(left, right, dims, preferred_element_type=f32)


def bucket_of(offset):
    distance = np.abs(offset)
    limits = 8.0 * 2.0 ** (np.arange(1, 8) / 2.0)
    counted = (distance[..., None] >= limits).sum(axis=-1)
    bucket = np.where(distance < 8, distance, 8 + counted)
    return (np.minimum(bucket, 15) + 16 * (offset < 0)).astype(np.int32)


def band_buckets():
    place = np.arange(wide)
    return bucket_of(np.where(place < span, place, place - wide) - reach * tile)


def key_tiles(b, tiles):
    return list(range(max(0, b - reach), min(tiles - 1, b + reach) + 1))


def whole(value):
    return pl.BlockSpec(value.shape, lambda *_: (0,) * len(value.shape))


def once(value):
    return pl.BlockSpec(value.shape, lambda *_: (0,) * len(value.shape), pipeline_mode=pl.Buffered(1))


def params(mebibytes):
    return pltpu.CompilerParams(vmem_limit_bytes=mebibytes * 1024 * 1024)


table_at = 8


def bundle_kernel(bq_ref, bv_ref, bu_ref, table_ref, out_ref):
    model = out_ref.shape[1]
    out_ref[...] = jnp.zeros_like(out_ref)
    out_ref[0:1, :] = jnp.concatenate([bq_ref[...].reshape(1, -1), bv_ref[...].reshape(1, -1)], axis=1)
    up = bu_ref[...].reshape(1, -1)
    for n in range(up.shape[1] // model):
        out_ref[1 + n : 2 + n, :] = up[:, n * model : (n + 1) * model]
    out_ref[table_at : table_at + table_ref.shape[0], : table_ref.shape[1]] = table_ref[...]


def bundle(bq, bv, bu, table):
    out_shape = jax.ShapeDtypeStruct((2 * table_at, 2 * bq.shape[0]), f32)
    return pl.pallas_call(bundle_kernel, out_shape=out_shape, compiler_params=params(60), name="bundle")(bq, bv, bu, table)


def attend_kernel(
    part, content_ref, query_ref, seg_ref, order_ref, flag_ref, hot_ref, bundle_ref, wq_ref, wk_ref, wv_ref,
    q_ref, k_ref, v_ref, o_ref, ot_ref, e_ref, linv_ref, *rest,
):
    mask_ref, bias_ref, band_ref, score_ref = rest[-4:]
    ahead = score_ref.shape[0]
    row_len = k_ref.shape[0]
    tiles = row_len // tile
    p = pl.program_id(0)

    @pl.when(p == 0)
    def _():
        row = pl.ds(part[0], 1)
        seg = seg_ref[row, :].astype(f32)
        order = order_ref[row, :].astype(f32)
        flag = flag_ref[row, :]
        at = lax.broadcasted_iota(jnp.int32, (1, row_len), 1)
        first = (seg != pltpu.roll(seg, 1, 1)) | (at == 0)
        key_content = jnp.where(flag == 0, -1.0, order)
        key_query = jnp.where(first, -1.0, key_content)

        def as_column(row):
            return jnp.transpose(jnp.broadcast_to(row, (tile, row_len)))

        seg_col, content_col, query_col = as_column(seg), as_column(key_content), as_column(key_query)
        for b in range(tiles):
            here = slice(b * tile, (b + 1) * tile)
            same = seg_col == seg[:, here]
            mask_ref[b, :, :tile] = jnp.where(same & (content_col <= order[:, here]), 0.0, big_negative)
            mask_ref[b, :, tile:] = jnp.where(same & (query_col < order[:, here]), 0.0, big_negative)
        width = bundle_ref.shape[1] // 2
        for n in range(2):
            for j in range(width // tile):
                at = n * width + j * tile
                bias_ref[8 * n + j : 8 * n + j + 1, :] = bundle_ref[0:1, at : at + tile]
        band_ref[...] = lax.dot_general(
            bundle_ref[table_at:, :tile], hot_ref[...], NT, precision=lax.Precision.HIGHEST, preferred_element_type=f32
        )
        if len(rest) == 5:
            for b in range(tiles):
                here = slice(b * tile, (b + 1) * tile)
                there = slice(row_len + b * tile, row_len + (b + 1) * tile)
                rest[0][:, here] = jnp.transpose(content_ref[here, :].astype(f32)).astype(bf16)
                rest[0][:, there] = jnp.transpose(query_ref[here, :].astype(f32)).astype(bf16)

    lane = lax.broadcasted_iota(jnp.int32, (1, tile), 1)
    half = tile // 2
    bq, bv = bias_ref[pl.ds(p, 1), :], bias_ref[pl.ds(p + 8, 1), :]
    q_ref[:row_len, :] = (dot(content_ref[...], wq_ref[...]) + bq).astype(bf16)
    q_ref[row_len:, :] = (dot(query_ref[...], wq_ref[...]) + bq).astype(bf16)
    kv = dot(content_ref[...], jnp.concatenate([wk_ref[...], wv_ref[...]], axis=1))
    k_ref[...] = kv[:, :tile].astype(bf16)
    v_ref[...] = (kv[:, tile:] + bv).astype(bf16)
    v_t = jnp.transpose(v_ref[...].astype(f32)).astype(bf16)
    keys = k_ref[...].astype(f32) * 0.125
    parts = [[None, None] for _ in range(tiles)]
    heads_in, bands = [], []
    for h in range(2):
        in_head = (lane >= h * half) & (lane < (h + 1) * half)
        heads_in.append(jnp.where(in_head, keys, 0.0).astype(bf16))
        band_row = band_ref[pl.ds(2 * p + h, 1), :]
        bands.append(pltpu.roll(jnp.broadcast_to(band_row, (tile, wide)), 0, 1, stride=1, stride_axis=0))
    turns = [(h, b) for b in range(tiles) for h in range(2)]

    def score(turn):
        h, b = turns[turn]
        q_tile = jnp.concatenate(
            [q_ref[b * tile : (b + 1) * tile, :], q_ref[row_len + b * tile : row_len + (b + 1) * tile, :]], axis=0
        )
        top = None
        for kb in key_tiles(b, tiles):
            d = b - kb + reach
            rows = slice(kb * tile, (kb + 1) * tile)
            bias = bands[h][:, d * tile : (d + 1) * tile]
            s = dot(heads_in[h][rows, :], q_tile, NT)
            s = s + jnp.concatenate([bias, bias], axis=1) + mask_ref[b, rows, :]
            score_ref[turn % ahead, rows, :] = s
            one_top = jnp.max(s, axis=0, keepdims=True)
            top = one_top if top is None else jnp.maximum(top, one_top)
        return top

    def weigh(turn, top):
        h, b = turns[turn]
        near = key_tiles(b, tiles)
        total = None
        weights = []
        for kb in near:
            rows = slice(kb * tile, (kb + 1) * tile)
            e = jnp.exp(score_ref[turn % ahead, rows, :] - top)
            one_total = jnp.sum(e, axis=0, keepdims=True)
            total = one_total if total is None else total + one_total
            e = e.astype(bf16)
            e_ref[0, h, b, rows, :] = e
            weights.append(e)
        inverse = 1.0 / total
        linv_ref[0, h * tiles + b : h * tiles + b + 1, :] = inverse
        mixed = dot(
            v_t[h * half : (h + 1) * half, near[0] * tile : (near[-1] + 1) * tile], jnp.concatenate(weights, axis=0)
        )
        parts[b][h] = mixed * inverse

    tops = [score(turn) for turn in range(ahead - 1)]
    for turn in range(len(turns)):
        if turn + ahead - 1 < len(turns):
            tops.append(score(turn + ahead - 1))
        weigh(turn, tops[turn])
    for b in range(tiles):
        both = jnp.concatenate(parts[b], axis=0)
        both_t = jnp.transpose(both).astype(bf16)
        both = both.astype(bf16)
        here = slice(b * tile, (b + 1) * tile)
        there = slice(row_len + b * tile, row_len + (b + 1) * tile)
        o_ref[here, :] = both_t[:tile]
        o_ref[there, :] = both_t[tile:]
        ot_ref[:, here] = both[:, :tile]
        ot_ref[:, there] = both[:, tile:]


def attend(part, content, query, rows, hot, bundled, wq, wk, wv, keep_t):
    row_len = rows[0].shape[1]
    tokens = 2 * row_len
    model, width = wq.shape
    pairs = width // tile
    tiles = row_len // tile
    own = lambda value: pl.BlockSpec((row_len, value.shape[1]), lambda p, part: (part[0], 0))
    cols = lambda n: pl.BlockSpec((n, tile), lambda p, part: (0, p))
    out = lambda *shape: jax.ShapeDtypeStruct(shape, bf16)
    out_specs = [
        cols(tokens),
        cols(row_len),
        cols(row_len),
        cols(tokens),
        pl.BlockSpec((tile, tokens), lambda p, part: (p, 0)),
        pl.BlockSpec((1, 2, tiles, row_len, 2 * tile), lambda p, part: (p, 0, 0, 0, 0)),
        pl.BlockSpec((1, 2 * tiles, 2 * tile), lambda p, part: (p, 0, 0)),
    ]
    out_shape = [
        out(tokens, width),
        out(row_len, width),
        out(row_len, width),
        out(tokens, width),
        out(width, tokens),
        out(pairs, 2, tiles, row_len, 2 * tile),
        jax.ShapeDtypeStruct((pairs, 2 * tiles, 2 * tile), f32),
    ]
    if keep_t:
        out_specs.append(pl.BlockSpec((model, tokens), lambda p, part: (0, 0)))
        out_shape.append(out(model, tokens))
    return pl.pallas_call(
        attend_kernel,
        grid_spec=pltpu.PrefetchScalarGridSpec(
            num_scalar_prefetch=1,
            grid=(pairs,),
            in_specs=[own(content), own(query)]
            + [whole(row) for row in rows]
            + [once(hot), once(bundled)]
            + [cols(model)] * 3,
            out_specs=out_specs,
            scratch_shapes=[pltpu.VMEM((tiles, row_len, 2 * tile), f32), pltpu.VMEM((16, tile), f32), pltpu.VMEM((8, wide), f32), pltpu.VMEM((4, row_len, 2 * tile), f32)],
        ),
        out_shape=out_shape,
        compiler_params=params(60),
        cost_estimate=light,
        name="attend",
    )(part, content, query, *rows, hot, bundled, wq, wk, wv)


def attend_back_kernel(
    al_ref, wo_ref, ot_ref, q_ref, k_ref, v_ref, e_ref, linv_ref, xt_ref, hot_ref,
    dw_ref, small_ref, dq_ref, dk_ref, dv_ref, dk_acc, dv_acc, g_acc, dp_ref, ds_ref,
):
    ahead = dp_ref.shape[0]
    row_len = k_ref.shape[0]
    tiles = row_len // tile
    half = tile // 2
    p = pl.program_id(0)
    lane = lax.broadcasted_iota(jnp.int32, (1, tile), 1)
    k_t = jnp.transpose(k_ref[...].astype(f32)).astype(bf16)
    do_all = dot(wo_ref[...], al_ref[...], NT).astype(bf16).astype(f32)
    dk_acc[...] = jnp.zeros_like(dk_acc)
    dv_acc[...] = jnp.zeros_like(dv_acc)
    g_acc[...] = jnp.zeros_like(g_acc)
    turns = [(h, b) for b in range(tiles) for h in range(2)]
    deltas, do_heads, q_heads = {}, {}, {}

    def places(b):
        return slice(b * tile, (b + 1) * tile), slice(row_len + b * tile, row_len + (b + 1) * tile)

    def spread(turn):
        h, b = turns[turn]
        here, there = places(b)
        mine = slice(h * half, (h + 1) * half)
        inverse = linv_ref[0, h * tiles + b : h * tiles + b + 1, :]
        do_t = jnp.concatenate([do_all[mine, here], do_all[mine, there]], axis=1)
        o_t = jnp.concatenate([ot_ref[mine, here], ot_ref[mine, there]], axis=1).astype(f32)
        deltas[turn] = jnp.sum(do_t * o_t, axis=0, keepdims=True) * inverse
        scaled = do_t * inverse
        blank = jnp.zeros_like(scaled)
        do_heads[turn] = jnp.concatenate([scaled, blank] if h == 0 else [blank, scaled], axis=0).astype(bf16)
        q_tile = jnp.concatenate([q_ref[here, :], q_ref[there, :]], axis=0)
        in_head = (lane >= h * half) & (lane < (h + 1) * half)
        q_heads[turn] = jnp.where(in_head, q_tile.astype(f32), 0.0).astype(bf16)
        for kb in key_tiles(b, tiles):
            rows = slice(kb * tile, (kb + 1) * tile)
            dp_ref[turn % ahead, rows, :] = dot(v_ref[rows, :], do_heads[turn])

    def combine(turn):
        h, b = turns[turn]
        for kb in key_tiles(b, tiles):
            d = b - kb + reach
            rows = slice(kb * tile, (kb + 1) * tile)
            ds = e_ref[0, h, b, rows, :].astype(f32) * (dp_ref[turn % ahead, rows, :] - deltas[turn])
            g_acc[h, :, d * tile : (d + 1) * tile] += ds[:, :tile] + ds[:, tile:]
            ds_ref[b % 2, h, rows, :] = ds.astype(bf16)

    def gather(b):
        here, there = places(b)
        near = key_tiles(b, tiles)
        keys = slice(near[0] * tile, (near[-1] + 1) * tile)
        two = (2 * b, 2 * b + 1)
        dv_acc[keys, :] += dot(
            jnp.concatenate([e_ref[0, h, b, keys, :] for h in range(2)], axis=1),
            jnp.concatenate([do_heads[turn] for turn in two], axis=1),
            NT,
        )
        dk_acc[keys, :] += dot(
            jnp.concatenate([ds_ref[b % 2, h, keys, :] for h in range(2)], axis=1),
            jnp.concatenate([q_heads[turn] for turn in two], axis=0),
        )
        dq_t = [dot(k_t[h * half : (h + 1) * half, keys], ds_ref[b % 2, h, keys, :]) for h in range(2)]
        dq = (jnp.transpose(jnp.concatenate(dq_t, axis=0)) * 0.125).astype(bf16)
        dq_ref[here, :] = dq[:tile]
        dq_ref[there, :] = dq[tile:]

    for turn in range(ahead - 1):
        spread(turn)
    for turn in range(len(turns)):
        if turn + ahead - 1 < len(turns):
            spread(turn + ahead - 1)
        combine(turn)
        if turn % 2 and turn >= 3:
            gather(turn // 2 - 1)
    gather(tiles - 1)
    dk = (dk_acc[...] * 0.125).astype(bf16)
    dv = dv_acc[...].astype(bf16)
    dq = dq_ref[...]
    dk_ref[...] = dk
    dv_ref[...] = dv
    dw_ref[:, :tile] = dot(xt_ref[...], dq).astype(bf16)
    dw_ref[:, tile:] = dot(xt_ref[:, :row_len], jnp.concatenate([dk, dv], axis=1)).astype(bf16)
    row = lax.broadcasted_iota(jnp.int32, (8, wide), 0)
    small_ref[0, 0:1, :] = jnp.sum(dq.astype(f32), axis=0, keepdims=True)
    small_ref[0, 1:2, :] = jnp.sum(dv.astype(f32), axis=0, keepdims=True)
    for h in range(2):
        folds = [g_acc[h, a : a + 8, :] for a in range(0, tile, 8)]
        step = 8
        while len(folds) > 1:
            folds = [folds[a] + pltpu.roll(folds[a + 1], wide - step, 1) for a in range(0, len(folds), 2)]
            step *= 2
        fold = folds[0]
        for bit in (1, 2, 4):
            fold = jnp.where((row & bit) != 0, pltpu.roll(fold, wide - bit, 1), fold)
        by_bucket = lax.dot_general(fold, hot_ref[...], NN, precision=lax.Precision.HIGHEST, preferred_element_type=f32)
        small_ref[0, 2 + h : 3 + h, :] = jnp.sum(by_bucket, axis=0, keepdims=True)


def attend_back(from_pair, pairs, al, wo, ot, q, k, v, e, linv, xt, hot):
    tokens, model = al.shape
    width = pairs * tile
    row_len = k.shape[0]
    tiles = row_len // tile
    cols = lambda n: pl.BlockSpec((n, tile), lambda p: (0, p + from_pair))
    rows = lambda n: pl.BlockSpec((tile, n), lambda p: (p + from_pair, 0))
    cols_out = lambda n: pl.BlockSpec((n, tile), lambda p: (0, p))
    shape = jax.ShapeDtypeStruct
    return pl.pallas_call(
        attend_back_kernel,
        grid=(pairs,),
        in_specs=[
            once(al),
            rows(model),
            rows(tokens),
            cols(tokens),
            cols(row_len),
            cols(row_len),
            pl.BlockSpec((1, 2, tiles, row_len, 2 * tile), lambda p: (p + from_pair, 0, 0, 0, 0)),
            pl.BlockSpec((1, 2 * tiles, 2 * tile), lambda p: (p + from_pair, 0, 0)),
            once(xt),
            once(hot),
        ],
        out_specs=[pl.BlockSpec((model, 3 * tile), lambda p: (0, p))]
        + [pl.BlockSpec((1, 8, tile), lambda p: (p, 0, 0)), cols_out(tokens), cols_out(row_len), cols_out(row_len)],
        out_shape=[shape((model, 3 * width), bf16)]
        + [shape((pairs, 8, tile), f32), shape((tokens, width), bf16)]
        + [shape((row_len, width), bf16)] * 2,
        scratch_shapes=[
            pltpu.VMEM((row_len, tile), f32),
            pltpu.VMEM((row_len, tile), f32),
            pltpu.VMEM((2, tile, wide), f32),
            pltpu.VMEM((3, row_len, 2 * tile), f32),
            pltpu.VMEM((2, 2, row_len, 2 * tile), bf16),
        ],
        compiler_params=params(26),
        cost_estimate=light,
        name="attend_back",
    )(al, wo, ot, q, k, v, e, linv, xt, hot)


def inputs_back_kernel(residual_ref, *refs):
    content_ref, query_ref = refs[-2:]
    row_len = content_ref.shape[0]
    content = residual_ref[:row_len, :]
    query = residual_ref[row_len:, :]
    for at in range(0, len(refs) - 2, 6):
        dq_ref, dk_ref, dv_ref, wq_ref, wk_ref, wv_ref = refs[at : at + 6]
        wq = wq_ref[...]
        content = content + dot(dq_ref[:row_len, :], wq, NT) + dot(dk_ref[...], wk_ref[...], NT) + dot(dv_ref[...], wv_ref[...], NT)
        query = query + dot(dq_ref[row_len:, :], wq, NT)
    content_ref[...] = content
    query_ref[...] = query


def inputs_back(residual, groups):
    tokens, model = residual.shape
    shape = jax.ShapeDtypeStruct((tokens // 2, model), f32)
    args = [residual]
    specs = [once(residual)]
    for grads, weights, at, width in groups:
        args += list(grads) + list(weights)
        specs += [once(one) for one in grads]
        specs += [pl.BlockSpec((model, width), lambda i, at=at: (0, at), pipeline_mode=pl.Buffered(1)) for _ in weights]
    return pl.pallas_call(
        inputs_back_kernel,
        grid=(1,),
        in_specs=specs,
        out_specs=[once(shape)] * 2,
        out_shape=[shape] * 2,
        compiler_params=params(30),
        cost_estimate=light,
        name="inputs_back",
    )(*args)


def normed_of(values):
    centre = jnp.mean(values, axis=-1, keepdims=True)
    centred = values - centre
    variance = jnp.mean(centred * centred, axis=-1, keepdims=True)
    inv_scale = lax.rsqrt(variance + norm_eps)
    return centred * inv_scale, inv_scale


def norm_back(upstream, normed, inv_scale, gain_vec):
    scaled = upstream * gain_vec
    centre = jnp.mean(scaled, axis=-1, keepdims=True)
    along_normed = jnp.mean(scaled * normed, axis=-1, keepdims=True)
    return inv_scale * (scaled - centre - normed * along_normed)


def eight(values):
    total = values[0:8]
    for i in range(8, values.shape[0], 8):
        total = total + values[i : i + 8]
    return total


def gelu_parts(u):
    bell = jnp.exp(-0.5 * (u * u))
    t = 1.0 / (1.0 + (0.3275911 * root_half) * jnp.abs(u))
    poly = 0.5307027145
    poly = poly * t - 0.7265760135
    poly = poly * t + 0.7107068705
    poly = poly * t - 0.142248368
    poly = poly * t + 0.127414796
    tail = poly * t * bell
    cdf = jnp.where(u >= 0.0, 1.0 - tail, tail)
    return u * cdf, cdf + (u * root_two_pi_inv) * bell


def feed_kernel(
    part, o0_ref, o1_ref, wo0_ref, wo1_ref, content_ref, query_ref, bo_ref, g1_ref, s1_ref, wu0_ref, wu1_ref, bu0_ref, bu1_ref,
    wd0_ref, wd1_ref, bd_ref, g2_ref, s2_ref, cu_ref, qu_ref,
    normed_out, first_out, second_out, inv_ref, fc_ref, fq_ref, sums_ref, dwd0_ref, dwd1_ref, low0_ref, low1_ref, dbu0_ref, dbu1_ref,
    normed_ref, first_ref, acc_ref, d2_ref, hidden_ref, slope_ref, bu_ref, up_ref, sems,
):
    row_len = content_ref.shape[0]
    bo, g1, s1, bd, g2, s2 = (ref[...].reshape(1, -1) for ref in (bo_ref, g1_ref, s1_ref, bd_ref, g2_ref, s2_ref))
    tokens, model = acc_ref.shape
    steps = pl.num_programs(0)
    i = pl.program_id(0)
    steps_of_half = hidden_ref.shape[0] // 2
    copies = [
        pltpu.make_async_copy(normed_ref, normed_out, sems.at[0]),
        pltpu.make_async_copy(first_ref, first_out, sems.at[1]),
        pltpu.make_async_copy(acc_ref, second_out, sems.at[2]),
    ]

    @pl.when(i == 0)
    def _():
        acc_ref[...] = dot(o0_ref[...], wo0_ref[...]) + dot(o1_ref[...], wo1_ref[...])
        for n, one_ref in enumerate((bu0_ref, bu1_ref)):
            flat = jnp.concatenate([one_ref[1 + j : 2 + j, :] for j in range(steps_of_half * chunk // model)], axis=1)
            for j in range(flat.shape[1] // chunk):
                at = n * (flat.shape[1] // chunk) + j
                bu_ref[at : at + 1, :] = flat[:, j * chunk : (j + 1) * chunk]
        for s, x_ref in enumerate((content_ref, query_ref)):

            def step(r, _, s=s, x_ref=x_ref):
                from_rows = pl.ds(pl.multiple_of(r * strip, strip), strip)
                rows = pl.ds(pl.multiple_of(s * row_len + r * strip, strip), strip)
                normed, inv = normed_of(x_ref[from_rows, :].astype(f32) + acc_ref[rows, :] + bo)
                first = normed * g1 + s1
                normed_ref[rows, :] = normed
                inv_ref[rows, :] = inv
                first_ref[rows, :] = first.astype(bf16)
                acc_ref[rows, :] = first + bd
                return 0

            lax.fori_loop(0, row_len // strip, step, 0, unroll=repeat)
        copies[1].start()

    def forward(wu_ref, wd_ref):
        bias = bu_ref[pl.ds(i, 1), :]
        splits = [slice(j, j + side) for j in range(0, chunk, side)]
        for j, cols in enumerate(splits):
            up_ref[:, cols] = dot(first_ref[...], wu_ref[:, cols]) + bias[:, cols]
        for cols in splits:
            for r in range(0, tokens, block):
                rows = slice(r, r + block)
                hidden, slope = gelu_parts(up_ref[rows, cols])
                hidden_ref[i, rows, cols] = hidden.astype(bf16)
                slope_ref[i, rows, cols] = slope.astype(bf16)
        acc_ref[...] += dot(hidden_ref[i], wd_ref[...])

    @pl.when(i < steps // 4)
    def _():
        forward(wu0_ref, wd0_ref)

    @pl.when((i >= steps // 4) & (i < steps // 2))
    def _():
        forward(wu1_ref, wd1_ref)

    @pl.when(i == steps // 2 - 1)
    def _():
        sums = (jnp.zeros((8, model), f32),) * 3
        for s, (c_ref, out_ref) in enumerate(((cu_ref, fc_ref), (qu_ref, fq_ref))):

            def step(r, sums, s=s, c_ref=c_ref, out_ref=out_ref):
                from_rows = pl.ds(pl.multiple_of(r * strip, strip), strip)
                rows = pl.ds(pl.multiple_of(s * row_len + r * strip, strip), strip)
                normed, inv = normed_of(acc_ref[rows, :])
                out_ref[from_rows, :] = (normed * g2 + s2).astype(bf16)
                c = c_ref[from_rows, :].astype(f32)
                second = norm_back(c, normed, inv, g2)
                acc_ref[rows, :] = second
                d2_ref[rows, :] = second.astype(bf16)
                return (sums[0] + eight(c * normed), sums[1] + eight(c), sums[2] + eight(second))

            sums = lax.fori_loop(0, row_len // strip, step, sums, unroll=repeat)
        for n in range(3):
            sums_ref[n : n + 1, :] = jnp.sum(sums[n], axis=0, keepdims=True)
        copies[2].start()

    def backward(wd_ref, dwd_ref, low_ref, dbu_ref):
        at = i - steps // 2
        up_ref[...] = dot(d2_ref[...], wd_ref[...], NT)
        dwd_ref[...] = dot(d2_ref[...], hidden_ref[at], TN).astype(bf16)
        total = jnp.zeros((8, chunk), f32)
        for r in range(0, tokens, block):
            rows = slice(r, r + block)
            grad = (up_ref[rows, :] * slope_ref[at, rows, :].astype(f32)).astype(bf16)
            low_ref[rows, :] = grad
            total = total + eight(grad.astype(f32))
        dbu_ref[...] = jnp.sum(total, axis=0, keepdims=True)

    @pl.when((i >= steps // 2) & (i < steps * 3 // 4))
    def _():
        backward(wd0_ref, dwd0_ref, low0_ref, dbu0_ref)

    @pl.when(i >= steps * 3 // 4)
    def _():
        backward(wd1_ref, dwd1_ref, low1_ref, dbu1_ref)

    @pl.when(i == 1)
    def _():
        copies[0].start()

    @pl.when(i == steps - 1)
    def _():
        for copy in copies:
            copy.wait()


def feed(part, o, wo, content, query, bo, g1, s1, wu, bu, wd, bd, g2, s2, cu, qu):
    tokens = o[0].shape[0]
    row_len = cu.shape[0]
    model, width = wu[0].shape
    c = width // chunk
    own = pl.BlockSpec((row_len, model), lambda i, part: (part[0], 0), pipeline_mode=pl.Buffered(1))
    up0 = lambda i: jnp.minimum(i, c - 1)
    up1 = lambda i: jnp.clip(i - c, 0, c - 1)
    down0 = lambda i: jnp.where(i < 2 * c, jnp.minimum(i, c - 1), jnp.minimum(i - 2 * c, c - 1))
    down1 = lambda i: jnp.where(i < 3 * c, jnp.clip(i - c, 0, c - 1), i - 3 * c)
    back0 = lambda i: jnp.clip(i - 2 * c, 0, c - 1)
    back1 = lambda i: jnp.clip(i - 3 * c, 0, c - 1)
    cols = lambda n, at: pl.BlockSpec((n, chunk), lambda i, part: (0, at(i)))
    rows = lambda at: pl.BlockSpec((chunk, model), lambda i, part: (at(i), 0))
    anywhere = pl.BlockSpec(memory_space=pl.ANY)
    shape = jax.ShapeDtypeStruct
    out_shape = [
        shape((tokens, model), f32),
        shape((tokens, model), bf16),
        shape((tokens, model), f32),
        shape((tokens, 1), f32),
        shape((row_len, model), bf16),
        shape((row_len, model), bf16),
        shape((8, model), f32),
    ]
    out_shape += [shape((model, width), bf16)] * 2 + [shape((tokens, width), bf16)] * 2 + [shape((1, width), f32)] * 2
    out_specs = [anywhere] * 3 + [once(one) for one in out_shape[3:7]]
    for n in (model, tokens, 1):
        out_specs += [cols(n, back0), cols(n, back1)]
    return pl.pallas_call(
        feed_kernel,
        grid_spec=pltpu.PrefetchScalarGridSpec(
            num_scalar_prefetch=1,
            grid=(4 * c,),
            in_specs=[once(o[0]), once(o[1]), once(wo[0]), once(wo[1]), own, own, once(bo), once(g1), once(s1)]
            + [cols(model, up0), cols(model, up1), once(bu[0]), once(bu[1]), rows(down0), rows(down1)]
            + [once(bd), once(g2), once(s2), once(cu), once(qu)],
            out_specs=out_specs,
            scratch_shapes=[
                pltpu.VMEM((tokens, model), f32),
                pltpu.VMEM((tokens, model), bf16),
                pltpu.VMEM((tokens, model), f32),
                pltpu.VMEM((tokens, model), bf16),
                pltpu.VMEM((2 * c, tokens, chunk), bf16),
                pltpu.VMEM((2 * c, tokens, chunk), bf16),
                pltpu.VMEM((8, chunk), f32),
                pltpu.VMEM((tokens, chunk), f32),
                pltpu.SemaphoreType.DMA((3,)),
            ],
        ),
        out_shape=out_shape,
        compiler_params=params(60),
        cost_estimate=light,
        name="feed",
    )(part, o[0], o[1], wo[0], wo[1], content, query, bo, g1, s1, wu[0], wu[1], bu[0], bu[1], wd[0], wd[1], bd, g2, s2, cu, qu)


def up_units(first_ref, low_ref, wu_ref, dwu_ref, acc_ref):
    @pl.when(pl.program_id(0) == 0)
    def _():
        acc_ref[...] = jnp.zeros_like(acc_ref)

    dwu_ref[...] = dot(first_ref[...], low_ref[...], TN).astype(bf16)
    acc_ref[...] += dot(low_ref[...], wu_ref[...], NT)


def up_back(first, low, wu):
    tokens, width = low.shape
    model = first.shape[1]
    cols = lambda n: pl.BlockSpec((n, chunk), lambda i: (0, i))
    acc = jax.ShapeDtypeStruct((tokens, model), f32)
    return pl.pallas_call(
        up_units,
        grid=(width // chunk,),
        in_specs=[once(first), cols(tokens), cols(model)],
        out_specs=[cols(model), once(acc)],
        out_shape=[jax.ShapeDtypeStruct((model, width), bf16), acc],
        compiler_params=params(60),
        cost_estimate=light,
        name="up_back",
    )(first, low, wu)


def up_back_last_kernel(
    first_ref, low_ref, wu_ref, g1_ref, inv_ref, normed_in, second_in, part_in, o0_in, o1_in,
    dwu_ref, residual_ref, al_ref, sums_ref, dwo0_ref, dwo1_ref,
    acc_ref, normed_ref, second_ref, part_ref, o0_ref, o1_ref, sems,
):
    tokens, model = acc_ref.shape
    i = pl.program_id(0)
    pairs = ((normed_in, normed_ref), (second_in, second_ref), (part_in, part_ref), (o0_in, o0_ref), (o1_in, o1_ref))
    copies = [pltpu.make_async_copy(here, there, sems.at[n]) for n, (here, there) in enumerate(pairs)]

    @pl.when(i == 0)
    def _():
        for copy in copies:
            copy.start()

    up_units(first_ref, low_ref, wu_ref, dwu_ref, acc_ref)

    @pl.when(i == pl.num_programs(0) - 1)
    def _():
        for copy in copies:
            copy.wait()
        g1 = g1_ref[...].reshape(1, -1)

        def step(r, sums):
            rows = pl.ds(pl.multiple_of(r * strip, strip), strip)
            back, normed = acc_ref[rows, :] + part_ref[rows, :] + second_ref[rows, :], normed_ref[rows, :]
            residual = norm_back(back, normed, inv_ref[rows, :], g1)
            residual_ref[rows, :] = residual
            al_ref[rows, :] = residual.astype(bf16)
            return (sums[0] + eight(back * normed), sums[1] + eight(back), sums[2] + eight(residual))

        sums = lax.fori_loop(0, tokens // strip, step, (jnp.zeros((8, model), f32),) * 3, unroll=repeat)
        for n in range(3):
            sums_ref[n : n + 1, :] = jnp.sum(sums[n], axis=0, keepdims=True)
        dwo0_ref[...] = dot(al_ref[...], o0_ref[...], TN).astype(bf16)
        dwo1_ref[...] = dot(al_ref[...], o1_ref[...], TN).astype(bf16)


def up_back_last(first, low, wu, g1, inv, normed, second, partial, o):
    tokens, width = low.shape
    model = first.shape[1]
    cols = lambda n: pl.BlockSpec((n, chunk), lambda i: (0, i))
    anywhere = pl.BlockSpec(memory_space=pl.ANY)
    shape = jax.ShapeDtypeStruct
    out_shape = [
        shape((model, width), bf16),
        shape((tokens, model), f32),
        shape((tokens, model), bf16),
        shape((8, model), f32),
        shape((model, o[0].shape[1]), bf16),
        shape((model, o[1].shape[1]), bf16),
    ]
    return pl.pallas_call(
        up_back_last_kernel,
        grid=(width // chunk,),
        in_specs=[once(first), cols(tokens), cols(model), once(g1), once(inv)] + [anywhere] * 5,
        out_specs=[cols(model)] + [once(one) for one in out_shape[1:]],
        out_shape=out_shape,
        scratch_shapes=[pltpu.VMEM((tokens, model), f32)] * 4
        + [pltpu.VMEM(o[0].shape, bf16), pltpu.VMEM(o[1].shape, bf16), pltpu.SemaphoreType.DMA((5,))],
        compiler_params=params(40),
        cost_estimate=light,
        name="up_back_last",
    )(first, low, wu, g1, inv, normed, second, partial, o[0], o[1])


def pack_kernel(part, one_ref, two_ref, dbu0_ref, dbu1_ref, *rest):
    smalls, out_ref = rest[:-1], rest[-1]
    first = part[0] == 0
    model = one_ref.shape[1]
    out_ref[...] = jnp.zeros_like(out_ref)
    out_ref[0:3, :] = one_ref[0:3, :]
    out_ref[3:6, :] = two_ref[0:3, :]
    pairs = model // tile // 2
    own = jnp.concatenate([ref[...] for ref in smalls[:-1]], axis=0)
    other = smalls[-1][...]
    for row in range(2):
        halves = [jnp.concatenate([half[n, row : row + 1, :] for n in range(pairs)], axis=1) for half in (own, other)]
        out_ref[6 + row : 7 + row, : model // 2] = jnp.where(first, halves[0], halves[1])
        out_ref[6 + row : 7 + row, model // 2 :] = jnp.where(first, halves[1], halves[0])
    tables = [
        jnp.concatenate([half[n, 2 + h : 3 + h, :] for n in range(pairs) for h in range(2)], axis=1) for half in (own, other)
    ]
    ups = [dbu0_ref[...], dbu1_ref[...]]
    for row, (a, b) in enumerate(((0, 1), (1, 0))):
        out_ref[8 + row : 9 + row, :] = jnp.where(first, tables[a], tables[b])
        up = jnp.where(first, ups[a], ups[b])
        rows = up.shape[1] // model
        for n in range(rows):
            at = 10 + row * rows + n
            out_ref[at : at + 1, :] = up[:, n * model : (n + 1) * model]


def pack(part, one, two, dbu0, dbu1, smalls):
    args = (one, two, dbu0, dbu1) + tuple(smalls)
    model = one.shape[1]
    return pl.pallas_call(
        pack_kernel,
        grid_spec=pltpu.PrefetchScalarGridSpec(
            num_scalar_prefetch=1, grid=(1,), in_specs=[whole(arg) for arg in args], out_specs=pl.BlockSpec((16, model), lambda *_: (0, 0))
        ),
        out_shape=jax.ShapeDtypeStruct((16, model), f32),
        compiler_params=params(4),
        name="pack",
    )(part, *args)


def exchange(value, axis_name, bit):
    count = lax.axis_size(axis_name)
    return lax.ppermute(value, axis_name, [(i, i ^ bit) for i in range(count)])


class Term:
    def __init__(self, pieces, left):
        self.pieces, self.left = pieces, left

    def places(self, flips, free):
        weight = {one: 1 << (len(self.left) - 1 - n) for n, one in enumerate(self.left)}
        own = {one: -w if one in flips else w for one, w in weight.items() if one not in free}
        start = sum(weight[one] for one in flips)
        for n in range(1 << len(free)):
            yield start + sum(weight[one] for m, one in enumerate(free) if n >> (len(free) - 1 - m) & 1), own


class Chain:
    def __init__(self, parts, order):
        bits = sum(len(step) for step in order)
        self.block = parts[0][0][0].shape[0] >> bits
        self.left = tuple(range(bits - 1, -1, -1))
        self.order = list(order)
        self.parts = [[Term([(array, 0, low, high - low)], self.left) for array, low, high in terms] for terms in parts]

    def step(self):
        bits = self.order.pop(0)
        self.left = tuple(one for one in self.left if one not in bits)
        return bits


def departures(chains, small=False):
    (bits,) = {chain.step() for chain in chains}
    before = [list(terms) for chain in chains for terms in chain.parts]
    masks = range(1, 1 << len(bits))
    return [Parcel(chains, before, [one for n, one in enumerate(bits) if mask >> n & 1], small) for mask in masks]


class Parcel:
    def __init__(self, chains, before, flips, small):
        self.chains, self.flips, self.small = chains, flips, small
        self.block = chains[0].block
        self.parts = list(zip(before, [chain.left for chain in chains for _ in chain.parts]))
        widths = [sum(piece[3] for piece in terms[0].pieces) for terms, _ in self.parts]
        self.width = math.gcd(*widths)
        self.spots, self.rows = [], 0
        for (_, left), n in zip(self.parts, widths):
            spots = []
            for at in range(0, n, self.width):
                spots.append((self.rows, at))
                self.rows += self.block << len(left)
            self.spots.append(spots)

    def go(self, sent):
        self.coming = exchange(sent, "dp", sum(1 << one for one in self.flips))

    def land(self, coming):
        spots = iter(self.spots)
        for chain in self.chains:
            for terms in chain.parts:
                terms.append(Term([(coming, row, 0, self.width) for row, _ in next(spots)], chain.left))
        return (coming, self.rows) if self.small else None


def read_plain(terms, flips, free, block):
    index = lax.axis_index("dp")
    total = 0.0
    for term in terms:
        rows = block << len(term.left)
        value = jnp.concatenate([array[row : row + rows, col : col + n] for array, row, col, n in term.pieces], axis=1)
        value = value.reshape((2,) * len(term.left) + (block, value.shape[1]))
        for axis, one in reversed(list(enumerate(term.left))):
            if one not in free:
                mine = (index >> one) & 1
                value = lax.dynamic_index_in_dim(value, 1 - mine if one in flips else mine, axis, keepdims=False)
        total = total + value.reshape(block << len(free), value.shape[-1]).astype(f32)
    return total


class Reader:
    def __init__(self, block):
        self.block, self.arrays, self.copies, self.counts = block, [], [], {}

    def read(self, terms, flips, free):
        blocks = [[] for _ in range(1 << len(free))]
        for term in terms:
            for n, (at, own) in enumerate(term.places(flips, free)):
                slots = []
                for array, row, col, width in term.pieces:
                    known = [m for m, one in enumerate(self.arrays) if one is array]
                    if not known:
                        known = [len(self.arrays)]
                        self.arrays.append(array)
                    slot = self.counts.get((width, array.dtype), 0)
                    self.counts[(width, array.dtype)] = slot + 1
                    self.copies.append((known[0], row + at * self.block, own, col, width, array.dtype, slot))
                    slots.append((width, array.dtype, slot))
                blocks[n].append(slots)
        return blocks

    def scratch(self):
        kinds = list(self.counts)
        return [pltpu.VMEM((self.counts[kind], self.block, kind[0]), kind[1]) for kind in kinds] + [
            pltpu.SemaphoreType.DMA((len(self.copies),))
        ]

    def start(self, index, array_refs, scratch):
        buffers = dict(zip(self.counts, scratch))
        made = []
        for n, (array, row, own, col, width, dtype, slot) in enumerate(self.copies):
            at = row + self.block * sum(((index >> one) & 1) * w for one, w in own.items())
            rows = pl.ds(pl.multiple_of(at, 16), self.block)
            copy = pltpu.make_async_copy(array_refs[array].at[rows, col : col + width], buffers[(width, dtype)].at[slot], scratch[-1].at[n])
            copy.start()
            made.append(copy)
        return buffers, made

    @staticmethod
    def add(buffers, terms):
        total = None
        for slots in terms:
            value = [buffers[(width, dtype)][slot].astype(f32) for width, dtype, slot in slots]
            value = value[0] if len(value) == 1 else jnp.concatenate(value, axis=1)
            total = value if total is None else total + value
        return total


def halves_of(got, rows):
    return [(coming[at : at + rows], coming[at + rows : at + 2 * rows]) for coming, at in got]


def join_small(packed, got):
    wide = [jnp.concatenate(one, axis=1).astype(f32) for one in got]
    if len(wide) == 3:
        return (packed + wide[0]) + (wide[1] + wide[2])
    return packed + wide[0] if wide else packed


def post(index, parcels, packed=None, got=()):
    block = parcels[0].block
    smalls = [parcel for parcel in parcels if parcel.small]
    if block % 16:
        sents = []
        if smalls:
            packed = lax.reduce_precision(join_small(packed, halves_of(got, packed.shape[0])), 8, 7)
        for parcel in parcels:
            values = []
            for (terms, left), spots in zip(parcel.parts, parcel.spots):
                value = read_plain(terms, parcel.flips, left, block).astype(bf16)
                values += [value[:, at : at + parcel.width] for _, at in spots]
            if parcel.small:
                half = packed.shape[1] // 2
                values += [packed[:, :half].astype(bf16), packed[:, half:].astype(bf16)]
            sents.append(jnp.concatenate(values, axis=0))
        return sents + ([packed] if smalls else [])
    reader = Reader(block)
    plans = [[reader.read(terms, parcel.flips, left) for terms, left in parcel.parts] for parcel in parcels]
    shapes = [jax.ShapeDtypeStruct((parcel.rows + (2 * packed.shape[0] if parcel.small else 0), parcel.width), bf16) for parcel in parcels]
    extra, extra_specs = [], []
    if smalls:
        extra = [packed] + [coming for coming, _ in got for _ in range(2)]
        shapes.append(jax.ShapeDtypeStruct(packed.shape, f32))
        extra_specs = [once(packed)] + [
            pl.BlockSpec((packed.shape[0], coming.shape[1]), lambda *_, n=at // packed.shape[0] + half: (n, 0))
            for coming, at in got
            for half in range(2)
        ]

    def kernel(index_ref, *refs):
        array_refs = refs[: len(reader.arrays)]
        extra_refs = refs[len(reader.arrays) : len(reader.arrays) + len(extra)]
        outs = refs[len(reader.arrays) + len(extra) :][: len(shapes)]
        buffers, made = reader.start(index_ref[0], array_refs, refs[len(reader.arrays) + len(extra) + len(shapes) :])
        if smalls:
            value = join_small(
                extra_refs[0][...], [(extra_refs[n][...], extra_refs[n + 1][...]) for n in range(1, len(extra), 2)]
            ).astype(bf16)
            outs[-1][...] = value.astype(f32)
            for parcel, out in zip(parcels, outs):
                if parcel.small:
                    half, rows = value.shape[1] // 2, value.shape[0]
                    at = parcel.rows
                    out[at : at + rows, :] = value[:, :half]
                    out[at + rows : at + 2 * rows, :] = value[:, half:]
        for copy in made:
            copy.wait()
        for parcel, plan, out in zip(parcels, plans, outs):
            for spots, blocks in zip(parcel.spots, plan):
                for n, terms in enumerate(blocks):
                    value = reader.add(buffers, terms).astype(bf16)
                    for row, at in spots:
                        out[row + n * block : row + (n + 1) * block, :] = value[:, at : at + parcel.width]

    return pl.pallas_call(
        kernel,
        grid_spec=pltpu.PrefetchScalarGridSpec(
            num_scalar_prefetch=1,
            grid=(1,),
            in_specs=[pl.BlockSpec(memory_space=pltpu.HBM)] * len(reader.arrays) + extra_specs,
            out_specs=[once(one) for one in shapes],
            scratch_shapes=reader.scratch(),
        ),
        out_shape=shapes,
        compiler_params=params(16),
        cost_estimate=light,
        name="post",
    )(index, *reader.arrays, *extra)


def total_of(index, name, parts, block, extra, shapes, write):
    plain = block % 16
    reader = Reader(block)
    plans = [] if plain else [reader.read(terms, (), ())[0] for terms in parts]
    arrays = [read_plain(terms, (), (), block) for terms in parts] if plain else reader.arrays

    def kernel(index_ref, *refs):
        array_refs, extra_refs = refs[: len(arrays)], refs[len(arrays) :][: len(extra)]
        outs, scratch = refs[len(arrays) + len(extra) :][: len(shapes)], refs[len(arrays) + len(extra) + len(shapes) :]
        if plain:
            sums = [ref[...] for ref in array_refs]
        else:
            buffers, made = reader.start(index_ref[0], array_refs, scratch)
            for copy in made:
                copy.wait()
            sums = [reader.add(buffers, plan) for plan in plans]
        write(sums, extra_refs, outs)

    return pl.pallas_call(
        kernel,
        grid_spec=pltpu.PrefetchScalarGridSpec(
            num_scalar_prefetch=1,
            grid=(1,),
            in_specs=[once(one) if plain else pl.BlockSpec(memory_space=pltpu.HBM) for one in arrays] + [once(one) for one in extra],
            out_specs=[once(one) for one in shapes],
            scratch_shapes=[] if plain else reader.scratch(),
        ),
        out_shape=shapes,
        compiler_params=params(8),
        cost_estimate=light,
        name=name,
    )(index, *arrays, *extra)


def finish_wide(index, groups, block):
    shapes = [jax.ShapeDtypeStruct((block, sum(sum(piece[3] for piece in terms[0].pieces) for terms in group)), f32) for group in groups]

    def write(sums, _, outs):
        for group, out in zip(groups, outs):
            out[...] = jnp.concatenate(sums[: len(group)], axis=1)
            sums = sums[len(group) :]

    return total_of(index, "finish_wide", [terms for group in groups for terms in group], block, [], shapes, write)


def finish(index, packed, far, parts, block, units, buckets, heads):
    model = packed.shape[1]
    f32_of = lambda *shape: jax.ShapeDtypeStruct(shape, f32)
    shapes = [f32_of(model)] * 8 + [f32_of(units), f32_of(heads, buckets)] + [f32_of(block, len(parts) * tile)] * 3

    def write(sums, extra_refs, outs):
        rows = extra_refs[0][...] + extra_refs[1][...]
        for n in range(8):
            outs[n][...] = rows[n : n + 1, :].reshape(model)
        up = jnp.concatenate([rows[n : n + 1, :] for n in range(10, 10 + units // model)], axis=1)
        outs[8][...] = up.reshape(units)
        heads_of = [rows[8 + half : 9 + half, n * tile : (n + 1) * tile] for half in range(2) for n in range(model // tile)]
        outs[9][...] = jnp.concatenate(heads_of, axis=0)[:heads, :buckets]
        for n in range(3):
            for pair, value in enumerate(sums):
                outs[10 + n][:, pair * tile : (pair + 1) * tile] = value[:, n * tile : (n + 1) * tile]

    return total_of(index, "finish", parts, block, [packed, far], shapes, write)


def wide_groups(x, y, z):
    return [[z.parts[1]], [y.parts[0], z.parts[0]], [x.parts[0]]]


def gate(*values):
    return lax.optimization_barrier(values)


def local(
    content_input,
    query_input,
    segment_ids,
    orders,
    predicted,
    query_weight,
    query_bias,
    key_weight,
    value_weight,
    value_bias,
    out_weight,
    out_bias,
    first_gain,
    first_shift,
    up_weight,
    up_bias,
    down_weight,
    down_bias,
    second_gain,
    second_shift,
    bias_table,
    content_upstream,
    query_upstream,
):
    tensor_index = lax.axis_index("tensor")
    bits = lax.axis_size("dp").bit_length() - 1
    part = tensor_index.astype(jnp.int32).reshape(1)
    far_of = lambda value: exchange(value, "tensor", 1)

    def order(*first):
        named = [bit for step in first for bit in step]
        return list(first) + [(bit,) for bit in range(bits) if bit not in named]

    own_bundle = bundle(query_bias, value_bias, up_bias, bias_table.T)
    own_attention = (own_bundle, query_weight, key_weight, value_weight)
    far_attention = tuple(far_of(value) for value in own_attention)
    rows = (segment_ids, orders, predicted)
    heads = bias_table.shape[1]
    buckets = band_buckets()
    hot = jnp.asarray((buckets[:, None] == np.arange(tile)[None, :]).astype(np.float32))

    def attention(values, keep_t):
        return attend(part, content_input, query_input, rows, hot, *values, keep_t)

    own = attention(own_attention, True)
    streams_t = own[7]
    sent = gate(*far_attention, out_weight, up_weight, down_weight)
    far_attention = sent[:4]
    out_far, up_far, down_far = (far_of(value) for value in sent[4:])
    saved = [own[:7], attention(far_attention, False)]
    out_w, up_w, down_w = (out_weight, out_far), (up_weight, up_far), (down_weight, down_far)
    bundles = (own_bundle, far_attention[0])
    attention_w = [own_attention[1:], far_attention[1:]]
    o = (saved[0][3], saved[1][3])
    normed, first, second, inv, final_c, final_q, sums_two, dwd0, dwd1, low0, low1, dbu0, dbu1 = feed(
        part, o, out_w, content_input, query_input, out_bias, first_gain, first_shift, up_w, bundles, down_w,
        down_bias, second_gain, second_shift, content_upstream, query_upstream,
    )
    far_d = far_of(dwd1)
    index = lax.axis_index("dp").astype(jnp.int32).reshape(1)
    units = dwd0.shape[1]
    cut = units * 3 // 4
    width = query_weight.shape[1]
    both = lambda own, far, low, high: [(own, low, high), (far, low, high)]

    def leave(parcels, after, packed=None, got=()):
        sents = post(index, parcels, packed, got)
        after, *sents = gate(after, *sents)
        for parcel, sent in zip(parcels, sents):
            parcel.go(sent)
        return (after, sents[-1]) if packed is not None else after

    def arrive(parcels, after):
        after, *came = gate(after, *[parcel.coming for parcel in parcels])
        return after, [parcel.land(one) for parcel, one in zip(parcels, came)]

    dwu1, partial = up_back(first, low1, up_w[1])
    chain_x = Chain([both(dwd0, far_d, 0, units)], order((0,), (1,), (2,)))
    first_x = departures([chain_x])
    partial, _ = gate(partial, far_d)
    partial, dwu1 = leave(first_x, (partial, dwu1))
    far_u = far_of(dwu1)
    dwu0, residual, al, sums_one, dwo0, dwo1 = up_back_last(first, low0, up_w[0], first_gain, inv, normed, second, partial, o)
    far_o = far_of(dwo1)
    al, far_u, far_o = gate(al, far_u, far_o)
    chain_y = Chain([both(dwu0, far_u, 0, cut)], order((1,), (0,), (2,)))
    chain_z = Chain([both(dwu0, far_u, cut, units), both(dwo0, far_o, 0, width)], order((2,), (3,), (0, 1)))
    first_y, first_z = departures([chain_y]), departures([chain_z])
    al = leave(first_y + first_z, al)

    def attention_back(s, from_pair, pairs, al):
        q, k, v, _, ot, e, linv = saved[s]
        return attend_back(from_pair, pairs, al, out_w[s], ot, q, k, v, e, linv, streams_t, hot)

    pairs = width // tile
    late = 1
    early = pairs - late
    split, side_width = early * tile, late * tile
    other = attention_back(1, 0, pairs, al)
    al, _ = arrive(first_x + first_y + first_z, gate(al, other[0])[0])
    second_x, second_y, second_z = (departures([chain]) for chain in (chain_x, chain_y, chain_z))
    al = leave(second_y + second_x + second_z, al)
    dw_other, al = gate(other[0], al)
    far = far_of(dw_other)
    own_early = attention_back(0, 0, early, al)
    al, far, dw_early = gate(al, far, own_early[0])
    al, _ = arrive(second_x + second_y + second_z, al)
    triple = 3 * tile
    of_pair = lambda n: (n * triple, (n + 1) * triple)
    chain_a = Chain([[(dw_early, *of_pair(n)), (far, *of_pair(n))] for n in range(early)], order((0, 1), (2, 3)))
    first_a, third = departures([chain_a]), departures([chain_x, chain_y])
    al = leave(first_a + third, al)
    own_late = attention_back(0, early, late, al)
    packed = pack(part, sums_one, sums_two, dbu0, dbu1, [own_early[1], own_late[1], other[1]])
    dw_late = own_late[0]
    chain_b = Chain([[(dw_late, *of_pair(n)), (far, *of_pair(early + n))] for n in range(late)], order((0, 1), (2, 3)))
    residual, _ = arrive(third, residual)
    fourth = departures([chain_x, chain_y])
    parcels = departures([chain_b, chain_z], True)
    residual, packed = leave(parcels + fourth, residual, packed)
    content_grad, query_grad = inputs_back(
        residual,
        [
            (own_early[2:5], attention_w[0], 0, split),
            (own_late[2:5], attention_w[0], early // late, side_width),
            (other[2:5], attention_w[1], 0, split + side_width),
        ],
    )
    content_grad, _ = arrive(first_a, content_grad)
    content_grad, got = arrive(parcels, content_grad)
    chains = [chain_a, chain_b]
    wide_out = None
    while chain_a.order:
        parcels = departures(chains, True)
        content_grad, packed = leave(parcels, content_grad, packed, got)
        if wide_out is None:
            content_grad, _ = arrive(fourth, content_grad)
        if not chain_x.order and wide_out is None:
            wide_out = finish_wide(index, wide_groups(chain_x, chain_y, chain_z), chain_a.block)
            content_grad, *wide_out = gate(content_grad, *wide_out)
        content_grad, got = arrive(parcels, content_grad)
        chains = [chain_a, chain_b, chain_x, chain_y, chain_z]
    if wide_out is None:
        wide_out = finish_wide(index, wide_groups(chain_x, chain_y, chain_z), chain_a.block)
    packed = join_small(packed, halves_of(got, packed.shape[0]))
    parts = chain_a.parts + chain_b.parts
    out = finish(index, packed, far_of(packed), parts, chain_a.block, 2 * units, bias_table.shape[0], 2 * heads)
    return (
        final_c,
        final_q,
        content_grad,
        query_grad,
        *out[10:13],
        wide_out[0].T,
        wide_out[1],
        wide_out[2].T,
        out[6],
        out[7],
        out[2],
        out[0],
        out[1],
        out[8],
        out[5],
        out[3],
        out[4],
        out[9].T,
    )


def solution(mesh):
    placed = (
        P("dp", None),
        P("dp", None),
        P("dp", None),
        P("dp", None),
        P("dp", None),
        P(None, "tensor"),
        P("tensor"),
        P(None, "tensor"),
        P(None, "tensor"),
        P("tensor"),
        P("tensor", None),
        P(),
        P(),
        P(),
        P(None, "tensor"),
        P("tensor"),
        P("tensor", None),
        P(),
        P(),
        P(),
        P(None, "tensor"),
        P(("dp", "tensor"), None),
        P(("dp", "tensor"), None),
    )
    rows_out = P(("dp", "tensor"), None)
    return jax.shard_map(
        local,
        mesh=mesh,
        in_specs=placed,
        out_specs=(
            rows_out,
            rows_out,
            rows_out,
            rows_out,
            P("dp", "tensor"),
            P("dp", "tensor"),
            P("dp", "tensor"),
            P("tensor", "dp"),
            P("dp", "tensor"),
            P("tensor", "dp"),
        )
        + (P(),) * 10,
        check_vma=False,
    )
```

```python
import math

import jax
import jax.numpy as jnp
import numpy as np
from jax import lax
from jax.experimental import pallas as pl
from jax.experimental.pallas import tpu as pltpu
from jax.sharding import PartitionSpec as P

norm_eps = 1e-05
big_negative = -1e30
root_half = 0.7071067811865476
root_two_pi_inv = 0.3989422804014327
bf16 = jnp.bfloat16
f32 = jnp.float32

tile = 128
reach = 2
span = (2 * reach + 1) * tile
wide = span + tile
chunk = 512
side = 256
block = 64
strip = 128
repeat = 4
TN = (((0,), (0,)), ((), ()))
NT = (((1,), (1,)), ((), ()))
NN = (((1,), (0,)), ((), ()))
light = pl.CostEstimate(flops=1_000_000, bytes_accessed=1_000_000, transcendentals=0)


def dot(left, right, dims=NN):
    return lax.dot_general(left, right, dims, preferred_element_type=f32)


def bucket_of(offset):
    distance = np.abs(offset)
    limits = 8.0 * 2.0 ** (np.arange(1, 8) / 2.0)
    counted = (distance[..., None] >= limits).sum(axis=-1)
    bucket = np.where(distance < 8, distance, 8 + counted)
    return (np.minimum(bucket, 15) + 16 * (offset < 0)).astype(np.int32)


def band_buckets():
    place = np.arange(wide)
    return bucket_of(np.where(place < span, place, place - wide) - reach * tile)


def key_tiles(b, tiles):
    return list(range(max(0, b - reach), min(tiles - 1, b + reach) + 1))


def whole(value):
    return pl.BlockSpec(value.shape, lambda *_: (0,) * len(value.shape))


def once(value):
    return pl.BlockSpec(value.shape, lambda *_: (0,) * len(value.shape), pipeline_mode=pl.Buffered(1))


def params(mebibytes):
    return pltpu.CompilerParams(vmem_limit_bytes=mebibytes * 1024 * 1024)


table_at = 8


def bundle_kernel(bq_ref, bv_ref, bu_ref, table_ref, out_ref):
    model = out_ref.shape[1]
    out_ref[...] = jnp.zeros_like(out_ref)
    out_ref[0:1, :] = jnp.concatenate([bq_ref[...].reshape(1, -1), bv_ref[...].reshape(1, -1)], axis=1)
    up = bu_ref[...].reshape(1, -1)
    for n in range(up.shape[1] // model):
        out_ref[1 + n : 2 + n, :] = up[:, n * model : (n + 1) * model]
    out_ref[table_at : table_at + table_ref.shape[0], : table_ref.shape[1]] = table_ref[...]


def bundle(bq, bv, bu, table):
    out_shape = jax.ShapeDtypeStruct((2 * table_at, 2 * bq.shape[0]), f32)
    return pl.pallas_call(bundle_kernel, out_shape=out_shape, compiler_params=params(60), name="bundle")(bq, bv, bu, table)


def attend_kernel(
    part, content_ref, query_ref, seg_ref, order_ref, flag_ref, hot_ref, bundle_ref, wq_ref, wk_ref, wv_ref,
    q_ref, k_ref, v_ref, o_ref, ot_ref, e_ref, linv_ref, *rest,
):
    mask_ref, bias_ref, band_ref, score_ref = rest[-4:]
    ahead = score_ref.shape[0]
    row_len = k_ref.shape[0]
    tiles = row_len // tile
    p = pl.program_id(0)

    @pl.when(p == 0)
    def _():
        row = pl.ds(part[0], 1)
        seg = seg_ref[row, :].astype(f32)
        order = order_ref[row, :].astype(f32)
        flag = flag_ref[row, :]
        at = lax.broadcasted_iota(jnp.int32, (1, row_len), 1)
        first = (seg != pltpu.roll(seg, 1, 1)) | (at == 0)
        key_content = jnp.where(flag == 0, -1.0, order)
        key_query = jnp.where(first, -1.0, key_content)

        def as_column(row):
            return jnp.transpose(jnp.broadcast_to(row, (tile, row_len)))

        seg_col, content_col, query_col = as_column(seg), as_column(key_content), as_column(key_query)
        for b in range(tiles):
            here = slice(b * tile, (b + 1) * tile)
            same = seg_col == seg[:, here]
            mask_ref[b, :, :tile] = jnp.where(same & (content_col <= order[:, here]), 0.0, big_negative)
            mask_ref[b, :, tile:] = jnp.where(same & (query_col < order[:, here]), 0.0, big_negative)
        width = bundle_ref.shape[1] // 2
        for n in range(2):
            for j in range(width // tile):
                at = n * width + j * tile
                bias_ref[8 * n + j : 8 * n + j + 1, :] = bundle_ref[0:1, at : at + tile]
        band_ref[...] = lax.dot_general(
            bundle_ref[table_at:, :tile], hot_ref[...], NT, precision=lax.Precision.HIGHEST, preferred_element_type=f32
        )
        if len(rest) == 5:
            for b in range(tiles):
                here = slice(b * tile, (b + 1) * tile)
                there = slice(row_len + b * tile, row_len + (b + 1) * tile)
                rest[0][:, here] = jnp.transpose(content_ref[here, :].astype(f32)).astype(bf16)
                rest[0][:, there] = jnp.transpose(query_ref[here, :].astype(f32)).astype(bf16)

    lane = lax.broadcasted_iota(jnp.int32, (1, tile), 1)
    half = tile // 2
    bq, bv = bias_ref[pl.ds(p, 1), :], bias_ref[pl.ds(p + 8, 1), :]
    q_ref[:row_len, :] = (dot(content_ref[...], wq_ref[...]) + bq).astype(bf16)
    q_ref[row_len:, :] = (dot(query_ref[...], wq_ref[...]) + bq).astype(bf16)
    kv = dot(content_ref[...], jnp.concatenate([wk_ref[...], wv_ref[...]], axis=1))
    k_ref[...] = kv[:, :tile].astype(bf16)
    v_ref[...] = (kv[:, tile:] + bv).astype(bf16)
    v_t = jnp.transpose(v_ref[...].astype(f32)).astype(bf16)
    keys = k_ref[...].astype(f32) * 0.125
    parts = [[None, None] for _ in range(tiles)]
    heads_in, bands = [], []
    for h in range(2):
        in_head = (lane >= h * half) & (lane < (h + 1) * half)
        heads_in.append(jnp.where(in_head, keys, 0.0).astype(bf16))
        band_row = band_ref[pl.ds(2 * p + h, 1), :]
        bands.append(pltpu.roll(jnp.broadcast_to(band_row, (tile, wide)), 0, 1, stride=1, stride_axis=0))
    turns = [(h, b) for b in range(tiles) for h in range(2)]

    def score(turn):
        h, b = turns[turn]
        q_tile = jnp.concatenate(
            [q_ref[b * tile : (b + 1) * tile, :], q_ref[row_len + b * tile : row_len + (b + 1) * tile, :]], axis=0
        )
        top = None
        for kb in key_tiles(b, tiles):
            d = b - kb + reach
            rows = slice(kb * tile, (kb + 1) * tile)
            bias = bands[h][:, d * tile : (d + 1) * tile]
            s = dot(heads_in[h][rows, :], q_tile, NT)
            s = s + jnp.concatenate([bias, bias], axis=1) + mask_ref[b, rows, :]
            score_ref[turn % ahead, rows, :] = s
            one_top = jnp.max(s, axis=0, keepdims=True)
            top = one_top if top is None else jnp.maximum(top, one_top)
        return top

    def weigh(turn, top):
        h, b = turns[turn]
        near = key_tiles(b, tiles)
        total = None
        weights = []
        for kb in near:
            rows = slice(kb * tile, (kb + 1) * tile)
            e = jnp.exp(score_ref[turn % ahead, rows, :] - top)
            one_total = jnp.sum(e, axis=0, keepdims=True)
            total = one_total if total is None else total + one_total
            e = e.astype(bf16)
            e_ref[0, h, b, rows, :] = e
            weights.append(e)
        inverse = 1.0 / total
        linv_ref[0, h * tiles + b : h * tiles + b + 1, :] = inverse
        mixed = dot(
            v_t[h * half : (h + 1) * half, near[0] * tile : (near[-1] + 1) * tile], jnp.concatenate(weights, axis=0)
        )
        parts[b][h] = mixed * inverse

    tops = [score(turn) for turn in range(ahead - 1)]
    for turn in range(len(turns)):
        if turn + ahead - 1 < len(turns):
            tops.append(score(turn + ahead - 1))
        weigh(turn, tops[turn])
    for b in range(tiles):
        both = jnp.concatenate(parts[b], axis=0)
        both_t = jnp.transpose(both).astype(bf16)
        both = both.astype(bf16)
        here = slice(b * tile, (b + 1) * tile)
        there = slice(row_len + b * tile, row_len + (b + 1) * tile)
        o_ref[here, :] = both_t[:tile]
        o_ref[there, :] = both_t[tile:]
        ot_ref[:, here] = both[:, :tile]
        ot_ref[:, there] = both[:, tile:]


def attend(part, content, query, rows, hot, bundled, wq, wk, wv, keep_t):
    row_len = rows[0].shape[1]
    tokens = 2 * row_len
    model, width = wq.shape
    pairs = width // tile
    tiles = row_len // tile
    own = lambda value: pl.BlockSpec((row_len, value.shape[1]), lambda p, part: (part[0], 0))
    cols = lambda n: pl.BlockSpec((n, tile), lambda p, part: (0, p))
    out = lambda *shape: jax.ShapeDtypeStruct(shape, bf16)
    out_specs = [
        cols(tokens),
        cols(row_len),
        cols(row_len),
        cols(tokens),
        pl.BlockSpec((tile, tokens), lambda p, part: (p, 0)),
        pl.BlockSpec((1, 2, tiles, row_len, 2 * tile), lambda p, part: (p, 0, 0, 0, 0)),
        pl.BlockSpec((1, 2 * tiles, 2 * tile), lambda p, part: (p, 0, 0)),
    ]
    out_shape = [
        out(tokens, width),
        out(row_len, width),
        out(row_len, width),
        out(tokens, width),
        out(width, tokens),
        out(pairs, 2, tiles, row_len, 2 * tile),
        jax.ShapeDtypeStruct((pairs, 2 * tiles, 2 * tile), f32),
    ]
    if keep_t:
        out_specs.append(pl.BlockSpec((model, tokens), lambda p, part: (0, 0)))
        out_shape.append(out(model, tokens))
    return pl.pallas_call(
        attend_kernel,
        grid_spec=pltpu.PrefetchScalarGridSpec(
            num_scalar_prefetch=1,
            grid=(pairs,),
            in_specs=[own(content), own(query)]
            + [whole(row) for row in rows]
            + [once(hot), once(bundled)]
            + [cols(model)] * 3,
            out_specs=out_specs,
            scratch_shapes=[pltpu.VMEM((tiles, row_len, 2 * tile), f32), pltpu.VMEM((16, tile), f32), pltpu.VMEM((8, wide), f32), pltpu.VMEM((4, row_len, 2 * tile), f32)],
        ),
        out_shape=out_shape,
        compiler_params=params(60),
        cost_estimate=light,
        name="attend",
    )(part, content, query, *rows, hot, bundled, wq, wk, wv)


def attend_back_kernel(
    al_ref, wo_ref, ot_ref, q_ref, k_ref, v_ref, e_ref, linv_ref, xt_ref, hot_ref,
    dw_ref, small_ref, dq_ref, dk_ref, dv_ref, dk_acc, dv_acc, g_acc, dp_ref, ds_ref,
):
    ahead = dp_ref.shape[0]
    row_len = k_ref.shape[0]
    tiles = row_len // tile
    half = tile // 2
    p = pl.program_id(0)
    lane = lax.broadcasted_iota(jnp.int32, (1, tile), 1)
    k_t = jnp.transpose(k_ref[...].astype(f32)).astype(bf16)
    do_all = dot(wo_ref[...], al_ref[...], NT).astype(bf16).astype(f32)
    dk_acc[...] = jnp.zeros_like(dk_acc)
    dv_acc[...] = jnp.zeros_like(dv_acc)
    g_acc[...] = jnp.zeros_like(g_acc)
    turns = [(h, b) for b in range(tiles) for h in range(2)]
    deltas, do_heads, q_heads = {}, {}, {}

    def places(b):
        return slice(b * tile, (b + 1) * tile), slice(row_len + b * tile, row_len + (b + 1) * tile)

    def spread(turn):
        h, b = turns[turn]
        here, there = places(b)
        mine = slice(h * half, (h + 1) * half)
        inverse = linv_ref[0, h * tiles + b : h * tiles + b + 1, :]
        do_t = jnp.concatenate([do_all[mine, here], do_all[mine, there]], axis=1)
        o_t = jnp.concatenate([ot_ref[mine, here], ot_ref[mine, there]], axis=1).astype(f32)
        deltas[turn] = jnp.sum(do_t * o_t, axis=0, keepdims=True) * inverse
        scaled = do_t * inverse
        blank = jnp.zeros_like(scaled)
        do_heads[turn] = jnp.concatenate([scaled, blank] if h == 0 else [blank, scaled], axis=0).astype(bf16)
        q_tile = jnp.concatenate([q_ref[here, :], q_ref[there, :]], axis=0)
        in_head = (lane >= h * half) & (lane < (h + 1) * half)
        q_heads[turn] = jnp.where(in_head, q_tile.astype(f32), 0.0).astype(bf16)
        for kb in key_tiles(b, tiles):
            rows = slice(kb * tile, (kb + 1) * tile)
            dp_ref[turn % ahead, rows, :] = dot(v_ref[rows, :], do_heads[turn])

    def combine(turn):
        h, b = turns[turn]
        for kb in key_tiles(b, tiles):
            d = b - kb + reach
            rows = slice(kb * tile, (kb + 1) * tile)
            ds = e_ref[0, h, b, rows, :].astype(f32) * (dp_ref[turn % ahead, rows, :] - deltas[turn])
            g_acc[h, :, d * tile : (d + 1) * tile] += ds[:, :tile] + ds[:, tile:]
            ds_ref[b % 2, h, rows, :] = ds.astype(bf16)

    def gather(b):
        here, there = places(b)
        near = key_tiles(b, tiles)
        keys = slice(near[0] * tile, (near[-1] + 1) * tile)
        two = (2 * b, 2 * b + 1)
        dv_acc[keys, :] += dot(
            jnp.concatenate([e_ref[0, h, b, keys, :] for h in range(2)], axis=1),
            jnp.concatenate([do_heads[turn] for turn in two], axis=1),
            NT,
        )
        dk_acc[keys, :] += dot(
            jnp.concatenate([ds_ref[b % 2, h, keys, :] for h in range(2)], axis=1),
            jnp.concatenate([q_heads[turn] for turn in two], axis=0),
        )
        dq_t = [dot(k_t[h * half : (h + 1) * half, keys], ds_ref[b % 2, h, keys, :]) for h in range(2)]
        dq = (jnp.transpose(jnp.concatenate(dq_t, axis=0)) * 0.125).astype(bf16)
        dq_ref[here, :] = dq[:tile]
        dq_ref[there, :] = dq[tile:]

    for turn in range(ahead - 1):
        spread(turn)
    for turn in range(len(turns)):
        if turn + ahead - 1 < len(turns):
            spread(turn + ahead - 1)
        combine(turn)
        if turn % 2 and turn >= 3:
            gather(turn // 2 - 1)
    gather(tiles - 1)
    dk = (dk_acc[...] * 0.125).astype(bf16)
    dv = dv_acc[...].astype(bf16)
    dq = dq_ref[...]
    dk_ref[...] = dk
    dv_ref[...] = dv
    dw_ref[:, :tile] = dot(xt_ref[...], dq).astype(bf16)
    dw_ref[:, tile:] = dot(xt_ref[:, :row_len], jnp.concatenate([dk, dv], axis=1)).astype(bf16)
    row = lax.broadcasted_iota(jnp.int32, (8, wide), 0)
    small_ref[0, 0:1, :] = jnp.sum(dq.astype(f32), axis=0, keepdims=True)
    small_ref[0, 1:2, :] = jnp.sum(dv.astype(f32), axis=0, keepdims=True)
    for h in range(2):
        folds = [g_acc[h, a : a + 8, :] for a in range(0, tile, 8)]
        step = 8
        while len(folds) > 1:
            folds = [folds[a] + pltpu.roll(folds[a + 1], wide - step, 1) for a in range(0, len(folds), 2)]
            step *= 2
        fold = folds[0]
        for bit in (1, 2, 4):
            fold = jnp.where((row & bit) != 0, pltpu.roll(fold, wide - bit, 1), fold)
        by_bucket = lax.dot_general(fold, hot_ref[...], NN, precision=lax.Precision.HIGHEST, preferred_element_type=f32)
        small_ref[0, 2 + h : 3 + h, :] = jnp.sum(by_bucket, axis=0, keepdims=True)


def attend_back(from_pair, pairs, al, wo, ot, q, k, v, e, linv, xt, hot):
    tokens, model = al.shape
    width = pairs * tile
    row_len = k.shape[0]
    tiles = row_len // tile
    cols = lambda n: pl.BlockSpec((n, tile), lambda p: (0, p + from_pair))
    rows = lambda n: pl.BlockSpec((tile, n), lambda p: (p + from_pair, 0))
    cols_out = lambda n: pl.BlockSpec((n, tile), lambda p: (0, p))
    shape = jax.ShapeDtypeStruct
    return pl.pallas_call(
        attend_back_kernel,
        grid=(pairs,),
        in_specs=[
            once(al),
            rows(model),
            rows(tokens),
            cols(tokens),
            cols(row_len),
            cols(row_len),
            pl.BlockSpec((1, 2, tiles, row_len, 2 * tile), lambda p: (p + from_pair, 0, 0, 0, 0)),
            pl.BlockSpec((1, 2 * tiles, 2 * tile), lambda p: (p + from_pair, 0, 0)),
            once(xt),
            once(hot),
        ],
        out_specs=[pl.BlockSpec((model, 3 * tile), lambda p: (0, p))]
        + [pl.BlockSpec((1, 8, tile), lambda p: (p, 0, 0)), cols_out(tokens), cols_out(row_len), cols_out(row_len)],
        out_shape=[shape((model, 3 * width), bf16)]
        + [shape((pairs, 8, tile), f32), shape((tokens, width), bf16)]
        + [shape((row_len, width), bf16)] * 2,
        scratch_shapes=[
            pltpu.VMEM((row_len, tile), f32),
            pltpu.VMEM((row_len, tile), f32),
            pltpu.VMEM((2, tile, wide), f32),
            pltpu.VMEM((3, row_len, 2 * tile), f32),
            pltpu.VMEM((2, 2, row_len, 2 * tile), bf16),
        ],
        compiler_params=params(26),
        cost_estimate=light,
        name="attend_back",
    )(al, wo, ot, q, k, v, e, linv, xt, hot)


def inputs_back_kernel(residual_ref, *refs):
    content_ref, query_ref = refs[-2:]
    row_len = content_ref.shape[0]
    content = residual_ref[:row_len, :]
    query = residual_ref[row_len:, :]
    for at in range(0, len(refs) - 2, 6):
        dq_ref, dk_ref, dv_ref, wq_ref, wk_ref, wv_ref = refs[at : at + 6]
        wq = wq_ref[...]
        content = content + dot(dq_ref[:row_len, :], wq, NT) + dot(dk_ref[...], wk_ref[...], NT) + dot(dv_ref[...], wv_ref[...], NT)
        query = query + dot(dq_ref[row_len:, :], wq, NT)
    content_ref[...] = content
    query_ref[...] = query


def inputs_back(residual, groups):
    tokens, model = residual.shape
    shape = jax.ShapeDtypeStruct((tokens // 2, model), f32)
    args = [residual]
    specs = [once(residual)]
    for grads, weights, at, width in groups:
        args += list(grads) + list(weights)
        specs += [once(one) for one in grads]
        specs += [pl.BlockSpec((model, width), lambda i, at=at: (0, at), pipeline_mode=pl.Buffered(1)) for _ in weights]
    return pl.pallas_call(
        inputs_back_kernel,
        grid=(1,),
        in_specs=specs,
        out_specs=[once(shape)] * 2,
        out_shape=[shape] * 2,
        compiler_params=params(30),
        cost_estimate=light,
        name="inputs_back",
    )(*args)


def normed_of(values):
    centre = jnp.mean(values, axis=-1, keepdims=True)
    centred = values - centre
    variance = jnp.mean(centred * centred, axis=-1, keepdims=True)
    inv_scale = lax.rsqrt(variance + norm_eps)
    return centred * inv_scale, inv_scale


def norm_back(upstream, normed, inv_scale, gain_vec):
    scaled = upstream * gain_vec
    centre = jnp.mean(scaled, axis=-1, keepdims=True)
    along_normed = jnp.mean(scaled * normed, axis=-1, keepdims=True)
    return inv_scale * (scaled - centre - normed * along_normed)


def eight(values):
    total = values[0:8]
    for i in range(8, values.shape[0], 8):
        total = total + values[i : i + 8]
    return total


def gelu_parts(u):
    bell = jnp.exp(-0.5 * (u * u))
    t = 1.0 / (1.0 + (0.3275911 * root_half) * jnp.abs(u))
    poly = 0.5307027145
    poly = poly * t - 0.7265760135
    poly = poly * t + 0.7107068705
    poly = poly * t - 0.142248368
    poly = poly * t + 0.127414796
    tail = poly * t * bell
    cdf = jnp.where(u >= 0.0, 1.0 - tail, tail)
    return u * cdf, cdf + (u * root_two_pi_inv) * bell


def feed_kernel(
    part, o0_ref, o1_ref, wo0_ref, wo1_ref, content_ref, query_ref, bo_ref, g1_ref, s1_ref, wu0_ref, wu1_ref, bu0_ref, bu1_ref,
    wd0_ref, wd1_ref, bd_ref, g2_ref, s2_ref, cu_ref, qu_ref,
    normed_out, first_out, second_out, inv_ref, fc_ref, fq_ref, sums_ref, dwd0_ref, dwd1_ref, low0_ref, low1_ref, dbu0_ref, dbu1_ref,
    normed_ref, first_ref, acc_ref, d2_ref, hidden_ref, slope_ref, bu_ref, up_ref, sems,
):
    row_len = content_ref.shape[0]
    bo, g1, s1, bd, g2, s2 = (ref[...].reshape(1, -1) for ref in (bo_ref, g1_ref, s1_ref, bd_ref, g2_ref, s2_ref))
    tokens, model = acc_ref.shape
    steps = pl.num_programs(0)
    i = pl.program_id(0)
    steps_of_half = hidden_ref.shape[0] // 2
    copies = [
        pltpu.make_async_copy(normed_ref, normed_out, sems.at[0]),
        pltpu.make_async_copy(first_ref, first_out, sems.at[1]),
        pltpu.make_async_copy(acc_ref, second_out, sems.at[2]),
    ]

    @pl.when(i == 0)
    def _():
        acc_ref[...] = dot(o0_ref[...], wo0_ref[...]) + dot(o1_ref[...], wo1_ref[...])
        for n, one_ref in enumerate((bu0_ref, bu1_ref)):
            flat = jnp.concatenate([one_ref[1 + j : 2 + j, :] for j in range(steps_of_half * chunk // model)], axis=1)
            for j in range(flat.shape[1] // chunk):
                at = n * (flat.shape[1] // chunk) + j
                bu_ref[at : at + 1, :] = flat[:, j * chunk : (j + 1) * chunk]
        for s, x_ref in enumerate((content_ref, query_ref)):

            def step(r, _, s=s, x_ref=x_ref):
                from_rows = pl.ds(pl.multiple_of(r * strip, strip), strip)
                rows = pl.ds(pl.multiple_of(s * row_len + r * strip, strip), strip)
                normed, inv = normed_of(x_ref[from_rows, :].astype(f32) + acc_ref[rows, :] + bo)
                first = normed * g1 + s1
                normed_ref[rows, :] = normed
                inv_ref[rows, :] = inv
                first_ref[rows, :] = first.astype(bf16)
                acc_ref[rows, :] = first + bd
                return 0

            lax.fori_loop(0, row_len // strip, step, 0, unroll=repeat)
        copies[1].start()

    def forward(wu_ref, wd_ref):
        bias = bu_ref[pl.ds(i, 1), :]
        splits = [slice(j, j + side) for j in range(0, chunk, side)]
        for j, cols in enumerate(splits):
            up_ref[:, cols] = dot(first_ref[...], wu_ref[:, cols]) + bias[:, cols]
        for cols in splits:
            for r in range(0, tokens, block):
                rows = slice(r, r + block)
                hidden, slope = gelu_parts(up_ref[rows, cols])
                hidden_ref[i, rows, cols] = hidden.astype(bf16)
                slope_ref[i, rows, cols] = slope.astype(bf16)
        acc_ref[...] += dot(hidden_ref[i], wd_ref[...])

    @pl.when(i < steps // 4)
    def _():
        forward(wu0_ref, wd0_ref)

    @pl.when((i >= steps // 4) & (i < steps // 2))
    def _():
        forward(wu1_ref, wd1_ref)

    @pl.when(i == steps // 2 - 1)
    def _():
        sums = (jnp.zeros((8, model), f32),) * 3
        for s, (c_ref, out_ref) in enumerate(((cu_ref, fc_ref), (qu_ref, fq_ref))):

            def step(r, sums, s=s, c_ref=c_ref, out_ref=out_ref):
                from_rows = pl.ds(pl.multiple_of(r * strip, strip), strip)
                rows = pl.ds(pl.multiple_of(s * row_len + r * strip, strip), strip)
                normed, inv = normed_of(acc_ref[rows, :])
                out_ref[from_rows, :] = (normed * g2 + s2).astype(bf16)
                c = c_ref[from_rows, :].astype(f32)
                second = norm_back(c, normed, inv, g2)
                acc_ref[rows, :] = second
                d2_ref[rows, :] = second.astype(bf16)
                return (sums[0] + eight(c * normed), sums[1] + eight(c), sums[2] + eight(second))

            sums = lax.fori_loop(0, row_len // strip, step, sums, unroll=repeat)
        for n in range(3):
            sums_ref[n : n + 1, :] = jnp.sum(sums[n], axis=0, keepdims=True)
        copies[2].start()

    def backward(wd_ref, dwd_ref, low_ref, dbu_ref):
        at = i - steps // 2
        up_ref[...] = dot(d2_ref[...], wd_ref[...], NT)
        dwd_ref[...] = dot(d2_ref[...], hidden_ref[at], TN).astype(bf16)
        total = jnp.zeros((8, chunk), f32)
        for r in range(0, tokens, block):
            rows = slice(r, r + block)
            grad = (up_ref[rows, :] * slope_ref[at, rows, :].astype(f32)).astype(bf16)
            low_ref[rows, :] = grad
            total = total + eight(grad.astype(f32))
        dbu_ref[...] = jnp.sum(total, axis=0, keepdims=True)

    @pl.when((i >= steps // 2) & (i < steps * 3 // 4))
    def _():
        backward(wd0_ref, dwd0_ref, low0_ref, dbu0_ref)

    @pl.when(i >= steps * 3 // 4)
    def _():
        backward(wd1_ref, dwd1_ref, low1_ref, dbu1_ref)

    @pl.when(i == 1)
    def _():
        copies[0].start()

    @pl.when(i == steps - 1)
    def _():
        for copy in copies:
            copy.wait()


def feed(part, o, wo, content, query, bo, g1, s1, wu, bu, wd, bd, g2, s2, cu, qu):
    tokens = o[0].shape[0]
    row_len = cu.shape[0]
    model, width = wu[0].shape
    c = width // chunk
    own = pl.BlockSpec((row_len, model), lambda i, part: (part[0], 0), pipeline_mode=pl.Buffered(1))
    up0 = lambda i: jnp.minimum(i, c - 1)
    up1 = lambda i: jnp.clip(i - c, 0, c - 1)
    down0 = lambda i: jnp.where(i < 2 * c, jnp.minimum(i, c - 1), jnp.minimum(i - 2 * c, c - 1))
    down1 = lambda i: jnp.where(i < 3 * c, jnp.clip(i - c, 0, c - 1), i - 3 * c)
    back0 = lambda i: jnp.clip(i - 2 * c, 0, c - 1)
    back1 = lambda i: jnp.clip(i - 3 * c, 0, c - 1)
    cols = lambda n, at: pl.BlockSpec((n, chunk), lambda i, part: (0, at(i)))
    rows = lambda at: pl.BlockSpec((chunk, model), lambda i, part: (at(i), 0))
    anywhere = pl.BlockSpec(memory_space=pl.ANY)
    shape = jax.ShapeDtypeStruct
    out_shape = [
        shape((tokens, model), f32),
        shape((tokens, model), bf16),
        shape((tokens, model), f32),
        shape((tokens, 1), f32),
        shape((row_len, model), bf16),
        shape((row_len, model), bf16),
        shape((8, model), f32),
    ]
    out_shape += [shape((model, width), bf16)] * 2 + [shape((tokens, width), bf16)] * 2 + [shape((1, width), f32)] * 2
    out_specs = [anywhere] * 3 + [once(one) for one in out_shape[3:7]]
    for n in (model, tokens, 1):
        out_specs += [cols(n, back0), cols(n, back1)]
    return pl.pallas_call(
        feed_kernel,
        grid_spec=pltpu.PrefetchScalarGridSpec(
            num_scalar_prefetch=1,
            grid=(4 * c,),
            in_specs=[once(o[0]), once(o[1]), once(wo[0]), once(wo[1]), own, own, once(bo), once(g1), once(s1)]
            + [cols(model, up0), cols(model, up1), once(bu[0]), once(bu[1]), rows(down0), rows(down1)]
            + [once(bd), once(g2), once(s2), once(cu), once(qu)],
            out_specs=out_specs,
            scratch_shapes=[
                pltpu.VMEM((tokens, model), f32),
                pltpu.VMEM((tokens, model), bf16),
                pltpu.VMEM((tokens, model), f32),
                pltpu.VMEM((tokens, model), bf16),
                pltpu.VMEM((2 * c, tokens, chunk), bf16),
                pltpu.VMEM((2 * c, tokens, chunk), bf16),
                pltpu.VMEM((8, chunk), f32),
                pltpu.VMEM((tokens, chunk), f32),
                pltpu.SemaphoreType.DMA((3,)),
            ],
        ),
        out_shape=out_shape,
        compiler_params=params(60),
        cost_estimate=light,
        name="feed",
    )(part, o[0], o[1], wo[0], wo[1], content, query, bo, g1, s1, wu[0], wu[1], bu[0], bu[1], wd[0], wd[1], bd, g2, s2, cu, qu)


def up_units(first_ref, low_ref, wu_ref, dwu_ref, acc_ref):
    @pl.when(pl.program_id(0) == 0)
    def _():
        acc_ref[...] = jnp.zeros_like(acc_ref)

    dwu_ref[...] = dot(first_ref[...], low_ref[...], TN).astype(bf16)
    acc_ref[...] += dot(low_ref[...], wu_ref[...], NT)


def up_back(first, low, wu):
    tokens, width = low.shape
    model = first.shape[1]
    cols = lambda n: pl.BlockSpec((n, chunk), lambda i: (0, i))
    acc = jax.ShapeDtypeStruct((tokens, model), f32)
    return pl.pallas_call(
        up_units,
        grid=(width // chunk,),
        in_specs=[once(first), cols(tokens), cols(model)],
        out_specs=[cols(model), once(acc)],
        out_shape=[jax.ShapeDtypeStruct((model, width), bf16), acc],
        compiler_params=params(60),
        cost_estimate=light,
        name="up_back",
    )(first, low, wu)


def up_back_last_kernel(
    first_ref, low_ref, wu_ref, g1_ref, inv_ref, normed_in, second_in, part_in, o0_in, o1_in,
    dwu_ref, residual_ref, al_ref, sums_ref, dwo0_ref, dwo1_ref,
    acc_ref, normed_ref, second_ref, part_ref, o0_ref, o1_ref, sems,
):
    tokens, model = acc_ref.shape
    i = pl.program_id(0)
    pairs = ((normed_in, normed_ref), (second_in, second_ref), (part_in, part_ref), (o0_in, o0_ref), (o1_in, o1_ref))
    copies = [pltpu.make_async_copy(here, there, sems.at[n]) for n, (here, there) in enumerate(pairs)]

    @pl.when(i == 0)
    def _():
        for copy in copies:
            copy.start()

    up_units(first_ref, low_ref, wu_ref, dwu_ref, acc_ref)

    @pl.when(i == pl.num_programs(0) - 1)
    def _():
        for copy in copies:
            copy.wait()
        g1 = g1_ref[...].reshape(1, -1)

        def step(r, sums):
            rows = pl.ds(pl.multiple_of(r * strip, strip), strip)
            back, normed = acc_ref[rows, :] + part_ref[rows, :] + second_ref[rows, :], normed_ref[rows, :]
            residual = norm_back(back, normed, inv_ref[rows, :], g1)
            residual_ref[rows, :] = residual
            al_ref[rows, :] = residual.astype(bf16)
            return (sums[0] + eight(back * normed), sums[1] + eight(back), sums[2] + eight(residual))

        sums = lax.fori_loop(0, tokens // strip, step, (jnp.zeros((8, model), f32),) * 3, unroll=repeat)
        for n in range(3):
            sums_ref[n : n + 1, :] = jnp.sum(sums[n], axis=0, keepdims=True)
        dwo0_ref[...] = dot(al_ref[...], o0_ref[...], TN).astype(bf16)
        dwo1_ref[...] = dot(al_ref[...], o1_ref[...], TN).astype(bf16)


def up_back_last(first, low, wu, g1, inv, normed, second, partial, o):
    tokens, width = low.shape
    model = first.shape[1]
    cols = lambda n: pl.BlockSpec((n, chunk), lambda i: (0, i))
    anywhere = pl.BlockSpec(memory_space=pl.ANY)
    shape = jax.ShapeDtypeStruct
    out_shape = [
        shape((model, width), bf16),
        shape((tokens, model), f32),
        shape((tokens, model), bf16),
        shape((8, model), f32),
        shape((model, o[0].shape[1]), bf16),
        shape((model, o[1].shape[1]), bf16),
    ]
    return pl.pallas_call(
        up_back_last_kernel,
        grid=(width // chunk,),
        in_specs=[once(first), cols(tokens), cols(model), once(g1), once(inv)] + [anywhere] * 5,
        out_specs=[cols(model)] + [once(one) for one in out_shape[1:]],
        out_shape=out_shape,
        scratch_shapes=[pltpu.VMEM((tokens, model), f32)] * 4
        + [pltpu.VMEM(o[0].shape, bf16), pltpu.VMEM(o[1].shape, bf16), pltpu.SemaphoreType.DMA((5,))],
        compiler_params=params(40),
        cost_estimate=light,
        name="up_back_last",
    )(first, low, wu, g1, inv, normed, second, partial, o[0], o[1])


def pack_kernel(part, one_ref, two_ref, dbu0_ref, dbu1_ref, *rest):
    smalls, out_ref = rest[:-1], rest[-1]
    first = part[0] == 0
    model = one_ref.shape[1]
    out_ref[...] = jnp.zeros_like(out_ref)
    out_ref[0:3, :] = one_ref[0:3, :]
    out_ref[3:6, :] = two_ref[0:3, :]
    pairs = model // tile // 2
    own = jnp.concatenate([ref[...] for ref in smalls[:-1]], axis=0)
    other = smalls[-1][...]
    for row in range(2):
        halves = [jnp.concatenate([half[n, row : row + 1, :] for n in range(pairs)], axis=1) for half in (own, other)]
        out_ref[6 + row : 7 + row, : model // 2] = jnp.where(first, halves[0], halves[1])
        out_ref[6 + row : 7 + row, model // 2 :] = jnp.where(first, halves[1], halves[0])
    tables = [
        jnp.concatenate([half[n, 2 + h : 3 + h, :] for n in range(pairs) for h in range(2)], axis=1) for half in (own, other)
    ]
    ups = [dbu0_ref[...], dbu1_ref[...]]
    for row, (a, b) in enumerate(((0, 1), (1, 0))):
        out_ref[8 + row : 9 + row, :] = jnp.where(first, tables[a], tables[b])
        up = jnp.where(first, ups[a], ups[b])
        rows = up.shape[1] // model
        for n in range(rows):
            at = 10 + row * rows + n
            out_ref[at : at + 1, :] = up[:, n * model : (n + 1) * model]


def pack(part, one, two, dbu0, dbu1, smalls):
    args = (one, two, dbu0, dbu1) + tuple(smalls)
    model = one.shape[1]
    return pl.pallas_call(
        pack_kernel,
        grid_spec=pltpu.PrefetchScalarGridSpec(
            num_scalar_prefetch=1, grid=(1,), in_specs=[whole(arg) for arg in args], out_specs=pl.BlockSpec((16, model), lambda *_: (0, 0))
        ),
        out_shape=jax.ShapeDtypeStruct((16, model), f32),
        compiler_params=params(4),
        name="pack",
    )(part, *args)


def exchange(value, axis_name, bit):
    count = lax.axis_size(axis_name)
    return lax.ppermute(value, axis_name, [(i, i ^ bit) for i in range(count)])


class Term:
    def __init__(self, pieces, left):
        self.pieces, self.left = pieces, left

    def places(self, flips, free):
        weight = {one: 1 << (len(self.left) - 1 - n) for n, one in enumerate(self.left)}
        own = {one: -w if one in flips else w for one, w in weight.items() if one not in free}
        start = sum(weight[one] for one in flips)
        for n in range(1 << len(free)):
            yield start + sum(weight[one] for m, one in enumerate(free) if n >> (len(free) - 1 - m) & 1), own


class Chain:
    def __init__(self, parts, order):
        bits = sum(len(step) for step in order)
        self.block = parts[0][0][0].shape[0] >> bits
        self.left = tuple(range(bits - 1, -1, -1))
        self.order = list(order)
        self.parts = [[Term([(array, 0, low, high - low)], self.left) for array, low, high in terms] for terms in parts]

    def step(self):
        bits = self.order.pop(0)
        self.left = tuple(one for one in self.left if one not in bits)
        return bits


def departures(chains, small=False):
    (bits,) = {chain.step() for chain in chains}
    before = [list(terms) for chain in chains for terms in chain.parts]
    masks = range(1, 1 << len(bits))
    return [Parcel(chains, before, [one for n, one in enumerate(bits) if mask >> n & 1], small) for mask in masks]


class Parcel:
    def __init__(self, chains, before, flips, small):
        self.chains, self.flips, self.small = chains, flips, small
        self.block = chains[0].block
        self.parts = list(zip(before, [chain.left for chain in chains for _ in chain.parts]))
        widths = [sum(piece[3] for piece in terms[0].pieces) for terms, _ in self.parts]
        self.width = math.gcd(*widths)
        self.spots, self.rows = [], 0
        for (_, left), n in zip(self.parts, widths):
            spots = []
            for at in range(0, n, self.width):
                spots.append((self.rows, at))
                self.rows += self.block << len(left)
            self.spots.append(spots)

    def go(self, sent):
        self.coming = exchange(sent, "dp", sum(1 << one for one in self.flips))

    def land(self, coming):
        spots = iter(self.spots)
        for chain in self.chains:
            for terms in chain.parts:
                terms.append(Term([(coming, row, 0, self.width) for row, _ in next(spots)], chain.left))
        return (coming, self.rows) if self.small else None


def read_plain(terms, flips, free, block):
    index = lax.axis_index("dp")
    total = 0.0
    for term in terms:
        rows = block << len(term.left)
        value = jnp.concatenate([array[row : row + rows, col : col + n] for array, row, col, n in term.pieces], axis=1)
        value = value.reshape((2,) * len(term.left) + (block, value.shape[1]))
        for axis, one in reversed(list(enumerate(term.left))):
            if one not in free:
                mine = (index >> one) & 1
                value = lax.dynamic_index_in_dim(value, 1 - mine if one in flips else mine, axis, keepdims=False)
        total = total + value.reshape(block << len(free), value.shape[-1]).astype(f32)
    return total


class Reader:
    def __init__(self, block):
        self.block, self.arrays, self.copies, self.counts = block, [], [], {}

    def read(self, terms, flips, free):
        blocks = [[] for _ in range(1 << len(free))]
        for term in terms:
            for n, (at, own) in enumerate(term.places(flips, free)):
                slots = []
                for array, row, col, width in term.pieces:
                    known = [m for m, one in enumerate(self.arrays) if one is array]
                    if not known:
                        known = [len(self.arrays)]
                        self.arrays.append(array)
                    slot = self.counts.get((width, array.dtype), 0)
                    self.counts[(width, array.dtype)] = slot + 1
                    self.copies.append((known[0], row + at * self.block, own, col, width, array.dtype, slot))
                    slots.append((width, array.dtype, slot))
                blocks[n].append(slots)
        return blocks

    def scratch(self):
        kinds = list(self.counts)
        return [pltpu.VMEM((self.counts[kind], self.block, kind[0]), kind[1]) for kind in kinds] + [
            pltpu.SemaphoreType.DMA((len(self.copies),))
        ]

    def start(self, index, array_refs, scratch):
        buffers = dict(zip(self.counts, scratch))
        made = []
        for n, (array, row, own, col, width, dtype, slot) in enumerate(self.copies):
            at = row + self.block * sum(((index >> one) & 1) * w for one, w in own.items())
            rows = pl.ds(pl.multiple_of(at, 16), self.block)
            copy = pltpu.make_async_copy(array_refs[array].at[rows, col : col + width], buffers[(width, dtype)].at[slot], scratch[-1].at[n])
            copy.start()
            made.append(copy)
        return buffers, made

    @staticmethod
    def add(buffers, terms):
        total = None
        for slots in terms:
            value = [buffers[(width, dtype)][slot].astype(f32) for width, dtype, slot in slots]
            value = value[0] if len(value) == 1 else jnp.concatenate(value, axis=1)
            total = value if total is None else total + value
        return total


def halves_of(got, rows):
    return [(coming[at : at + rows], coming[at + rows : at + 2 * rows]) for coming, at in got]


def join_small(packed, got):
    wide = [jnp.concatenate(one, axis=1).astype(f32) for one in got]
    if len(wide) == 3:
        return (packed + wide[0]) + (wide[1] + wide[2])
    return packed + wide[0] if wide else packed


def post(index, parcels, packed=None, got=()):
    block = parcels[0].block
    smalls = [parcel for parcel in parcels if parcel.small]
    if block % 16:
        sents = []
        if smalls:
            packed = lax.reduce_precision(join_small(packed, halves_of(got, packed.shape[0])), 8, 7)
        for parcel in parcels:
            values = []
            for (terms, left), spots in zip(parcel.parts, parcel.spots):
                value = read_plain(terms, parcel.flips, left, block).astype(bf16)
                values += [value[:, at : at + parcel.width] for _, at in spots]
            if parcel.small:
                half = packed.shape[1] // 2
                values += [packed[:, :half].astype(bf16), packed[:, half:].astype(bf16)]
            sents.append(jnp.concatenate(values, axis=0))
        return sents + ([packed] if smalls else [])
    reader = Reader(block)
    plans = [[reader.read(terms, parcel.flips, left) for terms, left in parcel.parts] for parcel in parcels]
    shapes = [jax.ShapeDtypeStruct((parcel.rows + (2 * packed.shape[0] if parcel.small else 0), parcel.width), bf16) for parcel in parcels]
    extra, extra_specs = [], []
    if smalls:
        extra = [packed] + [coming for coming, _ in got for _ in range(2)]
        shapes.append(jax.ShapeDtypeStruct(packed.shape, f32))
        extra_specs = [once(packed)] + [
            pl.BlockSpec((packed.shape[0], coming.shape[1]), lambda *_, n=at // packed.shape[0] + half: (n, 0))
            for coming, at in got
            for half in range(2)
        ]

    def kernel(index_ref, *refs):
        array_refs = refs[: len(reader.arrays)]
        extra_refs = refs[len(reader.arrays) : len(reader.arrays) + len(extra)]
        outs = refs[len(reader.arrays) + len(extra) :][: len(shapes)]
        buffers, made = reader.start(index_ref[0], array_refs, refs[len(reader.arrays) + len(extra) + len(shapes) :])
        if smalls:
            value = join_small(
                extra_refs[0][...], [(extra_refs[n][...], extra_refs[n + 1][...]) for n in range(1, len(extra), 2)]
            ).astype(bf16)
            outs[-1][...] = value.astype(f32)
            for parcel, out in zip(parcels, outs):
                if parcel.small:
                    half, rows = value.shape[1] // 2, value.shape[0]
                    at = parcel.rows
                    out[at : at + rows, :] = value[:, :half]
                    out[at + rows : at + 2 * rows, :] = value[:, half:]
        for copy in made:
            copy.wait()
        for parcel, plan, out in zip(parcels, plans, outs):
            for spots, blocks in zip(parcel.spots, plan):
                for n, terms in enumerate(blocks):
                    value = reader.add(buffers, terms).astype(bf16)
                    for row, at in spots:
                        out[row + n * block : row + (n + 1) * block, :] = value[:, at : at + parcel.width]

    return pl.pallas_call(
        kernel,
        grid_spec=pltpu.PrefetchScalarGridSpec(
            num_scalar_prefetch=1,
            grid=(1,),
            in_specs=[pl.BlockSpec(memory_space=pltpu.HBM)] * len(reader.arrays) + extra_specs,
            out_specs=[once(one) for one in shapes],
            scratch_shapes=reader.scratch(),
        ),
        out_shape=shapes,
        compiler_params=params(16),
        cost_estimate=light,
        name="post",
    )(index, *reader.arrays, *extra)


def total_of(index, name, parts, block, extra, shapes, write):
    plain = block % 16
    reader = Reader(block)
    plans = [] if plain else [reader.read(terms, (), ())[0] for terms in parts]
    arrays = [read_plain(terms, (), (), block) for terms in parts] if plain else reader.arrays

    def kernel(index_ref, *refs):
        array_refs, extra_refs = refs[: len(arrays)], refs[len(arrays) :][: len(extra)]
        outs, scratch = refs[len(arrays) + len(extra) :][: len(shapes)], refs[len(arrays) + len(extra) + len(shapes) :]
        if plain:
            sums = [ref[...] for ref in array_refs]
        else:
            buffers, made = reader.start(index_ref[0], array_refs, scratch)
            for copy in made:
                copy.wait()
            sums = [reader.add(buffers, plan) for plan in plans]
        write(sums, extra_refs, outs)

    return pl.pallas_call(
        kernel,
        grid_spec=pltpu.PrefetchScalarGridSpec(
            num_scalar_prefetch=1,
            grid=(1,),
            in_specs=[once(one) if plain else pl.BlockSpec(memory_space=pltpu.HBM) for one in arrays] + [once(one) for one in extra],
            out_specs=[once(one) for one in shapes],
            scratch_shapes=[] if plain else reader.scratch(),
        ),
        out_shape=shapes,
        compiler_params=params(8),
        cost_estimate=light,
        name=name,
    )(index, *arrays, *extra)


def finish_wide(index, groups, block):
    shapes = [jax.ShapeDtypeStruct((block, sum(sum(piece[3] for piece in terms[0].pieces) for terms in group)), f32) for group in groups]

    def write(sums, _, outs):
        for group, out in zip(groups, outs):
            out[...] = jnp.concatenate(sums[: len(group)], axis=1)
            sums = sums[len(group) :]

    return total_of(index, "finish_wide", [terms for group in groups for terms in group], block, [], shapes, write)


def finish(index, packed, far, parts, block, units, buckets, heads):
    model = packed.shape[1]
    f32_of = lambda *shape: jax.ShapeDtypeStruct(shape, f32)
    shapes = [f32_of(model)] * 8 + [f32_of(units), f32_of(heads, buckets)] + [f32_of(block, len(parts) * tile)] * 3

    def write(sums, extra_refs, outs):
        rows = extra_refs[0][...] + extra_refs[1][...]
        for n in range(8):
            outs[n][...] = rows[n : n + 1, :].reshape(model)
        up = jnp.concatenate([rows[n : n + 1, :] for n in range(10, 10 + units // model)], axis=1)
        outs[8][...] = up.reshape(units)
        heads_of = [rows[8 + half : 9 + half, n * tile : (n + 1) * tile] for half in range(2) for n in range(model // tile)]
        outs[9][...] = jnp.concatenate(heads_of, axis=0)[:heads, :buckets]
        for n in range(3):
            for pair, value in enumerate(sums):
                outs[10 + n][:, pair * tile : (pair + 1) * tile] = value[:, n * tile : (n + 1) * tile]

    return total_of(index, "finish", parts, block, [packed, far], shapes, write)


def wide_groups(x, y, z):
    return [[z.parts[1]], [y.parts[0], z.parts[0]], [x.parts[0]]]


def gate(*values):
    return lax.optimization_barrier(values)


def local(
    content_input,
    query_input,
    segment_ids,
    orders,
    predicted,
    query_weight,
    query_bias,
    key_weight,
    value_weight,
    value_bias,
    out_weight,
    out_bias,
    first_gain,
    first_shift,
    up_weight,
    up_bias,
    down_weight,
    down_bias,
    second_gain,
    second_shift,
    bias_table,
    content_upstream,
    query_upstream,
):
    tensor_index = lax.axis_index("tensor")
    bits = lax.axis_size("dp").bit_length() - 1
    part = tensor_index.astype(jnp.int32).reshape(1)
    far_of = lambda value: exchange(value, "tensor", 1)

    def order(*first):
        named = [bit for step in first for bit in step]
        return list(first) + [(bit,) for bit in range(bits) if bit not in named]

    own_bundle = bundle(query_bias, value_bias, up_bias, bias_table.T)
    own_attention = (own_bundle, query_weight, key_weight, value_weight)
    far_attention = tuple(far_of(value) for value in own_attention)
    rows = (segment_ids, orders, predicted)
    heads = bias_table.shape[1]
    buckets = band_buckets()
    hot = jnp.asarray((buckets[:, None] == np.arange(tile)[None, :]).astype(np.float32))

    def attention(values, keep_t):
        return attend(part, content_input, query_input, rows, hot, *values, keep_t)

    own = attention(own_attention, True)
    streams_t = own[7]
    sent = gate(*far_attention[1:], out_weight, up_weight, down_weight)
    far_attention = (far_attention[0], *sent[:3])
    out_far, up_far, down_far = (far_of(value) for value in sent[3:])
    saved = [own[:7], attention(far_attention, False)]
    out_w, up_w, down_w = (out_weight, out_far), (up_weight, up_far), (down_weight, down_far)
    bundles = (own_bundle, far_attention[0])
    attention_w = [own_attention[1:], far_attention[1:]]
    o = (saved[0][3], saved[1][3])
    normed, first, second, inv, final_c, final_q, sums_two, dwd0, dwd1, low0, low1, dbu0, dbu1 = feed(
        part, o, out_w, content_input, query_input, out_bias, first_gain, first_shift, up_w, bundles, down_w,
        down_bias, second_gain, second_shift, content_upstream, query_upstream,
    )
    far_d = far_of(dwd1)
    index = lax.axis_index("dp").astype(jnp.int32).reshape(1)
    units = dwd0.shape[1]
    cut = units * 3 // 4
    width = query_weight.shape[1]
    both = lambda own, far, low, high: [(own, low, high), (far, low, high)]

    def leave(parcels, after, packed=None, got=()):
        sents = post(index, parcels, packed, got)
        after, *sents = gate(after, *sents)
        for parcel, sent in zip(parcels, sents):
            parcel.go(sent)
        return (after, sents[-1]) if packed is not None else after

    def arrive(parcels, after):
        after, *came = gate(after, *[parcel.coming for parcel in parcels])
        return after, [parcel.land(one) for parcel, one in zip(parcels, came)]

    dwu1, partial = up_back(first, low1, up_w[1])
    chain_x = Chain([both(dwd0, far_d, 0, units)], order((0,), (1,), (2,)))
    first_x = departures([chain_x])
    partial, _ = gate(partial, far_d)
    partial, dwu1 = leave(first_x, (partial, dwu1))
    far_u = far_of(dwu1)
    dwu0, residual, al, sums_one, dwo0, dwo1 = up_back_last(first, low0, up_w[0], first_gain, inv, normed, second, partial, o)
    far_o = far_of(dwo1)
    al, far_u, far_o = gate(al, far_u, far_o)
    chain_y = Chain([both(dwu0, far_u, 0, cut)], order((1,), (0,), (2,)))
    chain_z = Chain([both(dwu0, far_u, cut, units), both(dwo0, far_o, 0, width)], order((2,), (3,), (0, 1)))
    first_y, first_z = departures([chain_y]), departures([chain_z])
    al = leave(first_y + first_z, al)

    def attention_back(s, from_pair, pairs, al):
        q, k, v, _, ot, e, linv = saved[s]
        return attend_back(from_pair, pairs, al, out_w[s], ot, q, k, v, e, linv, streams_t, hot)

    pairs = width // tile
    late = 1
    early = pairs - late
    split, side_width = early * tile, late * tile
    other = attention_back(1, 0, pairs, al)
    al, _ = arrive(first_x + first_y + first_z, gate(al, other[0])[0])
    second_x, second_y, second_z = (departures([chain]) for chain in (chain_x, chain_y, chain_z))
    al = leave(second_y + second_x + second_z, al)
    dw_other, al = gate(other[0], al)
    far = far_of(dw_other)
    own_early = attention_back(0, 0, early, al)
    al, far, dw_early = gate(al, far, own_early[0])
    al, _ = arrive(second_x + second_y + second_z, al)
    triple = 3 * tile
    of_pair = lambda n: (n * triple, (n + 1) * triple)
    chain_a = Chain([[(dw_early, *of_pair(n)), (far, *of_pair(n))] for n in range(early)], order((0, 1), (2, 3)))
    first_a, third = departures([chain_a]), departures([chain_x, chain_y])
    al = leave(first_a + third, al)
    own_late = attention_back(0, early, late, al)
    packed = pack(part, sums_one, sums_two, dbu0, dbu1, [own_early[1], own_late[1], other[1]])
    dw_late = own_late[0]
    chain_b = Chain([[(dw_late, *of_pair(n)), (far, *of_pair(early + n))] for n in range(late)], order((0, 1), (2, 3)))
    residual, _ = arrive(third, residual)
    fourth = departures([chain_x, chain_y])
    parcels = departures([chain_b, chain_z], True)
    residual, packed = leave(parcels + fourth, residual, packed)
    content_grad, query_grad = inputs_back(
        residual,
        [
            (own_early[2:5], attention_w[0], 0, split),
            (own_late[2:5], attention_w[0], early // late, side_width),
            (other[2:5], attention_w[1], 0, split + side_width),
        ],
    )
    content_grad, _ = arrive(first_a, content_grad)
    content_grad, got = arrive(parcels, content_grad)
    chains = [chain_a, chain_b]
    wide_out = None
    while chain_a.order:
        parcels = departures(chains, True)
        content_grad, packed = leave(parcels, content_grad, packed, got)
        if wide_out is None:
            content_grad, _ = arrive(fourth, content_grad)
        if not chain_x.order and wide_out is None:
            wide_out = finish_wide(index, wide_groups(chain_x, chain_y, chain_z), chain_a.block)
            content_grad, *wide_out = gate(content_grad, *wide_out)
        content_grad, got = arrive(parcels, content_grad)
        chains = [chain_a, chain_b, chain_x, chain_y, chain_z]
    if wide_out is None:
        wide_out = finish_wide(index, wide_groups(chain_x, chain_y, chain_z), chain_a.block)
    packed = join_small(packed, halves_of(got, packed.shape[0]))
    parts = chain_a.parts + chain_b.parts
    out = finish(index, packed, far_of(packed), parts, chain_a.block, 2 * units, bias_table.shape[0], 2 * heads)
    return (
        final_c,
        final_q,
        content_grad,
        query_grad,
        *out[10:13],
        wide_out[0].T,
        wide_out[1],
        wide_out[2].T,
        out[6],
        out[7],
        out[2],
        out[0],
        out[1],
        out[8],
        out[5],
        out[3],
        out[4],
        out[9].T,
    )


def solution(mesh):
    placed = (
        P("dp", None),
        P("dp", None),
        P("dp", None),
        P("dp", None),
        P("dp", None),
        P(None, "tensor"),
        P("tensor"),
        P(None, "tensor"),
        P(None, "tensor"),
        P("tensor"),
        P("tensor", None),
        P(),
        P(),
        P(),
        P(None, "tensor"),
        P("tensor"),
        P("tensor", None),
        P(),
        P(),
        P(),
        P(None, "tensor"),
        P(("dp", "tensor"), None),
        P(("dp", "tensor"), None),
    )
    rows_out = P(("dp", "tensor"), None)
    return jax.shard_map(
        local,
        mesh=mesh,
        in_specs=placed,
        out_specs=(
            rows_out,
            rows_out,
            rows_out,
            rows_out,
            P("dp", "tensor"),
            P("dp", "tensor"),
            P("dp", "tensor"),
            P("tensor", "dp"),
            P("dp", "tensor"),
            P("tensor", "dp"),
        )
        + (P(),) * 10,
        check_vma=False,
    )
```
